32 devices in a mesh: wide: 8 (over z, x), narrow: 4 (over y, core).
Axes of the slice: x: 2, y: 2, z: 4, core: 2. Of those that a mesh axis runs over, the one named last changes fastest.
Arguments:
- tokens: bfloat16 [64, 1024, 480], P(('wide', 'narrow')), may hold values from -6 to 6
- segment_ids: int32 [64, 1024], P(('wide', 'narrow')), may hold values from 0 to 3, never falling along the last dimension, each value on 1 to 512 neighbouring positions
- pad_mask: int32 [64, 1024], P(('wide', 'narrow')), may hold values 0 or 1
- cotangent: bfloat16 [64, 1024, 480], P(('wide', 'narrow')), may hold values from -6 to 6
- qkv_weight: float32 [691200], P(('wide', 'narrow')), may hold values from -0.25 to 0.25
- qkv_first: float32 [691200], P(('wide', 'narrow')), may hold values from -256 to 256
- qkv_second: float32 [691200], P(('wide', 'narrow')), may hold values from 65536 to 262144
- out_weight: float32 [230400], P(('wide', 'narrow')), may hold values from -6 to 6
- out_first: float32 [230400], P(('wide', 'narrow')), may hold values from -22.627417 to 22.627417
- out_second: float32 [230400], P(('wide', 'narrow')), may hold values from 512 to 2048
- up_weight: float32 [921600], P(('wide', 'narrow')), may hold values from -0.25 to 0.25
- up_first: float32 [921600], P(('wide', 'narrow')), may hold values from -89.6 to 89.6
- up_second: float32 [921600], P(('wide', 'narrow')), may hold values from 7864.32 to 31457.28
- down_weight: float32 [921600], P(('wide', 'narrow')), may hold values from -0.125 to 0.125
- down_first: float32 [921600], P(('wide', 'narrow')), may hold values from -204.8 to 204.8
- down_second: float32 [921600], P(('wide', 'narrow')), may hold values from 41943.04 to 167772.16
- gains: float32 [960], replicated, may hold values from 0.5 to 1.5
- gain_first: float32 [960], replicated, may hold values from -256 to 256
- gain_second: float32 [960], replicated, may hold values from 65536 to 262144
- biases: float32 [5280], replicated, may hold values from -1.75 to 1.75
- bias_first: float32 [5280], replicated, may hold values from -256 to 256
- bias_second: float32 [5280], replicated, may hold values from 65536 to 262144
Outputs:
- outputs: bfloat16 [64, 1024, 480], P(('wide', 'narrow'))
- input_grad: float32 [64, 1024, 480], P(('wide', 'narrow'))
- qkv_grad: float32 [691200], P(('wide', 'narrow'))
- qkv_new: float32 [691200], P(('wide', 'narrow'))
- qkv_first_new: float32 [691200], P(('wide', 'narrow'))
- qkv_second_new: float32 [691200], P(('wide', 'narrow'))
- out_grad: float32 [230400], P(('wide', 'narrow'))
- out_new: float32 [230400], P(('wide', 'narrow'))
- out_first_new: float32 [230400], P(('wide', 'narrow'))
- out_second_new: float32 [230400], P(('wide', 'narrow'))
- up_grad: float32 [921600], P(('wide', 'narrow'))
- up_new: float32 [921600], P(('wide', 'narrow'))
- up_first_new: float32 [921600], P(('wide', 'narrow'))
- up_second_new: float32 [921600], P(('wide', 'narrow'))
- down_grad: float32 [921600], P(('wide', 'narrow'))
- down_new: float32 [921600], P(('wide', 'narrow'))
- down_first_new: float32 [921600], P(('wide', 'narrow'))
- down_second_new: float32 [921600], P(('wide', 'narrow'))
- gain_grad: float32 [960], replicated
- gain_new: float32 [960], replicated
- gain_first_new: float32 [960], replicated
- gain_second_new: float32 [960], replicated
- bias_grad: float32 [5280], replicated
- bias_new: float32 [5280], replicated
- bias_first_new: float32 [5280], replicated
- bias_second_new: float32 [5280], replicated
- down_bias_grad: float32 [480], replicated
The draws below stay inside these ranges and needn't reach their ends.
Inputs may be any that keep to these rules, and one draw needn't show every extreme that they name: `segment_ids`: within a row the ids never fall; each of the 4 proteins of a row holds 1 to 512 residues, and some protein holds 512.
All inputs are finite; a program needn't handle non-finite values. No bound on the sum of `pad_mask` on one device may be relied on, other than what follows from the above.
Results may differ from the reference program's by a relative error of at most 0.012.
Values may be sent and summed in bfloat16 or wider, within the bound.
No kernel may reach another device: no remote copies, remote signals or barrier semaphores. Data moves between devices by JAX's collectives and lax.ppermute only.
A program may use at most 192 MiB of HBM per device.

```python
import functools
import math
import jax
import jax.numpy as jnp
import numpy as np
from jax import lax

D = 480
HEAD_DIM = 24
FF = 1920
LEN = 1024
SEGS = 4
STEP = 3
ROWS = 64
LONGEST = 512


def plant(values, own_key, smallest, top_value):
    spot = [jax.random.randint(jax.random.fold_in(own_key, axis), (), 0, length) for axis, length in enumerate(values.shape)]
    widest = values.shape.index(max(values.shape))
    next_to = spot[:widest] + [(spot[widest] + 1) % values.shape[widest]] + spot[widest + 1:]
    return values.at[tuple(spot)].set(smallest).at[tuple(next_to)].set(top_value)


def shard_levels(own_key, shape, split, least, high):
    loudness = 1.0
    for dim, blocks in split:
        steps = jax.random.uniform(jax.random.fold_in(jax.random.fold_in(own_key, 6), dim), (blocks,), jnp.float32, least / len(split), high / len(split))
        loudness = loudness * jnp.repeat(jnp.exp(steps), shape[dim] // blocks).reshape((-1,) + (1,) * (len(shape) - 1 - dim))
    return loudness


def length_profile(amount, total, limit, lean):
    weights = [(1 << 20) // math.isqrt(grade ** lean) + 1 for grade in range(2, amount + 1)]
    rest, holding = total - limit - (amount - 1), [1] * (amount - 1)
    while rest > 0:
        candidates = [i for i in range(amount - 1) if holding[i] < limit]
        mass, remaining = sum([weights[i] for i in candidates]), rest
        for i in candidates:
            extra = min(limit - holding[i], max(1, remaining * weights[i] // mass), rest)
            holding[i] = holding[i] + extra
            rest = rest - extra
    return np.array([limit] + holding)


def uneven_parts(stream_key, number_of, total, most, slope):
    if number_of == 2:
        one = jax.random.randint(stream_key, (), max(1, total - most), min(most, total - 1) + 1)
        return jnp.stack([one, total - one])
    tallies = jnp.asarray(length_profile(number_of, total, most, slope), jnp.int32)
    pairs = (number_of - 1) // 2
    source_of, receiver = tallies[1:1 + 2 * pairs:2], tallies[2:2 + 2 * pairs:2]
    margin = jnp.minimum(source_of - 1, most - receiver)
    passed = jax.random.randint(jax.random.fold_in(stream_key, 1), (pairs,), 0, 1 << 20) % (margin + 1)
    tallies = tallies.at[1:1 + 2 * pairs:2].set(source_of - passed).at[2:2 + 2 * pairs:2].set(receiver + passed)
    return tallies[jax.random.permutation(jax.random.fold_in(stream_key, 2), number_of)]


def scatter_about(stream_key, extent, scale, limit, cuts=(), kind=jnp.bfloat16):
    drawn = jax.random.normal(stream_key, extent, jnp.float32) * scale
    if len(cuts) > 0:
        drawn = shard_levels(stream_key, extent, cuts, -0.22, 0.18) * drawn
    return jnp.clip(drawn, min=-limit, max=limit).astype(kind)


def setup_inputs(seed: int = 0) -> dict:
    keys = jax.random.split(jax.random.key(seed), 23)
    return {
        "tokens": scatter_about(keys[0], (ROWS, LEN, D), 1.0, 6.0, ((0, 32),)),
        "segment_ids": jax.vmap(lambda own: jnp.searchsorted(jnp.cumsum(uneven_parts(own, SEGS, LEN, LONGEST, 2)), jnp.arange(LEN), side="right"))(jax.random.split(keys[1], ROWS)).reshape((ROWS, LEN)).astype(jnp.int32),
        "pad_mask": plant((jax.random.randint(keys[2], (ROWS, LEN), 0, 8) < 7).astype(jnp.int32), jax.random.fold_in(keys[2], 1), 0, 1),
        "cotangent": scatter_about(keys[3], (ROWS, LEN, D), 1.0, 6.0, ((0, 32),)),
        "qkv_weight": scatter_about(keys[4], (3 * D * D,), D ** -0.5, 0.25, ((0, 32),), jnp.float32),
        "qkv_first": jnp.clip(jax.random.uniform(keys[5], (3 * D * D,), jnp.float32, -256.0, 256.0) * shard_levels(keys[5], (3 * D * D,), ((0, 32),), -0.4, 0.0), -256.0, 256.0),
        "qkv_second": jnp.clip(jnp.exp(math.log(262144.0) - 1.3862944 * jax.random.uniform(keys[6], (3 * D * D,), jnp.float32) ** shard_levels(keys[6], (3 * D * D,), ((0, 32),), -0.2, 0.2)), 65536.0, 262144.0),
        "out_weight": scatter_about(keys[7], (D * D,), (D * SEGS // LEN) ** -0.5, 6.0, ((0, 32),), jnp.float32),
        "out_first": jnp.clip(jax.random.uniform(keys[8], (D * D,), jnp.float32, -22.627417, 22.627417) * shard_levels(keys[8], (D * D,), ((0, 32),), -0.4, 0.0), -22.627417, 22.627417),
        "out_second": jnp.clip(jnp.exp(math.log(2048.0) - 1.3862944 * jax.random.uniform(keys[9], (D * D,), jnp.float32) ** shard_levels(keys[9], (D * D,), ((0, 32),), -0.2, 0.2)), 512.0, 2048.0),
        "up_weight": scatter_about(keys[10], (D * FF,), D ** -0.5, 0.25, ((0, 32),), jnp.float32),
        "up_first": jnp.clip(jax.random.uniform(keys[11], (D * FF,), jnp.float32, -89.6, 89.6) * shard_levels(keys[11], (D * FF,), ((0, 32),), -0.4, 0.0), -89.6, 89.6),
        "up_second": jnp.clip(jnp.exp(math.log(31457.28) - 1.3862944 * jax.random.uniform(keys[12], (D * FF,), jnp.float32) ** shard_levels(keys[12], (D * FF,), ((0, 32),), -0.2, 0.2)), 7864.32, 31457.28),
        "down_weight": scatter_about(keys[13], (FF * D,), FF ** -0.5, 0.125, ((0, 32),), jnp.float32),
        "down_first": jnp.clip(jax.random.uniform(keys[14], (FF * D,), jnp.float32, -204.8, 204.8) * shard_levels(keys[14], (FF * D,), ((0, 32),), -0.4, 0.0), -204.8, 204.8),
        "down_second": jnp.clip(jnp.exp(math.log(167772.16) - 1.3862944 * jax.random.uniform(keys[15], (FF * D,), jnp.float32) ** shard_levels(keys[15], (FF * D,), ((0, 32),), -0.2, 0.2)), 41943.04, 167772.16),
        "gains": jnp.clip(1.0 + 0.1 * jax.random.normal(keys[16], (2 * D,), jnp.float32), 0.5, 1.5),
        "gain_first": jnp.clip(jax.random.uniform(keys[17], (2 * D,), jnp.float32, -256.0, 256.0), -256.0, 256.0),
        "gain_second": jnp.clip(jnp.exp(jax.random.uniform(keys[18], (2 * D,), jnp.float32, math.log(65536.0), math.log(262144.0))), 65536.0, 262144.0),
        "biases": scatter_about(keys[19], (7 * D + FF,), 0.3, 1.75, (), jnp.float32),
        "bias_first": jnp.clip(jax.random.uniform(keys[20], (7 * D + FF,), jnp.float32, -256.0, 256.0), -256.0, 256.0),
        "bias_second": jnp.clip(jnp.exp(jax.random.uniform(keys[21], (7 * D + FF,), jnp.float32, math.log(65536.0), math.log(262144.0))), 65536.0, 262144.0),
    }


@jax.custom_vjp
def low(v):
    return lax.optimization_barrier(v.astype(jnp.bfloat16)).astype(jnp.float32)

@jax.custom_vjp
def low_back(v):
    return v

def low_keep(v):
    return (low(v), None)

def low_pass(kept, grad):
    return (grad,)

def back_keep(v):
    return (v, None)

def back_low(kept, grad):
    return (low(grad),)
low.defvjp(low_keep, low_pass)
low_back.defvjp(back_keep, back_low)

def top_dot(left, right):
    return jnp.dot(left, right, precision=lax.Precision.HIGHEST, preferred_element_type=jnp.float32)

def layer_norm(field, gain_row, offset):
    average = lax.optimization_barrier(jnp.mean(field, axis=-1, keepdims=True))
    centered = field - average
    spread = lax.optimization_barrier(jnp.mean(centered * centered, axis=-1, keepdims=True))
    return centered * lax.rsqrt(spread + 1e-05) * gain_row + offset

def positions_of(segments):
    places = lax.broadcasted_iota(jnp.int32, segments.shape, segments.ndim - 1)
    change = jnp.concatenate([jnp.ones(segments.shape[:-1] + (1,), dtype=jnp.bool_), segments[..., 1:] != segments[..., :-1]], axis=-1)
    starts = lax.cummax(jnp.where(change, places, 0), axis=segments.ndim - 1)
    return (places - starts).astype(jnp.float32)

def angles(segments):
    half_dim = HEAD_DIM // 2
    frequency = jnp.exp(jnp.arange(half_dim).astype(jnp.float32) * (-math.log(10000.0) / half_dim))
    phases = positions_of(segments)[..., None] * frequency
    return (jnp.cos(phases)[..., None, :], jnp.sin(phases)[..., None, :])

def rotate(field, cosine, sine_part):
    half_dim = field.shape[-1] // 2
    front_half = field[..., :half_dim]
    back_half = field[..., half_dim:]
    return jnp.concatenate([front_half * cosine - back_half * sine_part, back_half * cosine + front_half * sine_part], axis=-1)

def allowed_mask(segments, pad_mask):
    length = segments.shape[-1]
    diagonal = jnp.arange(length)[:, None] == jnp.arange(length)[None, :]
    return (segments[:, :, None] == segments[:, None, :]) & ((pad_mask[:, None, :] == 1) | diagonal[None])

def head_attention(triple, allowed):
    scores = low_back(jnp.einsum('rie,rje->rij', triple[0], triple[1], precision=lax.Precision.HIGHEST))
    scores = jnp.where(allowed, scores, -1e+30)
    attn_probs = jax.nn.softmax(scores, axis=-1)
    return jnp.einsum('rij,rje->rie', low(attn_probs), triple[2], precision=lax.Precision.HIGHEST)

def forward(tokens, segments, pad_mask, w_qkv, w_out, w_up, w_down, gains, biases):
    row_count, length, model_width = tokens.shape
    head_count = model_width // HEAD_DIM
    cosine, sine_part = angles(segments)
    allowed = allowed_mask(segments, pad_mask)
    flat_tokens = tokens.reshape(row_count * length, model_width)
    normed = layer_norm(flat_tokens, gains[:model_width], biases[:model_width])
    mixed_qkv = top_dot(low(normed), low(w_qkv)) + biases[model_width:4 * model_width]
    mixed_qkv = low_back(mixed_qkv).reshape(row_count, length, 3, head_count, HEAD_DIM)
    queries = low(rotate(mixed_qkv[:, :, 0], cosine, sine_part) * HEAD_DIM ** (-0.5))
    keys_low = low(rotate(mixed_qkv[:, :, 1], cosine, sine_part))
    values = low(mixed_qkv[:, :, 2])
    per_head = (jnp.moveaxis(queries, 2, 0), jnp.moveaxis(keys_low, 2, 0), jnp.moveaxis(values, 2, 0))
    attended = lax.map(jax.checkpoint(functools.partial(head_attention, allowed=allowed)), per_head)
    attended = jnp.moveaxis(attended, 0, 2).reshape(row_count * length, model_width)
    attended = low(low_back(attended))
    branch = low_back(top_dot(attended, low(w_out)) + biases[4 * model_width:5 * model_width])
    middle = flat_tokens + branch
    normed_two = layer_norm(middle, gains[model_width:], biases[5 * model_width:6 * model_width])
    hidden = low_back(top_dot(low(normed_two), low(w_up)) + biases[6 * model_width:6 * model_width + FF])
    active = low(jax.nn.gelu(hidden, approximate=False))
    branch_two = low_back(top_dot(active, low(w_down)) + biases[6 * model_width + FF:])
    return (middle + branch_two).reshape(row_count, length, model_width)

def adamw_update(weight, first, second, gradient, learn_rate, step_value):
    first_new = 0.5 * first + 0.5 * gradient
    second_new = 0.5 * second + 0.5 * gradient * gradient
    correction = 1.0 - 0.5 ** step_value
    stepped = first_new / correction / (jnp.sqrt(second_new / correction) + 1e-08)
    return (weight - learn_rate * (stepped + 0.01 * weight), first_new, second_new)

def reference(tokens, segment_ids, pad_mask, cotangent, qkv_weight, qkv_first, qkv_second, out_weight, out_first, out_second, up_weight, up_first, up_second, down_weight, down_first, down_second, gains, gain_first, gain_second, biases, bias_first, bias_second):
    params = (qkv_weight.reshape(D, 3 * D), out_weight.reshape(D, D), up_weight.reshape(D, FF), down_weight.reshape(FF, D), gains, biases)
    group_rows = 4
    count_groups = ROWS // group_rows

    def reshaped(array):
        return array.reshape((count_groups, group_rows) + array.shape[1:])

    def one_group(totals, blocks):
        x_block, seg_block, pad_block, cot_block = blocks

        def local_forward(x_value, w_qkv, w_out, w_up, w_down, gain_rows, bias_rows):
            return forward(x_value, seg_block, pad_block, w_qkv, w_out, w_up, w_down, gain_rows, bias_rows)
        result_rows, pullback = jax.vjp(local_forward, x_block.astype(jnp.float32), *params)
        gradients = pullback(cot_block.astype(jnp.float32))
        totals = tuple((total + part for total, part in zip(totals, gradients[1:])))
        return (totals, (result_rows.astype(jnp.bfloat16), gradients[0]))
    zeros = tuple((jnp.zeros_like(item) for item in params))
    totals, (outputs, input_grad) = lax.scan(one_group, zeros, (reshaped(tokens), reshaped(segment_ids), reshaped(pad_mask), reshaped(cotangent)))
    outputs = outputs.reshape(ROWS, LEN, D)
    input_grad = input_grad.reshape(ROWS, LEN, D)
    step_value = float(STEP)
    qkv_grad = totals[0].reshape(-1)
    out_grad = totals[1].reshape(-1)
    up_grad = totals[2].reshape(-1)
    down_grad = totals[3].reshape(-1)
    gain_grad = totals[4]
    bias_grad = totals[5]
    down_bias_grad = bias_grad[6 * D + FF:]
    qkv_new, qkv_first_new, qkv_second_new = adamw_update(qkv_weight, qkv_first, qkv_second, qkv_grad, 0.05, step_value)
    out_new, out_first_new, out_second_new = adamw_update(out_weight, out_first, out_second, out_grad, 0.3, step_value)
    up_new, up_first_new, up_second_new = adamw_update(up_weight, up_first, up_second, up_grad, 0.05, step_value)
    down_new, down_first_new, down_second_new = adamw_update(down_weight, down_first, down_second, down_grad, 0.03, step_value)
    gain_new, gain_first_new, gain_second_new = adamw_update(gains, gain_first, gain_second, gain_grad, 0.2, step_value)
    bias_new, bias_first_new, bias_second_new = adamw_update(biases, bias_first, bias_second, bias_grad, 0.1, step_value)
    return (outputs, input_grad, qkv_grad, qkv_new, qkv_first_new, qkv_second_new, out_grad, out_new, out_first_new, out_second_new, up_grad, up_new, up_first_new, up_second_new, down_grad, down_new, down_first_new, down_second_new, gain_grad, gain_new, gain_first_new, gain_second_new, bias_grad, bias_new, bias_first_new, bias_second_new, down_bias_grad)
```

```python
import functools
import math

import jax
import jax.numpy as jnp
import numpy as np
from jax import lax
from jax.experimental import pallas as pl
from jax.experimental.pallas import tpu as pltpu
from jax.sharding import PartitionSpec as P

D = 480
HEAD_DIM = 24
FF = 1920
STEP = 3
AXES = ("wide", "narrow")

GROUP = 128
PER_GROUP = 5
GROUPS = 4
USED = PER_GROUP * HEAD_DIM
WIDTH = GROUPS * GROUP
HALF = HEAD_DIM // 2
BLOCK = 512
FAR = -1e30
LOG2E = math.log2(math.e)
SCALE = HEAD_DIM**-0.5
VMEM_LIMIT = 56 * 2**20
SAFE = 90.0

f32 = jnp.float32
bf16 = jnp.bfloat16


def contract(left, right, left_dim, right_dim):
    return lax.dot_general(
        left, right, (((left_dim,), (right_dim,)), ((), ())), preferred_element_type=f32
    )


def lanes():
    return lax.broadcasted_iota(jnp.int32, (1, GROUP), 1)


def head_lanes(m):
    lane = lanes()
    return (lane >= HEAD_DIM * m) & (lane < HEAD_DIM * (m + 1))


def of_head(x, m):
    return jnp.where(head_lanes(m) | (lanes() >= USED), x, jnp.zeros_like(x))


def same_head():
    rows = lax.broadcasted_iota(jnp.int32, (GROUP, GROUP), 0) // HEAD_DIM
    columns = lax.broadcasted_iota(jnp.int32, (GROUP, GROUP), 1) // HEAD_DIM
    return jnp.where((rows == columns) & (rows < PER_GROUP), 1.0, 0.0).astype(bf16)


def head_sums(product, same):
    high = product.astype(bf16)
    low = (product - high.astype(f32)).astype(bf16)
    return contract(high, same, 1, 0) + contract(low, same, 1, 0)


def normalized(field):
    average = jnp.mean(field, axis=-1, keepdims=True)
    centered = field - average
    spread = jnp.mean(centered * centered, axis=-1, keepdims=True)
    root = lax.rsqrt(spread + 1e-05)
    return centered * root, root


def norm_back(grad, unit, root, gain_row):
    scaled = grad * gain_row
    return root * (
        scaled
        - jnp.mean(scaled, axis=-1, keepdims=True)
        - unit * jnp.mean(scaled * unit, axis=-1, keepdims=True)
    )


def params(n_axes=1):
    return pltpu.CompilerParams(
        vmem_limit_bytes=VMEM_LIMIT, dimension_semantics=("arbitrary",) * n_axes
    )


def whole(shape):
    return pl.BlockSpec(shape, lambda *_: (0,) * len(shape))


def turn_kernel(
    start_ref, tokens_ref, cotangent_ref, norms_ref, trig_ref, info_ref, spread_ref,
    tokens_out, cotangent_out, normed_out, cosine_out, sine_out, query_out, key_out, pad_out,
):
    length = tokens_ref.shape[0]
    start = start_ref[pl.program_id(0)]
    gain, offset = norms_ref[0:1, :], norms_ref[1:2, :]
    step = 256
    for first in range(0, length, step):
        here = slice(first, first + step)
        target = lax.broadcasted_iota(jnp.int32, (step, length), 0) + (first + start)
        target = jnp.where(target >= length, target - length, target)
        source = lax.broadcasted_iota(jnp.int32, (step, length), 1)
        pick = jnp.where(target == source, 1.0, 0.0).astype(bf16)
        turned = jnp.dot(pick, tokens_ref[...], preferred_element_type=f32)
        tokens_out[here, :] = turned.astype(bf16)
        unit, _ = normalized(turned)
        normed_out[here, :] = (unit * gain + offset).astype(bf16)
        cotangent_out[here, :] = jnp.dot(
            pick, cotangent_ref[...], preferred_element_type=f32
        ).astype(bf16)
    for k, out in ((0, cosine_out), (1, sine_out)):
        part = trig_ref[0, 16 * k : 16 * k + 16, :]
        high = part.astype(bf16)
        rest = part - high.astype(f32)
        middle = rest.astype(bf16)
        low = (rest - middle.astype(f32)).astype(bf16)
        grid = spread_ref[0]
        out[...] = contract(high, grid, 0, 0) + contract(middle, grid, 0, 0) + contract(low, grid, 0, 0)
    info = info_ref[0]
    for k, out in ((1, query_out), (2, key_out), (3, pad_out)):
        out[...] = contract(info, spread_ref[k], 0, 0).astype(bf16)


def turn_rows(start, tokens, cotangent, norms, trig, info, spread):
    rows, length, width = tokens.shape
    row = pl.BlockSpec((length, width), lambda r: (r, 0))
    lane = pl.BlockSpec((length, GROUP), lambda r: (r, 0))
    small = pl.BlockSpec((1,) + trig.shape[1:], lambda r: (r, 0, 0))
    small_info = pl.BlockSpec((1,) + info.shape[1:], lambda r: (r, 0, 0))
    tall = jax.ShapeDtypeStruct((rows * length, width), bf16)

    def lane_shape(kind):
        return jax.ShapeDtypeStruct((rows * length, GROUP), kind)

    return pl.pallas_call(
        turn_kernel,
        grid=(rows,),
        in_specs=[
            pl.BlockSpec(memory_space=pltpu.SMEM), row, row, whole(norms.shape), small, small_info,
            whole(spread.shape),
        ],
        out_specs=[row, row, row, lane, lane, lane, lane, lane],
        out_shape=[tall, tall, tall, lane_shape(f32), lane_shape(f32)] + [lane_shape(bf16)] * 3,
        compiler_params=params(),
    )(
        start, tokens.reshape(rows * length, width), cotangent.reshape(rows * length, width), norms,
        trig, info, spread,
    )


def unturn_kernel(start_ref, outputs_ref, grad_ref, outputs_out, grad_out):
    length = outputs_ref.shape[0]
    start = start_ref[pl.program_id(0)]
    grad = grad_ref[...]
    high = grad.astype(bf16)
    low = (grad - high.astype(f32)).astype(bf16)
    step = 256
    for first in range(0, length, step):
        here = slice(first, first + step)
        target = lax.broadcasted_iota(jnp.int32, (step, length), 0) + (first - start)
        target = jnp.where(target < 0, target + length, target)
        source = lax.broadcasted_iota(jnp.int32, (step, length), 1)
        pick = jnp.where(target == source, 1.0, 0.0).astype(bf16)
        outputs_out[here, :] = jnp.dot(
            pick, outputs_ref[...], preferred_element_type=f32
        ).astype(bf16)
        grad_out[here, :] = jnp.dot(pick, high, preferred_element_type=f32) + jnp.dot(
            pick, low, preferred_element_type=f32
        )


def unturn_rows(start, outputs, grad, length):
    total, width = outputs.shape
    row = pl.BlockSpec((length, width), lambda r: (r, 0))
    return pl.pallas_call(
        unturn_kernel,
        grid=(total // length,),
        in_specs=[pl.BlockSpec(memory_space=pltpu.SMEM), row, row],
        out_specs=[row, row],
        out_shape=[
            jax.ShapeDtypeStruct((total, width), bf16),
            jax.ShapeDtypeStruct((total, width), f32),
        ],
        compiler_params=params(),
    )(start, outputs, grad)


def swap_halves(field, forward):
    low_half = lanes() % HEAD_DIM < HALF
    up = pltpu.roll(field, GROUP - HALF, 1)
    down = pltpu.roll(field, HALF, 1)
    if forward:
        return jnp.where(low_half, -up, down)
    return jnp.where(low_half, up, -down)


def project_kernel(
    normed_ref, gathered_ref, order_ref, bias_ref, cosine_ref, sine_ref, query_lanes, key_lanes,
    q_out, k_out, v_out, weight_out,
):
    @pl.when(pl.program_id(0) == 0)
    def _():
        weight_out[...] = jnp.dot(
            order_ref[...], gathered_ref[...], preferred_element_type=f32
        ).astype(bf16)

    cosine, sine = cosine_ref[...], sine_ref[...]
    own = lanes() < USED
    for g in range(GROUPS):
        to = slice(GROUP * g, GROUP * (g + 1))
        for part, out, factor, spare in (
            (0, q_out, SCALE * LOG2E, query_lanes),
            (1, k_out, 1.0, key_lanes),
        ):
            at = slice(WIDTH * part + GROUP * g, WIDTH * part + GROUP * (g + 1))
            mixed = jnp.dot(
                normed_ref[...], weight_out[:, at], preferred_element_type=f32
            ) + bias_ref[:, at]
            turned = mixed * cosine + swap_halves(mixed, True) * sine
            out[:, to] = jnp.where(own, (turned * factor).astype(bf16), spare[...])
    values = slice(2 * WIDTH, 3 * WIDTH)
    v_out[...] = (
        jnp.dot(normed_ref[...], weight_out[:, values], preferred_element_type=f32)
        + bias_ref[:, values]
    ).astype(bf16)


def project(normed, gathered, order, bias, cosine, sine, query_lanes, key_lanes):
    total = normed.shape[0]
    tile = 512

    def tiled(width):
        return pl.BlockSpec((tile, width), lambda t: (t, 0))

    return pl.pallas_call(
        project_kernel,
        grid=(total // tile,),
        in_specs=[
            tiled(D), whole(gathered.shape), whole(order.shape), whole(bias.shape),
            tiled(GROUP), tiled(GROUP), tiled(GROUP), tiled(GROUP),
        ],
        out_specs=[tiled(WIDTH)] * 3 + [whole((D, 3 * WIDTH))],
        out_shape=[jax.ShapeDtypeStruct((total, WIDTH), bf16)] * 3
        + [jax.ShapeDtypeStruct((D, 3 * WIDTH), bf16)],
        compiler_params=params(),
    )(normed, gathered, order, bias, cosine, sine, query_lanes, key_lanes)


def attend_kernel(q_ref, k_ref, v_ref, pad_ref, attended_out, log_out):
    length = q_ref.shape[0]
    same = same_head()
    own = lanes() < USED
    squares = []
    for ref in (q_ref, k_ref):
        kept = jnp.where(own, ref[...], jnp.zeros((), bf16)).astype(f32)
        sums = contract((kept * kept).astype(bf16), same, 1, 0)
        squares.append(jnp.max(sums, axis=0, keepdims=True))
    safe = jnp.max(squares[0] * squares[1]) <= SAFE * SAFE

    def finish(here, total, weight, shift):
        q, k, v = q_ref[here, :].astype(f32), k_ref[here, :].astype(f32), v_ref[here, :].astype(f32)
        own_score = head_sums(jnp.where(own, q * k, 0.0), same)
        extra = pad_ref[here, :].astype(f32) * jnp.exp2(own_score - shift)
        weight = jnp.where(own, weight + extra, 1.0)
        attended_out[here, :] = ((total + extra * v) / weight).astype(bf16)
        log_out[here, :] = shift + jnp.log2(weight)

    @pl.when(safe)
    def _():
        for first in range(0, length, BLOCK):
            here = slice(first, first + BLOCK)
            k = k_ref[here, :]
            values = jnp.concatenate([v_ref[here, :], jnp.ones((BLOCK, GROUP), bf16)], axis=1)
            total = jnp.zeros((BLOCK, GROUP), f32)
            weight = jnp.zeros((BLOCK, GROUP), f32)
            for m in range(PER_GROUP):
                scores = contract(of_head(q_ref[here, :], m), k, 1, 1)
                probs = jnp.exp2(scores).astype(bf16)
                got = jnp.dot(probs, values, preferred_element_type=f32)
                total = jnp.where(head_lanes(m), got[:, :GROUP], total)
                weight = jnp.where(head_lanes(m), got[:, GROUP:], weight)
            finish(here, total, weight, jnp.zeros((BLOCK, GROUP), f32))

    @pl.when(jnp.logical_not(safe))
    def _():
        for first in range(0, length, BLOCK):
            here = slice(first, first + BLOCK)
            k = k_ref[here, :]
            values = jnp.concatenate([v_ref[here, :], jnp.ones((BLOCK, GROUP), bf16)], axis=1)
            own_score = head_sums(
                jnp.where(own, q_ref[here, :].astype(f32) * k.astype(f32), 0.0), same
            )
            own_score = jnp.where(pad_ref[here, :].astype(f32) > 0.5, own_score, FAR)

            def one_head(m, carry):
                total, weight, shift = carry
                scores = contract(of_head(q_ref[here, :], m), k, 1, 1)
                diagonal = jnp.where(head_lanes(m), own_score, FAR)
                highest = jnp.maximum(
                    jnp.max(scores, axis=1, keepdims=True),
                    jnp.max(diagonal, axis=1, keepdims=True),
                )
                probs = jnp.exp2(scores - highest).astype(bf16)
                got = jnp.dot(probs, values, preferred_element_type=f32)
                return (
                    jnp.where(head_lanes(m), got[:, :GROUP], total),
                    jnp.where(head_lanes(m), got[:, GROUP:], weight),
                    jnp.where(head_lanes(m), highest, shift),
                )

            zero = jnp.zeros((BLOCK, GROUP), f32)
            total, weight, shift = lax.fori_loop(0, PER_GROUP, one_head, (zero, zero, zero))
            finish(here, total, weight, shift)


def attend(q, k, v, pad, length):
    total = q.shape[0]
    block = pl.BlockSpec((length, GROUP), lambda r, g: (r, g))
    pads = pl.BlockSpec((length, GROUP), lambda r, g: (r, 0))
    return pl.pallas_call(
        attend_kernel,
        grid=(total // length, GROUPS),
        in_specs=[block, block, block, pads],
        out_specs=[block, block],
        out_shape=[
            jax.ShapeDtypeStruct((total, WIDTH), bf16),
            jax.ShapeDtypeStruct((total, WIDTH), f32),
        ],
        compiler_params=params(2),
    )(q, k, v, pad)


def attend_back_kernel(
    q_ref, k_ref, v_ref, grad_ref, attended_ref, log_ref, pad_ref, cosine_ref, sine_ref,
    q_out, k_out, v_out,
):
    length = q_ref.shape[0]
    same = same_head()
    own = lanes() < USED
    for first in range(0, length, BLOCK):
        here = slice(first, first + BLOCK)
        q, k, v, grad = q_ref[here, :], k_ref[here, :], v_ref[here, :], grad_ref[here, :]
        logs = log_ref[here, :]
        qf = jnp.where(own, q.astype(f32), 0.0)
        kf = jnp.where(own, k.astype(f32), 0.0)
        vf, gf = v.astype(f32), grad.astype(f32)
        delta = head_sums(gf * attended_ref[here, :].astype(f32), same)
        q_flat = q.astype(f32).T.astype(bf16)
        grad_flat = gf.T.astype(bf16)
        signals, k_heads, grad_keys, grad_values = [], [], [], []
        for m in range(PER_GROUP):
            at = slice(HEAD_DIM * m, HEAD_DIM * (m + 1))
            column = slice(HEAD_DIM * m, HEAD_DIM * m + 1)
            k_head = of_head(k, m)
            scores = contract(q, k_head, 1, 1)
            probs = jnp.exp2(scores - logs[:, column])
            grad_probs = contract(grad, of_head(v, m), 1, 1)
            signal = (probs * (grad_probs - delta[:, column])).astype(bf16)
            grad_values.append(contract(grad_flat[at, :], probs.astype(bf16), 1, 0))
            grad_keys.append(contract(q_flat[at, :], signal, 1, 0))
            signals.append(signal)
            k_heads.append(k_head)
        grad_q = jnp.dot(
            jnp.concatenate(signals, axis=1), jnp.concatenate(k_heads, axis=0), preferred_element_type=f32
        )
        spare = jnp.zeros((GROUP - USED, BLOCK), f32)
        grad_k = jnp.concatenate(grad_keys + [spare], axis=0).T
        grad_v = jnp.concatenate(grad_values + [spare], axis=0).T
        own_score = head_sums(qf * kf, same)
        own_prob = pad_ref[here, :].astype(f32) * jnp.exp2(own_score - logs)
        own_signal = own_prob * (head_sums(gf * vf, same) - delta)
        grad_q = grad_q + own_signal * kf
        grad_k = grad_k + own_signal * qf
        grad_v = grad_v + own_prob * gf
        cosine, sine = cosine_ref[here, :], sine_ref[here, :]
        grad_q = jnp.where(own, grad_q, 0.0)
        q_out[here, :] = (
            SCALE * (grad_q * cosine + swap_halves(grad_q, False) * sine)
        ).astype(bf16)
        k_out[here, :] = (
            (1.0 / LOG2E) * (grad_k * cosine + swap_halves(grad_k, False) * sine)
        ).astype(bf16)
        v_out[here, :] = jnp.where(own, grad_v, 0.0).astype(bf16)


def attend_back(q, k, v, grad, attended, logs, pad, cosine, sine, length):
    total = q.shape[0]
    block = pl.BlockSpec((length, GROUP), lambda r, g: (r, g))
    row = pl.BlockSpec((length, GROUP), lambda r, g: (r, 0))
    return pl.pallas_call(
        attend_back_kernel,
        grid=(total // length, GROUPS),
        in_specs=[block] * 6 + [row] * 3,
        out_specs=[block] * 3,
        out_shape=[jax.ShapeDtypeStruct((total, WIDTH), bf16)] * 3,
        compiler_params=params(2),
    )(q, k, v, grad, attended, logs, pad, cosine, sine)


def gelu_both(v):
    e = jnp.exp2(v * v * (-0.5 * LOG2E))
    t = 1.0 / (1.0 + (0.3275911 / math.sqrt(2.0)) * jnp.abs(v))
    poly = t * (0.5 * 1.061405429) + (0.5 * -1.453152027)
    poly = poly * t + (0.5 * 1.421413741)
    poly = poly * t + (0.5 * -0.284496736)
    poly = poly * t + (0.5 * 0.254829592)
    tail = poly * t * e
    phi = jnp.where(v >= 0.0, 1.0 - tail, tail)
    return v * phi, phi + v * e * (1.0 / math.sqrt(2.0 * math.pi))


UP_AT, DOWN_AT, OUT_AT = 0, FF, FF + 4 * 512
PACK = FF + 4 * 512 + 512
CHUNK = 640


def feed_kernel(
    attended_ref, tokens_ref, cotangent_ref, gathered_ref, order_ref, group_order_ref, rows_ref, up_bias_ref,
    outputs_out, grad_middle_out, grad_attended_out, grads_out, sums_out,
    w_out, w_up, w_down, w_tall, d_out, d_up, d_down,
):
    step = pl.program_id(0)

    @pl.when(step == 0)
    def _():
        order = order_ref[...]
        w_up[...] = jnp.dot(
            order, gathered_ref[:, UP_AT : UP_AT + FF], preferred_element_type=f32
        ).astype(bf16)
        for m in range(4):
            at = DOWN_AT + 512 * m
            part = jnp.dot(order, gathered_ref[:, at : at + 512], preferred_element_type=f32)
            for c in range(0, 512, GROUP):
                w_tall[c // GROUP, pl.ds(m, D, stride=4), :] = part[:, c : c + GROUP]
        for c in range(4):
            n = min(GROUP, D - GROUP * c)
            w_down[:, GROUP * c : GROUP * c + n] = w_tall[c, :, :n].astype(bf16)
        w_out[...] = jnp.dot(
            group_order_ref[...], gathered_ref[:, OUT_AT : OUT_AT + 512], preferred_element_type=f32
        )[:, :D].astype(bf16)
        d_out[...] = jnp.zeros_like(d_out)
        d_up[...] = jnp.zeros_like(d_up)
        d_down[...] = jnp.zeros_like(d_down)
        sums_out[...] = jnp.zeros_like(sums_out)

    attended = attended_ref[...]
    cotangent = cotangent_ref[...]
    out_bias, gain, offset, down_bias = (rows_ref[i : i + 1, :] for i in range(4))
    middle = (
        tokens_ref[...].astype(f32)
        + jnp.dot(attended, w_out[...], preferred_element_type=f32)
        + out_bias
    )
    unit, root = normalized(middle)
    normed = (unit * gain + offset).astype(bf16)
    result = middle + down_bias
    grad_normed = jnp.zeros_like(middle)
    for first in range(0, FF, CHUNK):
        at = slice(first, first + CHUNK)
        hidden = (
            jnp.dot(normed, w_up[:, at], preferred_element_type=f32) + up_bias_ref[:, at]
        )
        active, slope = gelu_both(hidden)
        active = active.astype(bf16)
        result = result + jnp.dot(active, w_down[at, :], preferred_element_type=f32)
        grad_hidden = (contract(cotangent, w_down[at, :], 1, 1) * slope).astype(bf16)
        d_down[at, :] += contract(active, cotangent, 0, 0)
        d_up[:, at] += contract(normed, grad_hidden, 0, 0)
        grad_normed = grad_normed + contract(grad_hidden, w_up[:, at], 1, 1)
        sums_out[0:1, at] += jnp.sum(grad_hidden.astype(f32), axis=0, keepdims=True)
    outputs_out[...] = result.astype(bf16)
    grad_middle = cotangent.astype(f32) + norm_back(grad_normed, unit, root, gain)
    grad_middle_out[...] = grad_middle
    grad_branch = grad_middle.astype(bf16)
    d_out[...] += contract(attended, grad_branch, 0, 0)
    grad_attended_out[...] = contract(grad_branch, w_out[...], 1, 1).astype(bf16)
    for i, terms in enumerate(
        (cotangent.astype(f32), grad_branch.astype(f32), grad_normed * unit, grad_normed)
    ):
        sums_out[i + 1 : i + 2, :D] += jnp.sum(terms, axis=0, keepdims=True)

    @pl.when(step == pl.num_programs(0) - 1)
    def _():
        order = order_ref[...]
        grads_out[:, UP_AT : UP_AT + FF] = contract(order, d_up[...].astype(bf16), 0, 0).astype(bf16)
        for c in range(4):
            n = min(GROUP, D - GROUP * c)
            w_tall[c, :, :n] = d_down[:, GROUP * c : GROUP * c + n]
        for m in range(4):
            for c in range(4):
                at = DOWN_AT + 512 * m + GROUP * c
                part = w_tall[c, pl.ds(m, D, stride=4), :].astype(bf16)
                grads_out[:, at : at + GROUP] = contract(order, part, 0, 0).astype(bf16)
        grads_out[:, OUT_AT : OUT_AT + D] = contract(
            group_order_ref[...], d_out[...].astype(bf16), 0, 0
        ).astype(bf16)
        grads_out[:, OUT_AT + D :] = jnp.zeros_like(grads_out[:, OUT_AT + D :])


def feed(attended, tokens, cotangent, gathered, order, group_order, rows, up_bias):
    total = tokens.shape[0]
    tile = 512

    def tiled(width):
        return pl.BlockSpec((tile, width), lambda t: (t, 0))

    slots = order.shape[1]
    return pl.pallas_call(
        feed_kernel,
        grid=(total // tile,),
        in_specs=[
            tiled(WIDTH), tiled(D), tiled(D), whole(gathered.shape), whole(order.shape),
            whole(group_order.shape), whole(rows.shape), whole(up_bias.shape),
        ],
        out_specs=[tiled(D), tiled(D), tiled(WIDTH), whole((slots, PACK)), whole((8, FF))],
        out_shape=[
            jax.ShapeDtypeStruct((total, D), bf16),
            jax.ShapeDtypeStruct((total, D), f32),
            jax.ShapeDtypeStruct((total, WIDTH), bf16),
            jax.ShapeDtypeStruct((slots, PACK), bf16),
            jax.ShapeDtypeStruct((8, FF), f32),
        ],
        scratch_shapes=[
            pltpu.VMEM((WIDTH, D), bf16),
            pltpu.VMEM((D, FF), bf16),
            pltpu.VMEM((FF, D), bf16),
            pltpu.VMEM((4, FF, GROUP), f32),
            pltpu.VMEM((WIDTH, D), f32),
            pltpu.VMEM((D, FF), f32),
            pltpu.VMEM((FF, D), f32),
        ],
        compiler_params=params(),
    )(attended, tokens, cotangent, gathered, order, group_order, rows, up_bias)


def project_back_kernel(
    dq_ref, dk_ref, dv_ref, normed_ref, tokens_ref, grad_middle_ref, weight_ref, order_ref, gain_ref,
    grad_out, grads_out, sums_out, d_weight,
):
    step = pl.program_id(0)

    @pl.when(step == 0)
    def _():
        d_weight[...] = jnp.zeros_like(d_weight)
        sums_out[...] = jnp.zeros_like(sums_out)

    grad_normed = jnp.zeros(tokens_ref.shape, f32)
    for i, ref in enumerate((dq_ref, dk_ref, dv_ref)):
        at = slice(WIDTH * i, WIDTH * (i + 1))
        grad = ref[...]
        d_weight[:, at] += contract(normed_ref[...], grad, 0, 0)
        grad_normed = grad_normed + contract(grad, weight_ref[:, at], 1, 1)
        sums_out[0:1, at] += jnp.sum(grad.astype(f32), axis=0, keepdims=True)
    unit, root = normalized(tokens_ref[...].astype(f32))
    grad_out[...] = grad_middle_ref[...] + norm_back(grad_normed, unit, root, gain_ref[0:1, :])
    sums_out[1:2, :D] += jnp.sum(grad_normed * unit, axis=0, keepdims=True)
    sums_out[2:3, :D] += jnp.sum(grad_normed, axis=0, keepdims=True)

    @pl.when(step == pl.num_programs(0) - 1)
    def _():
        grads_out[...] = contract(order_ref[...], d_weight[...].astype(bf16), 0, 0).astype(bf16)


def project_back(dq, dk, dv, normed, tokens, grad_middle, weight, order, norms):
    total = tokens.shape[0]
    tile = 512

    def tiled(width):
        return pl.BlockSpec((tile, width), lambda t: (t, 0))

    slots = order.shape[1]
    return pl.pallas_call(
        project_back_kernel,
        grid=(total // tile,),
        in_specs=[tiled(WIDTH)] * 3
        + [tiled(D)] * 3
        + [whole(weight.shape), whole(order.shape), whole(norms.shape)],
        out_specs=[tiled(D), whole((slots, 3 * WIDTH)), whole((8, 3 * WIDTH))],
        out_shape=[
            jax.ShapeDtypeStruct((total, D), f32),
            jax.ShapeDtypeStruct((slots, 3 * WIDTH), bf16),
            jax.ShapeDtypeStruct((8, 3 * WIDTH), f32),
        ],
        scratch_shapes=[pltpu.VMEM((D, 3 * WIDTH), f32)],
        compiler_params=params(),
    )(dq, dk, dv, normed, tokens, grad_middle, weight, order, norms)


class Ring:
    def __init__(self, count):
        self.count = count
        self.bits = [1 << b for b in reversed(range(count.bit_length() - 1))]
        self.masks = [0]
        for bit in self.bits:
            self.masks = self.masks + [bit ^ mask for mask in self.masks]

    def swap(self, x, bit):
        return lax.ppermute(x, AXES, [(i, i ^ bit) for i in range(self.count)])

    def gather(self, x):
        for bit in self.bits:
            x = jnp.concatenate([x, self.swap(x, bit)], axis=0)
        return x

    def scatter_sum(self, x):
        for bit in reversed(self.bits):
            half = x.shape[0] // 2
            got = self.swap(x[half:].astype(bf16), bit)
            x = x[:half].astype(f32) + got.astype(f32)
        return x

    def total(self, x):
        for bit in self.bits:
            x = x + self.swap(x, bit)
        return x


def adamw_update(weight, first, second, gradient, learn_rate):
    first_new = 0.5 * first + 0.5 * gradient
    second_new = 0.5 * second + 0.5 * gradient * gradient
    correction = 1.0 - 0.5 ** float(STEP)
    stepped = first_new / correction / (jnp.sqrt(second_new / correction) + 1e-08)
    return (weight - learn_rate * (stepped + 0.01 * weight), first_new, second_new)


def grouped(rows):
    n, width = rows.shape
    split = rows.reshape(n, width // USED, USED)
    return jnp.pad(split, ((0, 0), (0, 0), (0, GROUP - USED))).reshape(n, width // USED * GROUP)


def ungrouped(rows):
    n, width = rows.shape
    return rows.reshape(n, width // GROUP, GROUP)[:, :, :USED].reshape(n, width // GROUP * USED)


def packed_feed(up, down, out):
    n = up.shape[0]
    down = jnp.pad(down.reshape(n, 4, D), ((0, 0), (0, 0), (0, 512 - D))).reshape(n, 4 * 512)
    return jnp.concatenate([up, down, jnp.pad(out, ((0, 0), (0, 512 - D)))], axis=1)


def unpacked_feed(rows):
    n = rows.shape[0]
    down = rows[:, DOWN_AT : DOWN_AT + 4 * 512].reshape(n, 4, 512)[:, :, :D].reshape(n, FF)
    return rows[:, :FF], down, rows[:, OUT_AT : OUT_AT + D]


def pad_rows(rows, to):
    return jnp.pad(rows, ((0, to - rows.shape[0]), (0, 0)))


def shards(
    devices, tokens, segment_ids, pad_mask, cotangent,
    qkv_weight, qkv_first, qkv_second, out_weight, out_first, out_second,
    up_weight, up_first, up_second, down_weight, down_first, down_second,
    gains, gain_first, gain_second, biases, bias_first, bias_second,
):
    row_count, length, _ = tokens.shape
    ring = Ring(devices)
    own_rows = out_weight.shape[0] // D
    by_rows = out_weight.shape[0] % D == 0
    if by_rows:
        slot = -(-own_rows // 16) * 16
        me = lax.axis_index(AXES)
        qkv_rows = grouped(qkv_weight.astype(bf16).reshape(own_rows, 3 * D))
        qkv_all = ring.gather(pad_rows(qkv_rows, slot))
        feed_rows = packed_feed(
            up_weight.astype(bf16).reshape(own_rows, FF),
            down_weight.astype(bf16).reshape(own_rows, FF),
            out_weight.astype(bf16).reshape(own_rows, D),
        )
        feed_all = ring.gather(pad_rows(feed_rows, slot))
        slots = slot * devices
        place = np.arange(slots)
        masks = jnp.asarray(np.asarray(ring.masks)[place // slot], jnp.int32)
        inner = place % slot
        held = jnp.where(inner < own_rows, (me ^ masks) * own_rows + inner, -1)[None, :]
    else:
        def fetch(weight, width):
            flat = lax.all_gather(weight.astype(bf16), AXES, axis=0, tiled=True)
            return flat.reshape(D, width)

        qkv_all = grouped(fetch(qkv_weight, 3 * D))
        feed_all = packed_feed(fetch(up_weight, FF), fetch(down_weight, FF), fetch(out_weight, D))
        held = jnp.arange(D)[None, :]
    order = (jnp.arange(D)[:, None] == held).astype(bf16)
    wide_row = np.arange(WIDTH)
    wide_row = np.where(wide_row % GROUP < USED, wide_row // GROUP * USED + wide_row % GROUP, -2)
    group_order = (jnp.asarray(wide_row, jnp.int32)[:, None] == held).astype(bf16)

    kinds = jnp.arange(4, dtype=jnp.int32)
    counts = jnp.sum((segment_ids[:, None, :] == kinds[None, :, None]).astype(jnp.int32), axis=2)
    begins = jnp.sum(
        jnp.where(kinds[None, :, None] > kinds[None, None, :], counts[:, None, :], 0), axis=2
    )
    start = jnp.sum(jnp.where(kinds[None, :] == jnp.argmax(counts, axis=1)[:, None], begins, 0), axis=1)
    place = (jnp.arange(length, dtype=jnp.int32)[None, :] + start[:, None]) % length
    among = place[:, None, :] >= begins[:, :, None]
    position = place - jnp.max(jnp.where(among, begins[:, :, None], 0), axis=1)
    segment = jnp.sum(among.astype(jnp.int32), axis=1) - 1
    twice = jnp.concatenate([pad_mask, pad_mask], axis=1)
    present = jnp.stack(
        [lax.dynamic_slice(twice[r], (start[r],), (length,)) for r in range(row_count)]
    ) == 1
    frequency = jnp.exp(jnp.arange(HALF).astype(f32) * (-math.log(10000.0) / HALF))
    phases = position.astype(f32)[:, None, :] * jnp.pad(frequency, (0, 16 - HALF))[None, :, None]
    trig = jnp.concatenate([jnp.cos(phases), jnp.sin(phases)], axis=1)
    is_kind = segment[:, None, :] == kinds[None, :, None]
    info = jnp.concatenate(
        [
            is_kind.astype(f32),
            jnp.where(is_kind & present[:, None, :], 0.0, FAR),
            jnp.where(present, 0.0, 1.0)[:, None, :],
            jnp.zeros((row_count, 7, length), f32),
        ],
        axis=1,
    ).astype(bf16)
    lane = np.arange(GROUP)
    entry = np.arange(16)[:, None]
    spread = np.stack(
        [
            (lane < USED) & (entry == lane % HALF),
            (lane >= USED) & (lane < USED + 4) & (entry == lane - USED),
            (lane >= USED) & (lane < USED + 4) & (entry == lane - USED + 4),
            entry == 8 + 0 * lane,
        ]
    )
    spread = jnp.asarray(spread, bf16)
    norms = jnp.stack([gains[:D], biases[:D]])
    tokens_low, cotangent_low, normed, cosine, sine, query_lanes, key_lanes, pad = turn_rows(
        start, tokens, cotangent, norms, trig, info, spread
    )

    qkv_bias = grouped(biases[D : 4 * D].reshape(1, 3 * D))
    q, k, v, qkv_wide = project(
        normed, qkv_all, order, qkv_bias, cosine, sine, query_lanes, key_lanes
    )
    attended, logs = attend(q, k, v, pad, length)
    rows = jnp.stack(
        [biases[4 * D : 5 * D], gains[D:], biases[5 * D : 6 * D], biases[6 * D + FF :]]
    )
    outputs_low, grad_middle, grad_attended, feed_grads, feed_sums = feed(
        attended, tokens_low, cotangent_low, feed_all, order, group_order, rows,
        biases[6 * D : 6 * D + FF].reshape(1, FF),
    )
    dq, dk, dv = attend_back(
        q, k, v, grad_attended, attended, logs, pad, cosine, sine, length
    )
    grad_tokens, qkv_grads, qkv_sums = project_back(
        dq, dk, dv, normed, tokens_low, grad_middle, qkv_wide, order, norms
    )
    outputs, input_grad = unturn_rows(start, outputs_low, grad_tokens, length)
    outputs = outputs.reshape(tokens.shape)
    input_grad = input_grad.reshape(tokens.shape)

    if by_rows:
        feed_part = ring.scatter_sum(feed_grads)[:own_rows]
        qkv_part = ring.scatter_sum(qkv_grads)[:own_rows]
        up_grad, down_grad, out_grad = (part.reshape(-1) for part in unpacked_feed(feed_part))
        qkv_grad = ungrouped(qkv_part).reshape(-1)
    else:
        def reduce(part):
            return lax.psum_scatter(
                part.astype(f32).reshape(-1), AXES, scatter_dimension=0, tiled=True
            )

        up_grad, down_grad, out_grad = (reduce(part) for part in unpacked_feed(feed_grads))
        qkv_grad = reduce(ungrouped(qkv_grads))
    feed_sums = ring.total(feed_sums)
    qkv_sums = ring.total(qkv_sums)
    gain_grad = jnp.concatenate([qkv_sums[1, :D], feed_sums[3, :D]])
    bias_grad = jnp.concatenate(
        [
            qkv_sums[2, :D], ungrouped(qkv_sums[0:1])[0], feed_sums[2, :D], feed_sums[4, :D],
            feed_sums[0], feed_sums[1, :D],
        ]
    )
    down_bias_grad = bias_grad[6 * D + FF :]
    return (
        outputs,
        input_grad,
        qkv_grad,
        *adamw_update(qkv_weight, qkv_first, qkv_second, qkv_grad, 0.05),
        out_grad,
        *adamw_update(out_weight, out_first, out_second, out_grad, 0.3),
        up_grad,
        *adamw_update(up_weight, up_first, up_second, up_grad, 0.05),
        down_grad,
        *adamw_update(down_weight, down_first, down_second, down_grad, 0.03),
        gain_grad,
        *adamw_update(gains, gain_first, gain_second, gain_grad, 0.2),
        bias_grad,
        *adamw_update(biases, bias_first, bias_second, bias_grad, 0.1),
        down_bias_grad,
    )


def solution(mesh):
    split, copied = P(AXES), P()
    rows, row = P(AXES, None, None), P(AXES, None)
    in_specs = (rows, row, row, rows) + (split,) * 12 + (copied,) * 6
    out_specs = (rows, rows) + (split,) * 16 + (copied,) * 9
    devices = math.prod(mesh.shape[axis] for axis in AXES)
    return jax.shard_map(
        functools.partial(shards, devices),
        mesh=mesh,
        in_specs=in_specs,
        out_specs=out_specs,
        check_vma=False,
    )
```

```python
import functools
import math

import jax
import jax.numpy as jnp
import numpy as np
from jax import lax
from jax.experimental import pallas as pl
from jax.experimental.pallas import tpu as pltpu
from jax.sharding import PartitionSpec as P

D = 480
HEAD_DIM = 24
FF = 1920
STEP = 3
AXES = ("wide", "narrow")

GROUP = 128
PER_GROUP = 5
GROUPS = 4
USED = PER_GROUP * HEAD_DIM
WIDTH = GROUPS * GROUP
HALF = HEAD_DIM // 2
BLOCK = 512
FAR = -1e30
LOG2E = math.log2(math.e)
SCALE = HEAD_DIM**-0.5
VMEM_LIMIT = 56 * 2**20
SAFE = 90.0
SUM_ROWS = 16

f32 = jnp.float32
bf16 = jnp.bfloat16


def contract(left, right, left_dim, right_dim):
    return lax.dot_general(
        left, right, (((left_dim,), (right_dim,)), ((), ())), preferred_element_type=f32
    )


def lanes():
    return lax.broadcasted_iota(jnp.int32, (1, GROUP), 1)


def head_lanes(m):
    lane = lanes()
    return (lane >= HEAD_DIM * m) & (lane < HEAD_DIM * (m + 1))


def of_head(x, m):
    return jnp.where(head_lanes(m) | (lanes() >= USED), x, jnp.zeros_like(x))


def same_head():
    rows = lax.broadcasted_iota(jnp.int32, (GROUP, GROUP), 0) // HEAD_DIM
    columns = lax.broadcasted_iota(jnp.int32, (GROUP, GROUP), 1) // HEAD_DIM
    return jnp.where((rows == columns) & (rows < PER_GROUP), 1.0, 0.0).astype(bf16)


def head_sums(product, same):
    high = product.astype(bf16)
    low = (product - high.astype(f32)).astype(bf16)
    return contract(high, same, 1, 0) + contract(low, same, 1, 0)


def normalized(field):
    average = jnp.mean(field, axis=-1, keepdims=True)
    centered = field - average
    spread = jnp.mean(centered * centered, axis=-1, keepdims=True)
    root = lax.rsqrt(spread + 1e-05)
    return centered * root, root


def norm_back(grad, unit, root, gain_row):
    scaled = grad * gain_row
    return root * (
        scaled
        - jnp.mean(scaled, axis=-1, keepdims=True)
        - unit * jnp.mean(scaled * unit, axis=-1, keepdims=True)
    )


def takes(microseconds):
    return pl.CostEstimate(
        flops=int(microseconds * 1.1e9), bytes_accessed=1024, transcendentals=0
    )


def params(n_axes=1):
    return pltpu.CompilerParams(
        vmem_limit_bytes=VMEM_LIMIT, dimension_semantics=("arbitrary",) * n_axes
    )


def whole(shape):
    return pl.BlockSpec(shape, lambda *_: (0,) * len(shape))


def turn_kernel(
    start_ref, tokens_ref, cotangent_ref, norms_ref, trig_ref, info_ref, spread_ref,
    tokens_out, cotangent_out, normed_out, cosine_out, sine_out, query_out, key_out, pad_out,
):
    length = tokens_ref.shape[2]
    start = start_ref[pl.program_id(0)]
    gain, offset = norms_ref[0:1, :], norms_ref[1:2, :]
    step = 256
    for first in range(0, length, step):
        here = slice(first, first + step)
        target = lax.broadcasted_iota(jnp.int32, (step, length), 0) + (first + start)
        target = jnp.where(target >= length, target - length, target)
        source = lax.broadcasted_iota(jnp.int32, (step, length), 1)
        pick = jnp.where(target == source, 1.0, 0.0).astype(bf16)
        turned = contract(pick, tokens_ref[0], 1, 1)
        tokens_out[here, :] = turned.astype(bf16)
        unit, _ = normalized(turned)
        normed_out[here, :] = (unit * gain + offset).astype(bf16)
        cotangent_out[here, :] = contract(pick, cotangent_ref[0], 1, 1).astype(bf16)
    for k, out in ((0, cosine_out), (1, sine_out)):
        part = trig_ref[0, 16 * k : 16 * k + 16, :]
        high = part.astype(bf16)
        rest = part - high.astype(f32)
        middle = rest.astype(bf16)
        low = (rest - middle.astype(f32)).astype(bf16)
        grid = spread_ref[0]
        out[...] = contract(high, grid, 0, 0) + contract(middle, grid, 0, 0) + contract(low, grid, 0, 0)
    info = info_ref[0]
    for k, out in ((1, query_out), (2, key_out), (3, pad_out)):
        out[...] = contract(info, spread_ref[k], 0, 0).astype(bf16)


def turn_rows(start, tokens, cotangent, norms, trig, info, spread):
    rows, width, length = tokens.shape
    row = pl.BlockSpec((length, width), lambda r: (r, 0))
    flat = pl.BlockSpec((1, width, length), lambda r: (r, 0, 0))
    lane = pl.BlockSpec((length, GROUP), lambda r: (r, 0))
    small = pl.BlockSpec((1,) + trig.shape[1:], lambda r: (r, 0, 0))
    small_info = pl.BlockSpec((1,) + info.shape[1:], lambda r: (r, 0, 0))
    tall = jax.ShapeDtypeStruct((rows * length, width), bf16)

    def lane_shape(kind):
        return jax.ShapeDtypeStruct((rows * length, GROUP), kind)

    return pl.pallas_call(
        turn_kernel,
        grid=(rows,),
        in_specs=[
            pl.BlockSpec(memory_space=pltpu.SMEM), flat, flat, whole(norms.shape), small, small_info,
            whole(spread.shape),
        ],
        out_specs=[row, row, row, lane, lane, lane, lane, lane],
        out_shape=[tall, tall, tall, lane_shape(f32), lane_shape(f32)] + [lane_shape(bf16)] * 3,
        compiler_params=params(),
        cost_estimate=takes(9),
    )(start, tokens, cotangent, norms, trig, info, spread)


def unturn_kernel(start_ref, rows_ref, out_ref):
    length = rows_ref.shape[0]
    start = start_ref[pl.program_id(0)]
    rows = rows_ref[...]
    high = rows.astype(bf16)
    step = 256
    for first in range(0, length, step):
        here = slice(first, first + step)
        target = lax.broadcasted_iota(jnp.int32, (length, step), 1) + (first - start)
        target = jnp.where(target < 0, target + length, target)
        source = lax.broadcasted_iota(jnp.int32, (length, step), 0)
        pick = jnp.where(target == source, 1.0, 0.0).astype(bf16)
        got = contract(high, pick, 0, 0)
        if rows.dtype == f32:
            got = got + contract((rows - high.astype(f32)).astype(bf16), pick, 0, 0)
        out_ref[0, :, here] = got.astype(out_ref.dtype)


def unturn_rows(start, rows, length):
    total, width = rows.shape
    return pl.pallas_call(
        unturn_kernel,
        grid=(total // length,),
        in_specs=[
            pl.BlockSpec(memory_space=pltpu.SMEM),
            pl.BlockSpec((length, width), lambda r: (r, 0)),
        ],
        out_specs=pl.BlockSpec((1, width, length), lambda r: (r, 0, 0)),
        out_shape=jax.ShapeDtypeStruct((total // length, width, length), rows.dtype),
        compiler_params=params(),
        cost_estimate=takes(3 if rows.dtype == bf16 else 6),
    )(start, rows)


def swap_halves(field, forward):
    low_half = lanes() % HEAD_DIM < HALF
    up = pltpu.roll(field, GROUP - HALF, 1)
    down = pltpu.roll(field, HALF, 1)
    if forward:
        return jnp.where(low_half, -up, down)
    return jnp.where(low_half, up, -down)


def in_order(order_ref, gathered_refs, columns):
    got, at = 0.0, 0
    for ref in gathered_refs:
        n = ref.shape[0]
        got = got + jnp.dot(order_ref[:, at : at + n], ref[:, columns], preferred_element_type=f32)
        at += n
    return got


def put_parts(outs, order_ref, columns, grad):
    n = outs[0].shape[0]
    for i, out in enumerate(outs):
        out[:n, columns] = contract(order_ref[:, n * i : n * (i + 1)], grad, 0, 0).astype(bf16)


def split_three(x):
    high = x.astype(bf16)
    rest = x - high.astype(f32)
    middle = rest.astype(bf16)
    return high, middle, (rest - middle.astype(f32)).astype(bf16)


def put_sums(outs, sums_ref):
    for out in outs:
        n = out.shape[0] - SUM_ROWS
        block = jnp.concatenate(
            [part.astype(f32) for part in split_three(sums_ref[0:2, :])]
            + [jnp.zeros((SUM_ROWS - 6, out.shape[1]), f32)],
            axis=0,
        )
        out[n:, :] = block.astype(bf16)


def part_shapes(slots, width, parts):
    n = slots // parts
    return [jax.ShapeDtypeStruct((n, width), bf16)] + [
        jax.ShapeDtypeStruct((n + SUM_ROWS, width), bf16)
    ] * (parts - 1)


def project_kernel(n_gathered, *refs):
    gathered_refs = refs[:n_gathered]
    (
        normed_ref, order_ref, bias_ref, cosine_ref, sine_ref, query_lanes, key_lanes,
        q_out, k_out, v_out, weight_out,
    ) = refs[n_gathered:]

    @pl.when(pl.program_id(0) == 0)
    def _():
        weight_out[...] = in_order(order_ref, gathered_refs, slice(None)).astype(bf16)

    cosine, sine = cosine_ref[...], sine_ref[...]
    own = lanes() < USED
    for g in range(GROUPS):
        to = slice(GROUP * g, GROUP * (g + 1))
        for part, out, factor, spare in (
            (0, q_out, SCALE * LOG2E, query_lanes),
            (1, k_out, 1.0, key_lanes),
        ):
            at = slice(WIDTH * part + GROUP * g, WIDTH * part + GROUP * (g + 1))
            mixed = jnp.dot(
                normed_ref[...], weight_out[:, at], preferred_element_type=f32
            ) + bias_ref[:, at]
            turned = mixed * cosine + swap_halves(mixed, True) * sine
            out[:, to] = jnp.where(own, (turned * factor).astype(bf16), spare[...])
    values = slice(2 * WIDTH, 3 * WIDTH)
    v_out[...] = (
        jnp.dot(normed_ref[...], weight_out[:, values], preferred_element_type=f32)
        + bias_ref[:, values]
    ).astype(bf16)


def project(normed, gathered, order, bias, cosine, sine, query_lanes, key_lanes):
    total = normed.shape[0]
    tile = 512

    def tiled(width):
        return pl.BlockSpec((tile, width), lambda t: (t, 0))

    return pl.pallas_call(
        functools.partial(project_kernel, len(gathered)),
        grid=(total // tile,),
        in_specs=[whole(x.shape) for x in gathered]
        + [
            tiled(D), whole(order.shape), whole(bias.shape),
            tiled(GROUP), tiled(GROUP), tiled(GROUP), tiled(GROUP),
        ],
        out_specs=[tiled(WIDTH)] * 3 + [whole((D, 3 * WIDTH))],
        out_shape=[jax.ShapeDtypeStruct((total, WIDTH), bf16)] * 3
        + [jax.ShapeDtypeStruct((D, 3 * WIDTH), bf16)],
        compiler_params=params(),
        cost_estimate=takes(10),
    )(*gathered, normed, order, bias, cosine, sine, query_lanes, key_lanes)


def attend_kernel(q_ref, k_ref, v_ref, pad_ref, attended_out, log_out):
    length = q_ref.shape[0]
    same = same_head()
    own = lanes() < USED
    squares = []
    for ref in (q_ref, k_ref):
        kept = jnp.where(own, ref[...], jnp.zeros((), bf16)).astype(f32)
        sums = contract((kept * kept).astype(bf16), same, 1, 0)
        squares.append(jnp.max(sums, axis=0, keepdims=True))
    safe = jnp.max(squares[0] * squares[1]) <= SAFE * SAFE

    def finish(here, total, weight, shift):
        q, k, v = q_ref[here, :].astype(f32), k_ref[here, :].astype(f32), v_ref[here, :].astype(f32)
        own_score = head_sums(jnp.where(own, q * k, 0.0), same)
        extra = pad_ref[here, :].astype(f32) * jnp.exp2(own_score - shift)
        weight = jnp.where(own, weight + extra, 1.0)
        attended_out[here, :] = ((total + extra * v) / weight).astype(bf16)
        log_out[here, :] = shift + jnp.log2(weight)

    @pl.when(safe)
    def _():
        for first in range(0, length, BLOCK):
            here = slice(first, first + BLOCK)
            k = k_ref[here, :]
            values = jnp.concatenate([v_ref[here, :], jnp.ones((BLOCK, GROUP), bf16)], axis=1)
            total = jnp.zeros((BLOCK, GROUP), f32)
            weight = jnp.zeros((BLOCK, GROUP), f32)
            for m in range(PER_GROUP):
                scores = contract(of_head(q_ref[here, :], m), k, 1, 1)
                probs = jnp.exp2(scores).astype(bf16)
                got = jnp.dot(probs, values, preferred_element_type=f32)
                total = jnp.where(head_lanes(m), got[:, :GROUP], total)
                weight = jnp.where(head_lanes(m), got[:, GROUP:], weight)
            finish(here, total, weight, jnp.zeros((BLOCK, GROUP), f32))

    @pl.when(jnp.logical_not(safe))
    def _():
        for first in range(0, length, BLOCK):
            here = slice(first, first + BLOCK)
            k = k_ref[here, :]
            values = jnp.concatenate([v_ref[here, :], jnp.ones((BLOCK, GROUP), bf16)], axis=1)
            own_score = head_sums(
                jnp.where(own, q_ref[here, :].astype(f32) * k.astype(f32), 0.0), same
            )
            own_score = jnp.where(pad_ref[here, :].astype(f32) > 0.5, own_score, FAR)

            def one_head(m, carry):
                total, weight, shift = carry
                scores = contract(of_head(q_ref[here, :], m), k, 1, 1)
                diagonal = jnp.where(head_lanes(m), own_score, FAR)
                highest = jnp.maximum(
                    jnp.max(scores, axis=1, keepdims=True),
                    jnp.max(diagonal, axis=1, keepdims=True),
                )
                probs = jnp.exp2(scores - highest).astype(bf16)
                got = jnp.dot(probs, values, preferred_element_type=f32)
                return (
                    jnp.where(head_lanes(m), got[:, :GROUP], total),
                    jnp.where(head_lanes(m), got[:, GROUP:], weight),
                    jnp.where(head_lanes(m), highest, shift),
                )

            zero = jnp.zeros((BLOCK, GROUP), f32)
            total, weight, shift = lax.fori_loop(0, PER_GROUP, one_head, (zero, zero, zero))
            finish(here, total, weight, shift)


def attend(q, k, v, pad, length, first, count):
    total = q.shape[0]
    block = pl.BlockSpec((length, GROUP), lambda r, g: (r, first + g))
    out = pl.BlockSpec((length, GROUP), lambda r, g: (r, g))
    pads = pl.BlockSpec((length, GROUP), lambda r, g: (r, 0))
    return pl.pallas_call(
        attend_kernel,
        grid=(total // length, count),
        in_specs=[block, block, block, pads],
        out_specs=[out, out],
        out_shape=[
            jax.ShapeDtypeStruct((total, GROUP * count), bf16),
            jax.ShapeDtypeStruct((total, GROUP * count), f32),
        ],
        compiler_params=params(2),
        cost_estimate=takes(8 * count),
    )(q, k, v, pad)


def attend_back_kernel(
    q_ref, k_ref, v_ref, grad_ref, attended_ref, log_ref, pad_ref, cosine_ref, sine_ref,
    q_out, k_out, v_out,
):
    length = q_ref.shape[0]
    same = same_head()
    own = lanes() < USED
    for first in range(0, length, BLOCK):
        here = slice(first, first + BLOCK)
        q, k, v, grad = q_ref[here, :], k_ref[here, :], v_ref[here, :], grad_ref[here, :]
        logs = log_ref[here, :]
        qf = jnp.where(own, q.astype(f32), 0.0)
        kf = jnp.where(own, k.astype(f32), 0.0)
        vf, gf = v.astype(f32), grad.astype(f32)
        delta = head_sums(gf * attended_ref[here, :].astype(f32), same)
        q_flat = q.astype(f32).T.astype(bf16)
        grad_flat = gf.T.astype(bf16)
        signals, k_heads, grad_keys, grad_values = [], [], [], []
        for m in range(PER_GROUP):
            at = slice(HEAD_DIM * m, HEAD_DIM * (m + 1))
            column = slice(HEAD_DIM * m, HEAD_DIM * m + 1)
            k_head = of_head(k, m)
            scores = contract(q, k_head, 1, 1)
            probs = jnp.exp2(scores - logs[:, column])
            grad_probs = contract(grad, of_head(v, m), 1, 1)
            signal = (probs * (grad_probs - delta[:, column])).astype(bf16)
            grad_values.append(contract(grad_flat[at, :], probs.astype(bf16), 1, 0))
            grad_keys.append(contract(q_flat[at, :], signal, 1, 0))
            signals.append(signal)
            k_heads.append(k_head)
        grad_q = jnp.dot(
            jnp.concatenate(signals, axis=1), jnp.concatenate(k_heads, axis=0), preferred_element_type=f32
        )
        spare = jnp.zeros((GROUP - USED, BLOCK), f32)
        grad_k = jnp.concatenate(grad_keys + [spare], axis=0).T
        grad_v = jnp.concatenate(grad_values + [spare], axis=0).T
        own_score = head_sums(qf * kf, same)
        own_prob = pad_ref[here, :].astype(f32) * jnp.exp2(own_score - logs)
        own_signal = own_prob * (head_sums(gf * vf, same) - delta)
        grad_q = grad_q + own_signal * kf
        grad_k = grad_k + own_signal * qf
        grad_v = grad_v + own_prob * gf
        cosine, sine = cosine_ref[here, :], sine_ref[here, :]
        grad_q = jnp.where(own, grad_q, 0.0)
        q_out[here, :] = (
            SCALE * (grad_q * cosine + swap_halves(grad_q, False) * sine)
        ).astype(bf16)
        k_out[here, :] = (
            (1.0 / LOG2E) * (grad_k * cosine + swap_halves(grad_k, False) * sine)
        ).astype(bf16)
        v_out[here, :] = jnp.where(own, grad_v, 0.0).astype(bf16)


def attend_back(q, k, v, grad, attended, logs, pad, cosine, sine, length, first, count, held):
    total = q.shape[0]
    block = pl.BlockSpec((length, GROUP), lambda r, g: (r, first + g))
    saved = pl.BlockSpec((length, GROUP), lambda r, g: (r, first - held + g))
    out = pl.BlockSpec((length, GROUP), lambda r, g: (r, g))
    row = pl.BlockSpec((length, GROUP), lambda r, g: (r, 0))
    return pl.pallas_call(
        attend_back_kernel,
        grid=(total // length, count),
        in_specs=[block] * 4 + [saved] * 2 + [row] * 3,
        out_specs=[out] * 3,
        out_shape=[jax.ShapeDtypeStruct((total, GROUP * count), bf16)] * 3,
        compiler_params=params(2),
        cost_estimate=takes(15 * count),
    )(q, k, v, grad, attended, logs, pad, cosine, sine)


def gelu_both(v):
    e = jnp.exp2(v * v * (-0.5 * LOG2E))
    t = 1.0 / (1.0 + (0.3275911 / math.sqrt(2.0)) * jnp.abs(v))
    poly = t * (0.5 * 1.061405429) + (0.5 * -1.453152027)
    poly = poly * t + (0.5 * 1.421413741)
    poly = poly * t + (0.5 * -0.284496736)
    poly = poly * t + (0.5 * 0.254829592)
    tail = poly * t * e
    phi = jnp.where(v >= 0.0, 1.0 - tail, tail)
    return v * phi, phi + v * e * (1.0 / math.sqrt(2.0 * math.pi))


UP_AT, DOWN_AT, OUT_AT = 0, FF, FF + 4 * 512
PACK = FF + 4 * 512 + 512
CHUNK = 640


def feed_kernel(
    n_attended, n_gathered, *refs
):
    attended_refs, refs = refs[:n_attended], refs[n_attended:]
    gathered_refs, refs = refs[:n_gathered], refs[n_gathered:]
    (
        tokens_ref, cotangent_ref, order_ref, group_order_ref, rows_ref, up_bias_ref,
        outputs_out, grad_middle_out, grad_attended_out, sums_out, *refs,
    ) = refs
    *grads_outs, w_out, w_up, w_down, w_tall, d_out, d_up, d_down = refs
    step = pl.program_id(0)

    @pl.when(step == 0)
    def _():
        w_up[...] = in_order(order_ref, gathered_refs, slice(UP_AT, UP_AT + FF)).astype(bf16)
        for m in range(4):
            at = DOWN_AT + 512 * m
            part = in_order(order_ref, gathered_refs, slice(at, at + 512))
            for c in range(0, 512, GROUP):
                w_tall[c // GROUP, pl.ds(m, D, stride=4), :] = part[:, c : c + GROUP]
        for c in range(4):
            n = min(GROUP, D - GROUP * c)
            w_down[:, GROUP * c : GROUP * c + n] = w_tall[c, :, :n].astype(bf16)
        w_out[...] = in_order(group_order_ref, gathered_refs, slice(OUT_AT, OUT_AT + 512))[
            :, :D
        ].astype(bf16)
        d_out[...] = jnp.zeros_like(d_out)
        d_up[...] = jnp.zeros_like(d_up)
        d_down[...] = jnp.zeros_like(d_down)
        sums_out[...] = jnp.zeros_like(sums_out)

    attended = jnp.concatenate([ref[...] for ref in attended_refs], axis=1)
    cotangent = cotangent_ref[...]
    out_bias, gain, offset, down_bias = (rows_ref[i : i + 1, :] for i in range(4))
    middle = (
        tokens_ref[...].astype(f32)
        + jnp.dot(attended, w_out[...], preferred_element_type=f32)
        + out_bias
    )
    unit, root = normalized(middle)
    normed = (unit * gain + offset).astype(bf16)
    result = middle + down_bias
    grad_normed = jnp.zeros_like(middle)
    for first in range(0, FF, CHUNK):
        at = slice(first, first + CHUNK)
        hidden = (
            jnp.dot(normed, w_up[:, at], preferred_element_type=f32) + up_bias_ref[:, at]
        )
        active, slope = gelu_both(hidden)
        active = active.astype(bf16)
        result = result + jnp.dot(active, w_down[at, :], preferred_element_type=f32)
        grad_hidden = (contract(cotangent, w_down[at, :], 1, 1) * slope).astype(bf16)
        d_down[at, :] += contract(active, cotangent, 0, 0)
        d_up[:, at] += contract(normed, grad_hidden, 0, 0)
        grad_normed = grad_normed + contract(grad_hidden, w_up[:, at], 1, 1)
        sums_out[0:1, at] += jnp.sum(grad_hidden.astype(f32), axis=0, keepdims=True)
    outputs_out[...] = result.astype(bf16)
    grad_middle = cotangent.astype(f32) + norm_back(grad_normed, unit, root, gain)
    grad_middle_out[...] = grad_middle
    grad_branch = grad_middle.astype(bf16)
    d_out[...] += contract(attended, grad_branch, 0, 0)
    grad_attended_out[...] = contract(grad_branch, w_out[...], 1, 1).astype(bf16)
    for i, terms in enumerate(
        (cotangent.astype(f32), grad_branch.astype(f32), grad_normed * unit, grad_normed)
    ):
        at = FF + 512 * i
        sums_out[0:1, at : at + D] += jnp.sum(terms, axis=0, keepdims=True)

    @pl.when(step == pl.num_programs(0) - 1)
    def _():
        put_parts(grads_outs, order_ref, slice(UP_AT, UP_AT + FF), d_up[...].astype(bf16))
        for c in range(4):
            n = min(GROUP, D - GROUP * c)
            w_tall[c, :, :n] = d_down[:, GROUP * c : GROUP * c + n]
        for m in range(4):
            for c in range(4):
                at = DOWN_AT + 512 * m + GROUP * c
                part = w_tall[c, pl.ds(m, D, stride=4), :].astype(bf16)
                put_parts(grads_outs, order_ref, slice(at, at + GROUP), part)
        put_parts(grads_outs, group_order_ref, slice(OUT_AT, OUT_AT + D), d_out[...].astype(bf16))
        put_sums(grads_outs[1:], sums_out)


def feed(attended, tokens, cotangent, gathered, order, group_order, rows, up_bias, parts):
    total = tokens.shape[0]
    tile = 512

    def tiled(width):
        return pl.BlockSpec((tile, width), lambda t: (t, 0))

    grads = part_shapes(order.shape[1], PACK, parts)
    return pl.pallas_call(
        functools.partial(feed_kernel, len(attended), len(gathered)),
        grid=(total // tile,),
        in_specs=[tiled(x.shape[1]) for x in attended]
        + [whole(x.shape) for x in gathered]
        + [
            tiled(D), tiled(D), whole(order.shape), whole(group_order.shape), whole(rows.shape),
            whole(up_bias.shape),
        ],
        out_specs=[tiled(D), tiled(D), tiled(WIDTH), whole((8, PACK))]
        + [whole(x.shape) for x in grads],
        out_shape=[
            jax.ShapeDtypeStruct((total, D), bf16),
            jax.ShapeDtypeStruct((total, D), f32),
            jax.ShapeDtypeStruct((total, WIDTH), bf16),
            jax.ShapeDtypeStruct((8, PACK), f32),
        ]
        + grads,
        scratch_shapes=[
            pltpu.VMEM((WIDTH, D), bf16),
            pltpu.VMEM((D, FF), bf16),
            pltpu.VMEM((FF, D), bf16),
            pltpu.VMEM((4, FF, GROUP), f32),
            pltpu.VMEM((WIDTH, D), f32),
            pltpu.VMEM((D, FF), f32),
            pltpu.VMEM((FF, D), f32),
        ],
        compiler_params=params(),
        cost_estimate=takes(50),
    )(*attended, *gathered, tokens, cotangent, order, group_order, rows, up_bias)


def project_back_kernel(n_parts, *refs):
    grad_refs = [refs[n_parts * i : n_parts * (i + 1)] for i in range(3)]
    (
        normed_ref, tokens_ref, grad_middle_ref, weight_ref, order_ref, gain_ref,
        grad_out, sums_out, *grads_outs, d_weight,
    ) = refs[3 * n_parts :]
    step = pl.program_id(0)

    @pl.when(step == 0)
    def _():
        d_weight[...] = jnp.zeros_like(d_weight)
        sums_out[...] = jnp.zeros_like(sums_out)

    grad_normed = jnp.zeros(tokens_ref.shape, f32)
    for i, parts in enumerate(grad_refs):
        at = slice(WIDTH * i, WIDTH * (i + 1))
        grad = jnp.concatenate([ref[...] for ref in parts], axis=1)
        d_weight[:, at] += contract(normed_ref[...], grad, 0, 0)
        grad_normed = grad_normed + contract(grad, weight_ref[:, at], 1, 1)
        sums_out[0:1, at] += jnp.sum(grad.astype(f32), axis=0, keepdims=True)
    unit, root = normalized(tokens_ref[...].astype(f32))
    grad_out[...] = grad_middle_ref[...] + norm_back(grad_normed, unit, root, gain_ref[0:1, :])
    sums_out[1:2, :D] += jnp.sum(grad_normed * unit, axis=0, keepdims=True)
    sums_out[1:2, 512 : 512 + D] += jnp.sum(grad_normed, axis=0, keepdims=True)

    @pl.when(step == pl.num_programs(0) - 1)
    def _():
        put_parts(grads_outs, order_ref, slice(None), d_weight[...].astype(bf16))
        put_sums(grads_outs[1:], sums_out)


def project_back(dq, dk, dv, normed, tokens, grad_middle, weight, order, norms, parts):
    total = tokens.shape[0]
    tile = 512

    def tiled(width):
        return pl.BlockSpec((tile, width), lambda t: (t, 0))

    grads = part_shapes(order.shape[1], 3 * WIDTH, parts)
    return pl.pallas_call(
        functools.partial(project_back_kernel, len(dq)),
        grid=(total // tile,),
        in_specs=[tiled(x.shape[1]) for x in dq + dk + dv]
        + [tiled(D)] * 3
        + [whole(weight.shape), whole(order.shape), whole(norms.shape)],
        out_specs=[tiled(D), whole((8, 3 * WIDTH))] + [whole(x.shape) for x in grads],
        out_shape=[
            jax.ShapeDtypeStruct((total, D), f32),
            jax.ShapeDtypeStruct((8, 3 * WIDTH), f32),
        ]
        + grads,
        scratch_shapes=[pltpu.VMEM((D, 3 * WIDTH), f32)],
        compiler_params=params(),
        cost_estimate=takes(12),
    )(*dq, *dk, *dv, normed, tokens, grad_middle, weight, order, norms)


def merge_kernel(n_got, n_parts, *refs):
    kept_ref, got_refs = refs[0], refs[1 : 1 + n_got]
    own_ref = refs[1 + n_got]
    kept_out, sums_out, *sent_outs = refs[2 + n_got :]
    rows = kept_ref.shape[0]
    n = rows // n_parts
    for i in range(n_parts):
        at = slice(n * i, n * (i + 1))
        block = kept_ref[at, :].astype(f32)
        for ref in got_refs:
            block = block + ref[at, :].astype(f32)
        if i == 0:
            kept_out[...] = block
        else:
            sent_outs[i - 1][:n, :] = block.astype(bf16)
    terms = [own_ref[0:2, :]]
    for ref in got_refs:
        tail = ref[rows:, :].astype(f32)
        terms.append((tail[0:2] + tail[2:4]) + tail[4:6])
    while len(terms) > 1:
        terms = [a + b for a, b in zip(terms[0::2], terms[1::2])]
    sums_out[...] = jnp.zeros_like(sums_out)
    sums_out[0:2, :] = terms[0]
    put_sums(sent_outs, sums_out)


def merge(kept, got, sums, parts):
    rows, width = kept.shape
    n = rows // parts
    sent = [jax.ShapeDtypeStruct((n + SUM_ROWS, width), bf16)] * (parts - 1)
    shapes = [jax.ShapeDtypeStruct((n, width), f32), jax.ShapeDtypeStruct(sums.shape, f32)] + sent
    return pl.pallas_call(
        functools.partial(merge_kernel, len(got), parts),
        in_specs=[pl.BlockSpec(memory_space=pltpu.VMEM)] * (2 + len(got)),
        out_specs=[pl.BlockSpec(memory_space=pltpu.VMEM)] * len(shapes),
        out_shape=shapes,
        compiler_params=pltpu.CompilerParams(vmem_limit_bytes=VMEM_LIMIT),
        cost_estimate=takes(2),
    )(kept, *got, sums)


class Exchange:
    def __init__(self, count):
        self.count = count
        bits = [1 << b for b in reversed(range(count.bit_length() - 1))]
        self.stages = []
        for i in range(0, len(bits) - 1, 2):
            low, high = bits[i + 1], bits[i]
            self.stages.append([low, high, low | high])
        if len(bits) % 2:
            self.stages.append([bits[-1]])
        self.masks = [0]
        for stage in self.stages:
            self.masks = [bit ^ mask for bit in [0] + stage for mask in self.masks]
        self.parts = len(self.stages[-1]) + 1 if self.stages else 1

    def swap(self, x, bit):
        return lax.ppermute(x, AXES, [(i, i ^ bit) for i in range(self.count)])

    def swaps(self, x, stage):
        return [self.swap(x, bit) for bit in stage]

    def gather(self, x, works=()):
        results = []
        for i, stage in enumerate(self.stages):
            got = self.swaps(x, stage)
            if i < len(works):
                results.append(works[i](x))
                got = [after(part, results[-1]) for part in got]
            last = i == len(self.stages) - 1
            x = [x] + got if last else jnp.concatenate([x] + got, axis=0)
        results += [work(x[0]) for work in works[len(self.stages) :]]
        return x, results

    def scatter_sum(self, kept, sent, sums, works):
        stages, results = self.stages[::-1], []
        for i, stage in enumerate(stages):
            got = [self.swap(x, bit) for x, bit in zip(sent, stage)]
            if i < len(works):
                results.append(works[i](kept))
                got = [after(part, results[-1]) for part in got]
            parts = len(stages[i + 1]) + 1 if i + 1 < len(stages) else 1
            kept, sums, *sent = merge(kept, got, sums, parts)
        results += [work(kept) for work in works[len(stages) :]]
        return kept, sums, results

    def total(self, x):
        for stage in self.stages:
            terms = [x] + self.swaps(x, stage)
            while len(terms) > 1:
                terms = [a + b for a, b in zip(terms[0::2], terms[1::2])]
            x = terms[0]
        return x


def after(x, earlier):
    return lax.optimization_barrier((x, earlier))[0]


def adamw_update(weight, first, second, gradient, learn_rate):
    first_new = 0.5 * first + 0.5 * gradient
    second_new = 0.5 * second + 0.5 * gradient * gradient
    correction = 1.0 - 0.5 ** float(STEP)
    stepped = first_new / correction / (jnp.sqrt(second_new / correction) + 1e-08)
    return (weight - learn_rate * (stepped + 0.01 * weight), first_new, second_new)


def grouped(rows):
    n, width = rows.shape
    split = rows.reshape(n, width // USED, USED)
    return jnp.pad(split, ((0, 0), (0, 0), (0, GROUP - USED))).reshape(n, width // USED * GROUP)


def ungrouped(rows):
    n, width = rows.shape
    return rows.reshape(n, width // GROUP, GROUP)[:, :, :USED].reshape(n, width // GROUP * USED)


def packed_feed(up, down, out):
    n = up.shape[0]
    down = jnp.pad(down.reshape(n, 4, D), ((0, 0), (0, 0), (0, 512 - D))).reshape(n, 4 * 512)
    return jnp.concatenate([up, down, jnp.pad(out, ((0, 0), (0, 512 - D)))], axis=1)


def unpacked_feed(rows):
    n = rows.shape[0]
    down = rows[:, DOWN_AT : DOWN_AT + 4 * 512].reshape(n, 4, 512)[:, :, :D].reshape(n, FF)
    return rows[:, :FF], down, rows[:, OUT_AT : OUT_AT + D]


def pad_rows(rows, to):
    return jnp.pad(rows, ((0, to - rows.shape[0]), (0, 0)))


def shards(
    devices, tokens, segment_ids, pad_mask, cotangent,
    qkv_weight, qkv_first, qkv_second, out_weight, out_first, out_second,
    up_weight, up_first, up_second, down_weight, down_first, down_second,
    gains, gain_first, gain_second, biases, bias_first, bias_second,
):
    row_count, length, _ = tokens.shape
    ring = Exchange(devices)
    own_rows = out_weight.shape[0] // D
    by_rows = out_weight.shape[0] % D == 0
    slot = -(-own_rows // 16) * 16 if by_rows else D
    parts = ring.parts if by_rows else 1

    kinds = jnp.arange(4, dtype=jnp.int32)
    counts = jnp.sum((segment_ids[:, None, :] == kinds[None, :, None]).astype(jnp.int32), axis=2)
    begins = jnp.sum(
        jnp.where(kinds[None, :, None] > kinds[None, None, :], counts[:, None, :], 0), axis=2
    )
    start = jnp.sum(jnp.where(kinds[None, :] == jnp.argmax(counts, axis=1)[:, None], begins, 0), axis=1)
    place = (jnp.arange(length, dtype=jnp.int32)[None, :] + start[:, None]) % length
    among = place[:, None, :] >= begins[:, :, None]
    position = place - jnp.max(jnp.where(among, begins[:, :, None], 0), axis=1)
    segment = jnp.sum(among.astype(jnp.int32), axis=1) - 1
    twice = jnp.concatenate([pad_mask, pad_mask], axis=1)
    present = jnp.stack(
        [lax.dynamic_slice(twice[r], (start[r],), (length,)) for r in range(row_count)]
    ) == 1
    frequency = jnp.exp(jnp.arange(HALF).astype(f32) * (-math.log(10000.0) / HALF))
    phases = position.astype(f32)[:, None, :] * jnp.pad(frequency, (0, 16 - HALF))[None, :, None]
    trig = jnp.concatenate([jnp.cos(phases), jnp.sin(phases)], axis=1)
    is_kind = segment[:, None, :] == kinds[None, :, None]
    info = jnp.concatenate(
        [
            is_kind.astype(f32),
            jnp.where(is_kind & present[:, None, :], 0.0, FAR),
            jnp.where(present, 0.0, 1.0)[:, None, :],
            jnp.zeros((row_count, 7, length), f32),
        ],
        axis=1,
    ).astype(bf16)
    lane = np.arange(GROUP)
    entry = np.arange(16)[:, None]
    spread = np.stack(
        [
            (lane < USED) & (entry == lane % HALF),
            (lane >= USED) & (lane < USED + 4) & (entry == lane - USED),
            (lane >= USED) & (lane < USED + 4) & (entry == lane - USED + 4),
            entry == 8 + 0 * lane,
        ]
    )
    spread = jnp.asarray(spread, bf16)
    norms = jnp.stack([gains[:D], biases[:D]])

    def turned(sent):
        return turn_rows(
            start, after(jnp.swapaxes(tokens, 1, 2), sent), jnp.swapaxes(cotangent, 1, 2), norms, trig, info,
            spread,
        )

    def prepared(sent):
        small, feed_weights, out_weights, me = after(
            (biases, (up_weight, down_weight), out_weight, lax.axis_index(AXES)), sent
        )
        if by_rows:
            slots = slot * devices
            place = np.arange(slots)
            masks = jnp.asarray(np.asarray(ring.masks)[place // slot], jnp.int32)
            inner = place % slot
            held = jnp.where(inner < own_rows, (me ^ masks) * own_rows + inner, -1)[None, :]
        else:
            held = jnp.arange(D)[None, :]
        order = (jnp.arange(D)[:, None] == held).astype(bf16)
        wide_row = np.arange(WIDTH)
        wide_row = np.where(
            wide_row % GROUP < USED, wide_row // GROUP * USED + wide_row % GROUP, -2
        )
        group_order = (jnp.asarray(wide_row, jnp.int32)[:, None] == held).astype(bf16)
        qkv_bias = grouped(small[D : 4 * D].reshape(1, 3 * D))
        rows = jnp.stack(
            [small[4 * D : 5 * D], gains[D:], small[5 * D : 6 * D], small[6 * D + FF :]]
        )
        up_bias = small[6 * D : 6 * D + FF].reshape(1, FF)
        if by_rows:
            feed_rows = packed_feed(
                feed_weights[0].astype(bf16).reshape(own_rows, FF),
                feed_weights[1].astype(bf16).reshape(own_rows, FF),
                out_weights.astype(bf16).reshape(own_rows, D),
            )
            feed_rows = pad_rows(feed_rows, slot)
        else:
            feed_rows = packed_feed(
                fetch(feed_weights[0], FF), fetch(feed_weights[1], FF), fetch(out_weights, D)
            )
        return order, group_order, qkv_bias, rows, up_bias, feed_rows

    def fetch(weight, width):
        flat = lax.all_gather(weight.astype(bf16), AXES, axis=0, tiled=True)
        return flat.reshape(D, width)

    if by_rows:
        qkv_rows = grouped(qkv_weight.astype(bf16).reshape(own_rows, 3 * D))
        qkv_all, (first_turned, small) = ring.gather(
            pad_rows(qkv_rows, slot), (turned, prepared)
        )
    else:
        qkv_all = [grouped(fetch(qkv_weight, 3 * D))]
        first_turned, small = turned(qkv_all[0]), prepared(qkv_all[0])
    tokens_low, cotangent_low, normed, cosine, sine, query_lanes, key_lanes, pad = first_turned
    order, group_order, qkv_bias, rows, up_bias, feed_rows = small

    def projected(sent):
        return project(
            after(normed, sent), qkv_all, order, qkv_bias, cosine, sine, query_lanes, key_lanes
        )

    made = []

    def attending(first, count):
        def work(sent):
            q, k, v, _ = made[0]
            made.append(attend(after(q, sent), k, v, pad, length, first, count))
            return made[-1]

        return work

    def projecting(sent):
        made.append(projected(sent))
        return made[-1]

    works = (projecting, attending(0, 3), attending(3, 1))
    if by_rows:
        feed_all, _ = ring.gather(feed_rows, works)
    else:
        feed_all = [feed_rows]
        for work in works:
            work(feed_rows)
    (q, k, v, qkv_wide), *saved = made
    outputs_low, grad_middle, grad_attended, feed_sums, *feed_grads = feed(
        [attended for attended, _ in saved], tokens_low, cotangent_low, feed_all, order, group_order,
        rows, up_bias, parts,
    )

    def attending_back(first, count, which, held):
        def work(sent):
            return attend_back(
                q, k, v, after(grad_attended, sent), *saved[which], pad, cosine, sine, length,
                first, count, held,
            )

        return work

    works = (attending_back(0, 1, 0, 0), attending_back(1, 2, 0, 0), attending_back(3, 1, 1, 3))
    if by_rows:
        feed_part, feed_sums, backs = ring.scatter_sum(feed_grads[0], feed_grads[1:], feed_sums, works)
    else:
        feed_part, backs = feed_grads[0], [work(feed_sums) for work in works]
    dq, dk, dv = (list(x) for x in zip(*backs))
    grad_tokens, qkv_sums, *qkv_grads = project_back(
        dq, dk, dv, after(normed, feed_part), tokens_low, grad_middle, qkv_wide, order, norms, parts
    )

    def outputs_back(sent):
        return jnp.swapaxes(unturn_rows(start, after(outputs_low, sent), length), 1, 2)

    def grads_back(sent):
        return jnp.swapaxes(unturn_rows(start, after(grad_tokens, sent), length), 1, 2)

    def feed_updated(sent):
        part = after(feed_part, sent)
        if by_rows:
            grads = [x.reshape(-1) for x in unpacked_feed(part[:own_rows])]
        else:
            grads = [reduce(x) for x in unpacked_feed(part)]
        up_grad, down_grad, out_grad = grads
        return (
            (up_grad, *adamw_update(up_weight, up_first, up_second, up_grad, 0.05)),
            (down_grad, *adamw_update(down_weight, down_first, down_second, down_grad, 0.03)),
            (out_grad, *adamw_update(out_weight, out_first, out_second, out_grad, 0.3)),
        )

    def reduce(part):
        return lax.psum_scatter(part.astype(f32).reshape(-1), AXES, scatter_dimension=0, tiled=True)

    works = (outputs_back, grads_back, feed_updated)
    if by_rows:
        qkv_part, qkv_sums, results = ring.scatter_sum(qkv_grads[0], qkv_grads[1:], qkv_sums, works)
        qkv_grad = ungrouped(qkv_part[:own_rows]).reshape(-1)
    else:
        results = [work(qkv_sums) for work in works]
        qkv_grad = reduce(ungrouped(qkv_grads[0]))
        feed_sums, qkv_sums = ring.total(feed_sums), ring.total(qkv_sums)
    outputs, input_grad, (up_results, down_results, out_results) = results
    down_sum, out_sum, gain_sum, offset_sum = (
        feed_sums[0, at : at + D] for at in range(FF, FF + 4 * 512, 512)
    )
    gain_grad = jnp.concatenate([qkv_sums[1, :D], gain_sum])
    bias_grad = jnp.concatenate(
        [
            qkv_sums[1, 512 : 512 + D], ungrouped(qkv_sums[0:1])[0], out_sum, offset_sum,
            feed_sums[0, :FF], down_sum,
        ]
    )
    return (
        outputs,
        input_grad,
        qkv_grad,
        *adamw_update(qkv_weight, qkv_first, qkv_second, qkv_grad, 0.05),
        *out_results,
        *up_results,
        *down_results,
        gain_grad,
        *adamw_update(gains, gain_first, gain_second, gain_grad, 0.2),
        bias_grad,
        *adamw_update(biases, bias_first, bias_second, bias_grad, 0.1),
        bias_grad[6 * D + FF :],
    )


def solution(mesh):
    split, copied = P(AXES), P()
    rows, row = P(AXES, None, None), P(AXES, None)
    in_specs = (rows, row, row, rows) + (split,) * 12 + (copied,) * 6
    out_specs = (rows, rows) + (split,) * 16 + (copied,) * 9
    devices = math.prod(mesh.shape[axis] for axis in AXES)
    return jax.shard_map(
        functools.partial(shards, devices),
        mesh=mesh,
        in_specs=in_specs,
        out_specs=out_specs,
        check_vma=False,
    )
```

```python
import functools
import math

import jax
import jax.numpy as jnp
import numpy as np
from jax import lax
from jax.experimental import pallas as pl
from jax.experimental.pallas import tpu as pltpu
from jax.sharding import PartitionSpec as P

D = 480
HEAD_DIM = 24
FF = 1920
STEP = 3
AXES = ("wide", "narrow")

GROUP = 128
PER_GROUP = 5
GROUPS = 4
USED = PER_GROUP * HEAD_DIM
WIDTH = GROUPS * GROUP
HALF = HEAD_DIM // 2
BLOCK = 512
FAR = -1e30
LOG2E = math.log2(math.e)
SCALE = HEAD_DIM**-0.5
VMEM_LIMIT = 56 * 2**20
SAFE = 60.0
ATTEND = 1024
ATTEND_BACK = 512
SUM_ROWS = 16

f32 = jnp.float32
bf16 = jnp.bfloat16


def contract(left, right, left_dim, right_dim):
    return lax.dot_general(
        left, right, (((left_dim,), (right_dim,)), ((), ())), preferred_element_type=f32
    )


def lanes():
    return lax.broadcasted_iota(jnp.int32, (1, GROUP), 1)


def head_lanes(m):
    lane = lanes()
    return (lane >= HEAD_DIM * m) & (lane < HEAD_DIM * (m + 1))


def of_head(x, m):
    return jnp.where(head_lanes(m) | (lanes() >= USED), x, jnp.zeros_like(x))


def same_head():
    rows = lax.broadcasted_iota(jnp.int32, (GROUP, GROUP), 0) // HEAD_DIM
    columns = lax.broadcasted_iota(jnp.int32, (GROUP, GROUP), 1) // HEAD_DIM
    return jnp.where((rows == columns) & (rows < PER_GROUP), 1.0, 0.0).astype(bf16)


def head_sums(product, same):
    high = product.astype(bf16)
    low = (product - high.astype(f32)).astype(bf16)
    return contract(high, same, 1, 0) + contract(low, same, 1, 0)


def normalized(field):
    average = jnp.mean(field, axis=-1, keepdims=True)
    centered = field - average
    spread = jnp.mean(centered * centered, axis=-1, keepdims=True)
    root = lax.rsqrt(spread + 1e-05)
    return centered * root, root


def norm_back(grad, unit, root, gain_row):
    scaled = grad * gain_row
    return root * (
        scaled
        - jnp.mean(scaled, axis=-1, keepdims=True)
        - unit * jnp.mean(scaled * unit, axis=-1, keepdims=True)
    )


def takes(microseconds):
    return pl.CostEstimate(
        flops=int(microseconds * 1.1e9), bytes_accessed=1024, transcendentals=0
    )


def params(n_axes=1):
    return pltpu.CompilerParams(
        vmem_limit_bytes=VMEM_LIMIT, dimension_semantics=("arbitrary",) * n_axes
    )


def whole(shape):
    return pl.BlockSpec(shape, lambda *_: (0,) * len(shape))


def turn_kernel(
    segments_ref, mask_ref, tokens_ref, cotangent_ref, gains_ref, biases_ref,
    tokens_out, cotangent_out, normed_out, cosine_out, sine_out, query_out, key_out, pad_out, start_out,
):
    length = tokens_ref.shape[2]
    r = pl.program_id(0)
    segments = segments_ref[pl.ds(r, 1), :]
    counts = [jnp.sum(jnp.where(segments == c, 1.0, 0.0)) for c in range(3)]
    begins = [counts[0], counts[0] + counts[1], counts[0] + counts[1] + counts[2]]
    start = begins[2]
    for c, begin in ((2, begins[1]), (1, begins[0]), (0, 0.0)):
        start = jnp.where(counts[c] == float(BLOCK), begin, start)
    start_out[r] = start

    def places(shape, dim, first):
        place = lax.broadcasted_iota(jnp.int32, shape, dim).astype(f32) + (start + float(first))
        return jnp.where(place >= float(length), place - float(length), place)

    place = places((1, length), 1, 0)
    begin = jnp.where(place >= begins[0], begins[0], 0.0)
    for c in (1, 2):
        begin = jnp.where(place >= begins[c], begins[c], begin)
    exponent = lax.broadcasted_iota(jnp.int32, (16, 1), 0).astype(f32)
    phases = (place - begin) * jnp.exp(exponent * (-math.log(10000.0) / HALF))
    lane = lax.broadcasted_iota(jnp.int32, (16, GROUP), 1)
    entry = lax.broadcasted_iota(jnp.int32, (16, GROUP), 0)
    grid = jnp.where((lane < USED) & (lane % HALF == entry), 1.0, 0.0).astype(bf16)
    for part, out in ((jnp.cos(phases), cosine_out), (jnp.sin(phases), sine_out)):
        high, middle, low = split_three(part)
        out[...] = contract(high, grid, 0, 0) + contract(middle, grid, 0, 0) + contract(low, grid, 0, 0)

    mask = jnp.broadcast_to(mask_ref[pl.ds(r, 1), :].astype(f32), (GROUP, length)).astype(bf16)
    gain, offset = gains_ref[:, :D], biases_ref[:, :D]
    step = 256
    spare = lax.broadcasted_iota(jnp.int32, (step, GROUP), 1).astype(f32) - float(USED)
    for first in range(0, length, step):
        here = slice(first, first + step)
        source = lax.broadcasted_iota(jnp.int32, (step, length), 1).astype(f32)
        pick = jnp.where(places((step, length), 0, first) == source, 1.0, 0.0).astype(bf16)
        turned = contract(pick, tokens_ref[0], 1, 1)
        tokens_out[here, :] = turned.astype(bf16)
        unit, _ = normalized(turned)
        normed_out[here, :] = (unit * gain + offset).astype(bf16)
        cotangent_out[here, :] = contract(pick, cotangent_ref[0], 1, 1).astype(bf16)
        present = contract(pick, mask, 1, 1)
        place = places((step, GROUP), 0, first)
        segment = sum(jnp.where(place >= begin, 1.0, 0.0) for begin in begins)
        mine = segment == spare
        query_out[here, :] = jnp.where(mine, 1.0, 0.0).astype(bf16)
        key_out[here, :] = jnp.where(mine & (present > 0.5), 0.0, FAR).astype(bf16)
        pad_out[here, :] = (1.0 - present).astype(bf16)


def turn_rows(segments, mask, tokens, cotangent, gains, biases):
    rows, width, length = tokens.shape
    row = pl.BlockSpec((length, width), lambda r: (r, 0))
    flat = pl.BlockSpec((1, width, length), lambda r: (r, 0, 0))
    lane = pl.BlockSpec((length, GROUP), lambda r: (r, 0))
    tall = jax.ShapeDtypeStruct((rows * length, width), bf16)

    def lane_shape(kind):
        return jax.ShapeDtypeStruct((rows * length, GROUP), kind)

    return pl.pallas_call(
        turn_kernel,
        grid=(rows,),
        in_specs=[
            whole(segments.shape), whole(mask.shape), flat, flat, whole(gains.shape), whole(biases.shape),
        ],
        out_specs=[row] * 3 + [lane] * 5 + [pl.BlockSpec(memory_space=pltpu.SMEM)],
        out_shape=[tall, tall, tall, lane_shape(f32), lane_shape(f32)]
        + [lane_shape(bf16)] * 3
        + [jax.ShapeDtypeStruct((rows,), f32)],
        compiler_params=params(),
        cost_estimate=takes(12),
    )(segments, mask, tokens, cotangent, gains, biases)


def unturn_kernel(start_ref, rows_ref, out_ref):
    length = rows_ref.shape[0]
    start = start_ref[pl.program_id(0)]
    rows = rows_ref[...]
    high = rows.astype(bf16)
    step = 256
    for first in range(0, length, step):
        here = slice(first, first + step)
        target = lax.broadcasted_iota(jnp.int32, (length, step), 1).astype(f32) + (float(first) - start)
        target = jnp.where(target < 0.0, target + float(length), target)
        source = lax.broadcasted_iota(jnp.int32, (length, step), 0).astype(f32)
        pick = jnp.where(target == source, 1.0, 0.0).astype(bf16)
        got = contract(high, pick, 0, 0)
        if rows.dtype == f32:
            got = got + contract((rows - high.astype(f32)).astype(bf16), pick, 0, 0)
        out_ref[0, :, here] = got.astype(out_ref.dtype)


def unturn_rows(start, rows, length):
    total, width = rows.shape
    return pl.pallas_call(
        unturn_kernel,
        grid=(total // length,),
        in_specs=[
            pl.BlockSpec(memory_space=pltpu.SMEM),
            pl.BlockSpec((length, width), lambda r: (r, 0)),
        ],
        out_specs=pl.BlockSpec((1, width, length), lambda r: (r, 0, 0)),
        out_shape=jax.ShapeDtypeStruct((total // length, width, length), rows.dtype),
        compiler_params=params(),
        cost_estimate=takes(3 if rows.dtype == bf16 else 6),
    )(start, rows)


def swap_halves(field, forward):
    low_half = lanes() % HEAD_DIM < HALF
    up = pltpu.roll(field, GROUP - HALF, 1)
    down = pltpu.roll(field, HALF, 1)
    if forward:
        return jnp.where(low_half, -up, down)
    return jnp.where(low_half, up, -down)


def order_of(held_ref):
    shape = (D, held_ref.shape[1])
    row = lax.broadcasted_iota(jnp.int32, shape, 0)
    return jnp.where(row == held_ref[...], 1.0, 0.0).astype(bf16)


def group_order_of(held_ref):
    shape = (WIDTH, held_ref.shape[1])
    row = lax.broadcasted_iota(jnp.int32, shape, 0)
    row = jnp.where(row % GROUP < USED, row // GROUP * USED + row % GROUP, -2)
    return jnp.where(row == held_ref[...], 1.0, 0.0).astype(bf16)


def in_order(order, gathered_refs, columns):
    got, at = 0.0, 0
    for ref in gathered_refs:
        n = ref.shape[0]
        got = got + jnp.dot(order[:, at : at + n], ref[:, columns], preferred_element_type=f32)
        at += n
    return got


def put_parts(outs, order, columns, grad):
    n = outs[0].shape[0]
    for i, out in enumerate(outs):
        out[:n, columns] = contract(order[:, n * i : n * (i + 1)], grad, 0, 0).astype(bf16)


def split_three(x):
    high = x.astype(bf16)
    rest = x - high.astype(f32)
    middle = rest.astype(bf16)
    return high, middle, (rest - middle.astype(f32)).astype(bf16)


def put_sums(outs, sums_ref):
    for out in outs:
        n = out.shape[0] - SUM_ROWS
        block = jnp.concatenate(
            [part.astype(f32) for part in split_three(sums_ref[0:2, :])]
            + [jnp.zeros((SUM_ROWS - 6, out.shape[1]), f32)],
            axis=0,
        )
        out[n:, :] = block.astype(bf16)


def part_shapes(slots, width, parts):
    n = slots // parts
    return [jax.ShapeDtypeStruct((n, width), bf16)] + [
        jax.ShapeDtypeStruct((n + SUM_ROWS, width), bf16)
    ] * (parts - 1)


def project_kernel(n_gathered, *refs):
    gathered_refs = refs[:n_gathered]
    (
        normed_ref, held_ref, biases_ref, cosine_ref, sine_ref, query_lanes, key_lanes,
        q_out, k_out, v_out, weight_out, bias_ref,
    ) = refs[n_gathered:]

    @pl.when(pl.program_id(0) == 0)
    def _():
        weight_out[...] = in_order(order_of(held_ref), gathered_refs, slice(None)).astype(bf16)
        bias_ref[...] = jnp.zeros_like(bias_ref)
        for i in range(3 * GROUPS):
            at = D + USED * i
            bias_ref[:, GROUP * i : GROUP * i + USED] = biases_ref[:, at : at + USED]

    cosine, sine = cosine_ref[...], sine_ref[...]
    own = lanes() < USED
    for g in range(GROUPS):
        to = slice(GROUP * g, GROUP * (g + 1))
        for part, out, factor, spare in (
            (0, q_out, SCALE, query_lanes),
            (1, k_out, 1.0, key_lanes),
        ):
            at = slice(WIDTH * part + GROUP * g, WIDTH * part + GROUP * (g + 1))
            mixed = jnp.dot(
                normed_ref[...], weight_out[:, at], preferred_element_type=f32
            ) + bias_ref[:, at]
            turned = mixed * cosine + swap_halves(mixed, True) * sine
            out[:, to] = jnp.where(own, (turned * factor).astype(bf16), spare[...])
    values = slice(2 * WIDTH, 3 * WIDTH)
    v_out[...] = (
        jnp.dot(normed_ref[...], weight_out[:, values], preferred_element_type=f32)
        + bias_ref[:, values]
    ).astype(bf16)


def project(normed, gathered, held, biases, cosine, sine, query_lanes, key_lanes):
    total = normed.shape[0]
    tile = 512

    def tiled(width):
        return pl.BlockSpec((tile, width), lambda t: (t, 0))

    return pl.pallas_call(
        functools.partial(project_kernel, len(gathered)),
        grid=(total // tile,),
        in_specs=[whole(x.shape) for x in gathered]
        + [
            tiled(D), whole(held.shape), whole(biases.shape),
            tiled(GROUP), tiled(GROUP), tiled(GROUP), tiled(GROUP),
        ],
        out_specs=[tiled(WIDTH)] * 3 + [whole((D, 3 * WIDTH))],
        out_shape=[jax.ShapeDtypeStruct((total, WIDTH), bf16)] * 3
        + [jax.ShapeDtypeStruct((D, 3 * WIDTH), bf16)],
        scratch_shapes=[pltpu.VMEM((1, 3 * WIDTH), f32)],
        compiler_params=params(),
        cost_estimate=takes(10),
    )(*gathered, normed, held, biases, cosine, sine, query_lanes, key_lanes)


def heads_flat(field, spare):
    flat = field.astype(f32).T
    tail = jnp.full((8, field.shape[0]), spare, f32)
    return [
        jnp.concatenate([flat[HEAD_DIM * m : HEAD_DIM * (m + 1)], tail], axis=0).astype(bf16)
        for m in range(PER_GROUP)
    ]


def attend_kernel(q_ref, k_ref, v_ref, pad_ref, attended_out, probs_out, scale_out, own_out):
    length = q_ref.shape[0]
    same = same_head()
    own = lanes() < USED
    squares = []
    for ref in (q_ref, k_ref):
        kept = jnp.where(own, ref[...], jnp.zeros((), bf16))
        squares.append(jnp.max(contract(kept * kept, same, 1, 0), axis=0, keepdims=True))
    safe = jnp.max(squares[0] * squares[1]) <= SAFE * SAFE

    def diagonal(here):
        q, k = q_ref[here, :].astype(f32), k_ref[here, :].astype(f32)
        return head_sums(jnp.where(own, q * k, 0.0), same) * LOG2E

    def block_of(first):
        here = slice(first, first + BLOCK)
        values = jnp.concatenate([v_ref[here, :], jnp.ones((BLOCK, GROUP), bf16)], axis=1)
        return here, k_ref[here, :], values

    def rows_of(first, m):
        return pl.ds((first // BLOCK * PER_GROUP + m) * BLOCK, BLOCK)

    @pl.when(safe)
    def _():
        for first in range(0, length, BLOCK):
            here, k, values = block_of(first)
            total = jnp.zeros((BLOCK, GROUP), f32)
            weight = jnp.zeros((BLOCK, GROUP), f32)
            for m in range(PER_GROUP):
                scores = contract(of_head(q_ref[here, :], m), k, 1, 1)
                probs = jnp.exp2(scores * LOG2E).astype(bf16)
                probs_out[rows_of(first, m), :] = probs
                got = jnp.dot(probs, values, preferred_element_type=f32)
                total = jnp.where(head_lanes(m), got[:, :GROUP], total)
                weight = jnp.where(head_lanes(m), got[:, GROUP:], weight)
            extra = pad_ref[here, :].astype(f32) * jnp.exp2(diagonal(here))
            scale = 1.0 / jnp.where(own, weight + extra, 1.0)
            extra = extra * scale
            attended_out[here, :] = (total * scale + extra * v_ref[here, :].astype(f32)).astype(bf16)
            scale_out[here, :] = scale
            own_out[here, :] = extra.astype(bf16)

    @pl.when(jnp.logical_not(safe))
    def _():
        for first in range(0, length, BLOCK):
            here, k, values = block_of(first)
            padded = pad_ref[here, :].astype(f32)
            on_diagonal = jnp.where(padded > 0.5, diagonal(here), FAR)

            def one_head(m, carry):
                total, extra = carry
                scores = contract(of_head(q_ref[here, :], m), k, 1, 1) * LOG2E
                mine = jnp.where(head_lanes(m), on_diagonal, FAR)
                single = jnp.max(mine, axis=1, keepdims=True)
                highest = jnp.maximum(jnp.max(scores, axis=1, keepdims=True), single)
                weight = jnp.sum(jnp.exp2(scores - highest), axis=1, keepdims=True)
                shift = highest + jnp.log2(weight + jnp.exp2(single - highest))
                probs = jnp.exp2(scores - shift).astype(bf16)
                probs_out[rows_of(first, m), :] = probs
                got = jnp.dot(probs, values, preferred_element_type=f32)
                return (
                    jnp.where(head_lanes(m), got[:, :GROUP], total),
                    jnp.where(head_lanes(m), jnp.exp2(single - shift), extra),
                )

            zero = jnp.zeros((BLOCK, GROUP), f32)
            total, extra = lax.fori_loop(0, PER_GROUP, one_head, (zero, zero))
            attended_out[here, :] = (total + extra * v_ref[here, :].astype(f32)).astype(bf16)
            scale_out[here, :] = jnp.ones((BLOCK, GROUP), f32)
            own_out[here, :] = extra.astype(bf16)


def attend(q, k, v, pad, first, count):
    total = q.shape[0]
    block = pl.BlockSpec((ATTEND, GROUP), lambda r, g: (r, first + g))
    out = pl.BlockSpec((ATTEND, GROUP), lambda r, g: (r, g))
    pads = pl.BlockSpec((ATTEND, GROUP), lambda r, g: (r, 0))
    width = GROUP * count
    return pl.pallas_call(
        attend_kernel,
        grid=(total // ATTEND, count),
        in_specs=[block, block, block, pads],
        out_specs=[
            out, pl.BlockSpec((PER_GROUP * ATTEND, BLOCK), lambda r, g: (r * count + g, 0)), out, out,
        ],
        out_shape=[
            jax.ShapeDtypeStruct((total, width), bf16),
            jax.ShapeDtypeStruct((total * count * PER_GROUP, BLOCK), bf16),
            jax.ShapeDtypeStruct((total, width), f32),
            jax.ShapeDtypeStruct((total, width), bf16),
        ],
        compiler_params=params(2),
        cost_estimate=takes(8 * count),
    )(q, k, v, pad)


def attend_back_kernel(
    q_ref, k_ref, v_ref, grad_ref, attended_ref, probs_ref, scale_ref, own_ref, cosine_ref, sine_ref,
    q_out, k_out, v_out,
):
    same = same_head()
    own = lanes() < USED
    for first in range(0, q_ref.shape[0], BLOCK):
        here = slice(first, first + BLOCK)
        v = v_ref[here, :]
        qf, kf, vf = q_ref[here, :].astype(f32), k_ref[here, :].astype(f32), v.astype(f32)
        gf, scale = grad_ref[here, :].astype(f32), scale_ref[here, :]
        delta = head_sums(gf * attended_ref[here, :].astype(f32), same)
        scaled = (gf * scale).astype(bf16)
        scaled_delta = delta * scale
        q_flat = heads_flat(jnp.where(own, qf, 0.0), 0.0)
        grad_flat = heads_flat(scaled, 0.0)
        k_flat = heads_flat(jnp.where(own, kf, 0.0), 0.0)
        grad_queries, grad_keys, grad_values = [], [], []
        for m in range(PER_GROUP):
            column = slice(HEAD_DIM * m, HEAD_DIM * m + 1)
            row = (first // BLOCK * PER_GROUP + m) * BLOCK
            probs = probs_ref[row : row + BLOCK, :]
            grad_probs = contract(scaled, jnp.where(head_lanes(m), v, jnp.zeros_like(v)), 1, 1)
            signal = (probs.astype(f32) * (grad_probs - scaled_delta[:, column])).astype(bf16)
            grad_values.append(contract(grad_flat[m], probs, 1, 0)[:HEAD_DIM])
            grad_keys.append(contract(q_flat[m], signal, 1, 0)[:HEAD_DIM])
            grad_queries.append(contract(k_flat[m], signal, 1, 1)[:HEAD_DIM])
        spare = jnp.zeros((GROUP - USED, BLOCK), f32)
        grad_q = jnp.concatenate(grad_queries + [spare], axis=0).T
        grad_k = jnp.concatenate(grad_keys + [spare], axis=0).T
        grad_v = jnp.concatenate(grad_values + [spare], axis=0).T
        own_prob = own_ref[here, :].astype(f32)
        own_signal = own_prob * (head_sums(gf * vf, same) - delta)
        grad_q = jnp.where(own, grad_q + own_signal * kf, 0.0)
        grad_k = jnp.where(own, grad_k + own_signal * qf, 0.0)
        grad_v = grad_v + own_prob * gf
        cosine, sine = cosine_ref[here, :], sine_ref[here, :]
        q_out[here, :] = (
            SCALE * (grad_q * cosine + swap_halves(grad_q, False) * sine)
        ).astype(bf16)
        k_out[here, :] = (grad_k * cosine + swap_halves(grad_k, False) * sine).astype(bf16)
        v_out[here, :] = grad_v.astype(bf16)


def attend_back(q, k, v, grad, attended, probs, scale, own, cosine, sine, first, count, held):
    total = q.shape[0]
    kept, per = attended.shape[1] // GROUP, ATTEND // ATTEND_BACK

    def at(offset):
        return pl.BlockSpec((ATTEND_BACK, GROUP), lambda r, g: (r, offset + g))

    saved, row = at(first - held), pl.BlockSpec((ATTEND_BACK, GROUP), lambda r, g: (r, 0))
    probs_block = pl.BlockSpec(
        (PER_GROUP * ATTEND_BACK, BLOCK),
        lambda r, g: ((r // per * kept + first - held + g) * per + r % per, 0),
    )
    return pl.pallas_call(
        attend_back_kernel,
        grid=(total // ATTEND_BACK, count),
        in_specs=[at(first)] * 4 + [saved, probs_block, saved, saved, row, row],
        out_specs=[at(0)] * 3,
        out_shape=[jax.ShapeDtypeStruct((total, GROUP * count), bf16)] * 3,
        compiler_params=params(2),
        cost_estimate=takes(14 * count),
    )(q, k, v, grad, attended, probs, scale, own, cosine, sine)


def gelu_both(v):
    e = jnp.exp2(v * v * (-0.5 * LOG2E))
    t = 1.0 / (1.0 + (0.3275911 / math.sqrt(2.0)) * jnp.abs(v))
    poly = t * (0.5 * 1.061405429) + (0.5 * -1.453152027)
    poly = poly * t + (0.5 * 1.421413741)
    poly = poly * t + (0.5 * -0.284496736)
    poly = poly * t + (0.5 * 0.254829592)
    tail = poly * t * e
    phi = jnp.where(v >= 0.0, 1.0 - tail, tail)
    return v * phi, phi + v * e * (1.0 / math.sqrt(2.0 * math.pi))


UP_AT, DOWN_AT, OUT_AT = 0, FF, FF + 4 * 512
PACK = FF + 4 * 512 + 512
CHUNK = 640


def feed_kernel(
    n_attended, n_gathered, *refs
):
    attended_refs, refs = refs[:n_attended], refs[n_attended:]
    gathered_refs, refs = refs[:n_gathered], refs[n_gathered:]
    (
        tokens_ref, cotangent_ref, held_ref, gains_ref, biases_ref,
        outputs_out, grad_middle_out, grad_attended_out, sums_out, *refs,
    ) = refs
    *grads_outs, w_out, w_up, w_down, w_tall, d_out, d_up, d_down = refs
    step = pl.program_id(0)

    @pl.when(step == 0)
    def _():
        order = order_of(held_ref)
        w_up[...] = in_order(order, gathered_refs, slice(UP_AT, UP_AT + FF)).astype(bf16)
        for m in range(4):
            at = DOWN_AT + 512 * m
            part = in_order(order, gathered_refs, slice(at, at + 512))
            for c in range(0, 512, GROUP):
                w_tall[c // GROUP, pl.ds(m, D, stride=4), :] = part[:, c : c + GROUP]
        for c in range(4):
            n = min(GROUP, D - GROUP * c)
            w_down[:, GROUP * c : GROUP * c + n] = w_tall[c, :, :n].astype(bf16)
        w_out[...] = in_order(group_order_of(held_ref), gathered_refs, slice(OUT_AT, OUT_AT + 512))[
            :, :D
        ].astype(bf16)
        d_out[...] = jnp.zeros_like(d_out)
        d_up[...] = jnp.zeros_like(d_up)
        d_down[...] = jnp.zeros_like(d_down)
        sums_out[...] = jnp.zeros_like(sums_out)

    attended = jnp.concatenate([ref[...] for ref in attended_refs], axis=1)
    cotangent = cotangent_ref[...]
    out_bias, offset = biases_ref[:, 4 * D : 5 * D], biases_ref[:, 5 * D : 6 * D]
    gain, down_bias = gains_ref[:, D:], biases_ref[:, 6 * D + FF :]
    middle = (
        tokens_ref[...].astype(f32)
        + jnp.dot(attended, w_out[...], preferred_element_type=f32)
        + out_bias
    )
    unit, root = normalized(middle)
    normed = (unit * gain + offset).astype(bf16)
    result = middle + down_bias
    grad_normed = jnp.zeros_like(middle)
    for first in range(0, FF, CHUNK):
        at = slice(first, first + CHUNK)
        hidden = (
            jnp.dot(normed, w_up[:, at], preferred_element_type=f32) + biases_ref[:, 6 * D + first : 6 * D + first + CHUNK]
        )
        active, slope = gelu_both(hidden)
        active = active.astype(bf16)
        result = result + jnp.dot(active, w_down[at, :], preferred_element_type=f32)
        grad_hidden = (contract(cotangent, w_down[at, :], 1, 1) * slope).astype(bf16)
        d_down[at, :] += contract(active, cotangent, 0, 0)
        d_up[:, at] += contract(normed, grad_hidden, 0, 0)
        grad_normed = grad_normed + contract(grad_hidden, w_up[:, at], 1, 1)
        sums_out[0:1, at] += jnp.sum(grad_hidden.astype(f32), axis=0, keepdims=True)
    outputs_out[...] = result.astype(bf16)
    grad_middle = cotangent.astype(f32) + norm_back(grad_normed, unit, root, gain)
    grad_middle_out[...] = grad_middle
    grad_branch = grad_middle.astype(bf16)
    d_out[...] += contract(attended, grad_branch, 0, 0)
    grad_attended_out[...] = contract(grad_branch, w_out[...], 1, 1).astype(bf16)
    for i, terms in enumerate(
        (cotangent.astype(f32), grad_branch.astype(f32), grad_normed * unit, grad_normed)
    ):
        at = FF + 512 * i
        sums_out[0:1, at : at + D] += jnp.sum(terms, axis=0, keepdims=True)

    @pl.when(step == pl.num_programs(0) - 1)
    def _():
        order = order_of(held_ref)
        put_parts(grads_outs, order, slice(UP_AT, UP_AT + FF), d_up[...].astype(bf16))
        for c in range(4):
            n = min(GROUP, D - GROUP * c)
            w_tall[c, :, :n] = d_down[:, GROUP * c : GROUP * c + n]
        for m in range(4):
            for c in range(4):
                at = DOWN_AT + 512 * m + GROUP * c
                part = w_tall[c, pl.ds(m, D, stride=4), :].astype(bf16)
                put_parts(grads_outs, order, slice(at, at + GROUP), part)
        put_parts(
            grads_outs, group_order_of(held_ref), slice(OUT_AT, OUT_AT + D), d_out[...].astype(bf16)
        )
        put_sums(grads_outs[1:], sums_out)


def feed(attended, tokens, cotangent, gathered, held, gains, biases, parts):
    total = tokens.shape[0]
    tile = 512

    def tiled(width):
        return pl.BlockSpec((tile, width), lambda t: (t, 0))

    grads = part_shapes(held.shape[1], PACK, parts)
    return pl.pallas_call(
        functools.partial(feed_kernel, len(attended), len(gathered)),
        grid=(total // tile,),
        in_specs=[tiled(x.shape[1]) for x in attended]
        + [whole(x.shape) for x in gathered]
        + [
            tiled(D), tiled(D), whole(held.shape), whole(gains.shape), whole(biases.shape),
        ],
        out_specs=[tiled(D), tiled(D), tiled(WIDTH), whole((8, PACK))]
        + [whole(x.shape) for x in grads],
        out_shape=[
            jax.ShapeDtypeStruct((total, D), bf16),
            jax.ShapeDtypeStruct((total, D), f32),
            jax.ShapeDtypeStruct((total, WIDTH), bf16),
            jax.ShapeDtypeStruct((8, PACK), f32),
        ]
        + grads,
        scratch_shapes=[
            pltpu.VMEM((WIDTH, D), bf16),
            pltpu.VMEM((D, FF), bf16),
            pltpu.VMEM((FF, D), bf16),
            pltpu.VMEM((4, FF, GROUP), f32),
            pltpu.VMEM((WIDTH, D), f32),
            pltpu.VMEM((D, FF), f32),
            pltpu.VMEM((FF, D), f32),
        ],
        compiler_params=params(),
        cost_estimate=takes(50),
    )(*attended, *gathered, tokens, cotangent, held, gains, biases)


def project_back_kernel(n_parts, *refs):
    grad_refs = [refs[n_parts * i : n_parts * (i + 1)] for i in range(3)]
    (
        normed_ref, tokens_ref, grad_middle_ref, weight_ref, held_ref, gains_ref,
        grad_out, sums_out, *grads_outs, d_weight,
    ) = refs[3 * n_parts :]
    step = pl.program_id(0)

    @pl.when(step == 0)
    def _():
        d_weight[...] = jnp.zeros_like(d_weight)
        sums_out[...] = jnp.zeros_like(sums_out)

    grad_normed = jnp.zeros(tokens_ref.shape, f32)
    for i, parts in enumerate(grad_refs):
        at = slice(WIDTH * i, WIDTH * (i + 1))
        grad = jnp.concatenate([ref[...] for ref in parts], axis=1)
        d_weight[:, at] += contract(normed_ref[...], grad, 0, 0)
        grad_normed = grad_normed + contract(grad, weight_ref[:, at], 1, 1)
        sums_out[0:1, at] += jnp.sum(grad.astype(f32), axis=0, keepdims=True)
    unit, root = normalized(tokens_ref[...].astype(f32))
    grad_out[...] = grad_middle_ref[...] + norm_back(grad_normed, unit, root, gains_ref[:, :D])
    sums_out[1:2, :D] += jnp.sum(grad_normed * unit, axis=0, keepdims=True)
    sums_out[1:2, 512 : 512 + D] += jnp.sum(grad_normed, axis=0, keepdims=True)

    @pl.when(step == pl.num_programs(0) - 1)
    def _():
        put_parts(grads_outs, order_of(held_ref), slice(None), d_weight[...].astype(bf16))
        put_sums(grads_outs[1:], sums_out)


def project_back(dq, dk, dv, normed, tokens, grad_middle, weight, held, gains, parts):
    total = tokens.shape[0]
    tile = 512

    def tiled(width):
        return pl.BlockSpec((tile, width), lambda t: (t, 0))

    grads = part_shapes(held.shape[1], 3 * WIDTH, parts)
    return pl.pallas_call(
        functools.partial(project_back_kernel, len(dq)),
        grid=(total // tile,),
        in_specs=[tiled(x.shape[1]) for x in dq + dk + dv]
        + [tiled(D)] * 3
        + [whole(weight.shape), whole(held.shape), whole(gains.shape)],
        out_specs=[tiled(D), whole((8, 3 * WIDTH))] + [whole(x.shape) for x in grads],
        out_shape=[
            jax.ShapeDtypeStruct((total, D), f32),
            jax.ShapeDtypeStruct((8, 3 * WIDTH), f32),
        ]
        + grads,
        scratch_shapes=[pltpu.VMEM((D, 3 * WIDTH), f32)],
        compiler_params=params(),
        cost_estimate=takes(12),
    )(*dq, *dk, *dv, normed, tokens, grad_middle, weight, held, gains)


def merge_kernel(n_got, n_parts, *refs):
    kept_ref, got_refs = refs[0], refs[1 : 1 + n_got]
    own_ref = refs[1 + n_got]
    kept_out, sums_out, *sent_outs = refs[2 + n_got :]
    rows = kept_ref.shape[0]
    n = rows // n_parts
    for i in range(n_parts):
        at = slice(n * i, n * (i + 1))
        block = kept_ref[at, :].astype(f32)
        for ref in got_refs:
            block = block + ref[at, :].astype(f32)
        if i == 0:
            kept_out[...] = block
        else:
            sent_outs[i - 1][:n, :] = block.astype(bf16)
    terms = [own_ref[0:2, :]]
    for ref in got_refs:
        tail = ref[rows:, :].astype(f32)
        terms.append((tail[0:2] + tail[2:4]) + tail[4:6])
    while len(terms) > 1:
        terms = [a + b for a, b in zip(terms[0::2], terms[1::2])]
    sums_out[...] = jnp.zeros_like(sums_out)
    sums_out[0:2, :] = terms[0]
    put_sums(sent_outs, sums_out)


def merge(kept, got, sums, parts):
    rows, width = kept.shape
    n = rows // parts
    sent = [jax.ShapeDtypeStruct((n + SUM_ROWS, width), bf16)] * (parts - 1)
    shapes = [jax.ShapeDtypeStruct((n, width), f32), jax.ShapeDtypeStruct(sums.shape, f32)] + sent
    return pl.pallas_call(
        functools.partial(merge_kernel, len(got), parts),
        in_specs=[pl.BlockSpec(memory_space=pltpu.VMEM)] * (2 + len(got)),
        out_specs=[pl.BlockSpec(memory_space=pltpu.VMEM)] * len(shapes),
        out_shape=shapes,
        compiler_params=pltpu.CompilerParams(vmem_limit_bytes=20 * 2**20),
        cost_estimate=takes(2),
    )(kept, *got, sums)


class Exchange:
    def __init__(self, count):
        self.count = count
        bits = [1 << b for b in reversed(range(count.bit_length() - 1))]
        self.stages = []
        for i in range(0, len(bits) - 1, 2):
            low, high = bits[i + 1], bits[i]
            self.stages.append([low, high, low | high])
        if len(bits) % 2:
            self.stages.append([bits[-1]])
        self.masks = [0]
        for stage in self.stages:
            self.masks = [bit ^ mask for bit in [0] + stage for mask in self.masks]
        self.parts = len(self.stages[-1]) + 1 if self.stages else 1

    def swap(self, x, bit):
        return lax.ppermute(x, AXES, [(i, i ^ bit) for i in range(self.count)])

    def swaps(self, x, stage):
        return [self.swap(x, bit) for bit in stage]

    def gather(self, x, works=()):
        results = []
        for i, stage in enumerate(self.stages):
            got = self.swaps(x, stage)
            if i < len(works):
                results.append(works[i](x))
                got = [after(part, results[-1]) for part in got]
            last = i == len(self.stages) - 1
            x = [x] + got if last else jnp.concatenate([x] + got, axis=0)
        results += [work(x[0]) for work in works[len(self.stages) :]]
        return x, results

    def scatter_sum(self, kept, sent, sums, works):
        stages, results = self.stages[::-1], []
        for i, stage in enumerate(stages):
            got = [self.swap(x, bit) for x, bit in zip(sent, stage)]
            if i < len(works):
                results.append(works[i](kept))
                got = [after(part, results[-1]) for part in got]
            parts = len(stages[i + 1]) + 1 if i + 1 < len(stages) else 1
            kept, sums, *sent = merge(kept, got, sums, parts)
        results += [work(kept) for work in works[len(stages) :]]
        return kept, sums, results

    def total(self, x):
        for stage in self.stages:
            terms = [x] + self.swaps(x, stage)
            while len(terms) > 1:
                terms = [a + b for a, b in zip(terms[0::2], terms[1::2])]
            x = terms[0]
        return x


def after(x, earlier):
    return lax.optimization_barrier((x, earlier))[0]


def adamw_update(weight, first, second, gradient, learn_rate):
    first_new = 0.5 * first + 0.5 * gradient
    second_new = 0.5 * second + 0.5 * gradient * gradient
    correction = 1.0 - 0.5 ** float(STEP)
    stepped = first_new / correction / (jnp.sqrt(second_new / correction) + 1e-08)
    return (weight - learn_rate * (stepped + 0.01 * weight), first_new, second_new)


def grouped(rows):
    n, width = rows.shape
    split = rows.reshape(n, width // USED, USED)
    return jnp.pad(split, ((0, 0), (0, 0), (0, GROUP - USED))).reshape(n, width // USED * GROUP)


def ungrouped(rows):
    n, width = rows.shape
    return rows.reshape(n, width // GROUP, GROUP)[:, :, :USED].reshape(n, width // GROUP * USED)


def packed_feed(up, down, out):
    n = up.shape[0]
    down = jnp.pad(down.reshape(n, 4, D), ((0, 0), (0, 0), (0, 512 - D))).reshape(n, 4 * 512)
    return jnp.concatenate([up, down, jnp.pad(out, ((0, 0), (0, 512 - D)))], axis=1)


def unpacked_feed(rows):
    n = rows.shape[0]
    down = rows[:, DOWN_AT : DOWN_AT + 4 * 512].reshape(n, 4, 512)[:, :, :D].reshape(n, FF)
    return rows[:, :FF], down, rows[:, OUT_AT : OUT_AT + D]


def pad_rows(rows, to):
    return jnp.pad(rows, ((0, to - rows.shape[0]), (0, 0)))


def shards(
    devices, tokens, segment_ids, pad_mask, cotangent,
    qkv_weight, qkv_first, qkv_second, out_weight, out_first, out_second,
    up_weight, up_first, up_second, down_weight, down_first, down_second,
    gains, gain_first, gain_second, biases, bias_first, bias_second,
):
    row_count, length, _ = tokens.shape
    ring = Exchange(devices)
    own_rows = out_weight.shape[0] // D
    by_rows = out_weight.shape[0] % D == 0
    slot = -(-own_rows // 16) * 16 if by_rows else D
    parts = ring.parts if by_rows else 1

    flat_gains, flat_biases = gains.reshape(1, -1), biases.reshape(1, -1)
    if by_rows:
        slots = slot * devices
        place = np.arange(slots)
        masks = jnp.asarray(np.asarray(ring.masks)[place // slot], jnp.int32)
        inner = place % slot
        me = lax.axis_index(AXES)
        held = jnp.where(inner < own_rows, (me ^ masks) * own_rows + inner, -1)[None, :]
    else:
        held = jnp.arange(D, dtype=jnp.int32)[None, :]

    def turned(sent):
        return turn_rows(
            segment_ids, pad_mask, after(jnp.swapaxes(tokens, 1, 2), sent),
            jnp.swapaxes(cotangent, 1, 2), flat_gains, flat_biases,
        )

    def prepared(sent):
        feed_weights, out_weights, own_held = after(((up_weight, down_weight), out_weight, held), sent)
        if by_rows:
            feed_rows = packed_feed(
                feed_weights[0].astype(bf16).reshape(own_rows, FF),
                feed_weights[1].astype(bf16).reshape(own_rows, FF),
                out_weights.astype(bf16).reshape(own_rows, D),
            )
            feed_rows = pad_rows(feed_rows, slot)
        else:
            feed_rows = packed_feed(
                fetch(feed_weights[0], FF), fetch(feed_weights[1], FF), fetch(out_weights, D)
            )
        return own_held, feed_rows

    def fetch(weight, width):
        flat = lax.all_gather(weight.astype(bf16), AXES, axis=0, tiled=True)
        return flat.reshape(D, width)

    if by_rows:
        qkv_rows = grouped(qkv_weight.astype(bf16).reshape(own_rows, 3 * D))
        qkv_all, (small, first_turned) = ring.gather(pad_rows(qkv_rows, slot), (prepared, turned))
    else:
        qkv_all = [grouped(fetch(qkv_weight, 3 * D))]
        first_turned, small = turned(qkv_all[0]), prepared(qkv_all[0])
    tokens_low, cotangent_low, normed, cosine, sine, query_lanes, key_lanes, pad, start = first_turned
    held, feed_rows = small

    def projected(sent):
        return project(
            after(normed, sent), qkv_all, held, flat_biases, cosine, sine, query_lanes, key_lanes
        )

    made = []

    def attending(first, count):
        def work(sent):
            q, k, v, _ = made[0]
            made.append(attend(after(q, sent), k, v, pad, first, count))
            return made[-1]

        return work

    def projecting(sent):
        made.append(projected(sent))
        return made[-1]

    works = (projecting, attending(0, 3), attending(3, 1))
    if by_rows:
        feed_all, _ = ring.gather(feed_rows, works)
    else:
        feed_all = [feed_rows]
        for work in works:
            work(feed_rows)
    (q, k, v, qkv_wide), *saved = made
    outputs_low, grad_middle, grad_attended, feed_sums, *feed_grads = feed(
        [attended for attended, *_ in saved], tokens_low, cotangent_low, feed_all, held,
        flat_gains, flat_biases, parts,
    )

    def outputs_back(sent):
        return jnp.swapaxes(unturn_rows(start, after(outputs_low, sent), length), 1, 2)

    def both(*works):
        return lambda sent: tuple(work(sent) for work in works)

    def attending_back(first, count, which, held):
        def work(sent):
            return attend_back(
                q, k, v, after(grad_attended, sent), *saved[which], cosine, sine, first, count,
                held,
            )

        return work

    works = (
        attending_back(0, 1, 0, 0),
        both(attending_back(1, 2, 0, 0), outputs_back),
        attending_back(3, 1, 1, 3),
    )
    if by_rows:
        feed_part, feed_sums, backs = ring.scatter_sum(feed_grads[0], feed_grads[1:], feed_sums, works)
    else:
        feed_part, backs = feed_grads[0], [work(feed_sums) for work in works]
    backs[1], outputs = backs[1]
    dq, dk, dv = (list(x) for x in zip(*backs))
    grad_tokens, qkv_sums, *qkv_grads = project_back(
        dq, dk, dv, after(normed, feed_part), tokens_low, grad_middle, qkv_wide, held, flat_gains, parts
    )

    def grads_back(sent):
        return jnp.swapaxes(unturn_rows(start, after(grad_tokens, sent), length), 1, 2)

    def feed_updated(sent):
        part = after(feed_part, sent)
        if by_rows:
            grads = [x.reshape(-1) for x in unpacked_feed(part[:own_rows])]
        else:
            grads = [reduce(x) for x in unpacked_feed(part)]
        up_grad, down_grad, out_grad = grads
        return (
            (up_grad, *adamw_update(up_weight, up_first, up_second, up_grad, 0.05)),
            (down_grad, *adamw_update(down_weight, down_first, down_second, down_grad, 0.03)),
            (out_grad, *adamw_update(out_weight, out_first, out_second, out_grad, 0.3)),
        )

    def reduce(part):
        return lax.psum_scatter(part.astype(f32).reshape(-1), AXES, scatter_dimension=0, tiled=True)

    works = (feed_updated, grads_back)
    if by_rows:
        qkv_part, qkv_sums, results = ring.scatter_sum(qkv_grads[0], qkv_grads[1:], qkv_sums, works)
        qkv_grad = ungrouped(qkv_part[:own_rows]).reshape(-1)
    else:
        results = [work(qkv_sums) for work in works]
        qkv_grad = reduce(ungrouped(qkv_grads[0]))
        feed_sums, qkv_sums = ring.total(feed_sums), ring.total(qkv_sums)
    (up_results, down_results, out_results), input_grad = results
    down_sum, out_sum, gain_sum, offset_sum = (
        feed_sums[0, at : at + D] for at in range(FF, FF + 4 * 512, 512)
    )
    gain_grad = jnp.concatenate([qkv_sums[1, :D], gain_sum])
    bias_grad = jnp.concatenate(
        [
            qkv_sums[1, 512 : 512 + D], ungrouped(qkv_sums[0:1])[0], out_sum, offset_sum,
            feed_sums[0, :FF], down_sum,
        ]
    )
    return (
        outputs,
        input_grad,
        qkv_grad,
        *adamw_update(qkv_weight, qkv_first, qkv_second, qkv_grad, 0.05),
        *out_results,
        *up_results,
        *down_results,
        gain_grad,
        *adamw_update(gains, gain_first, gain_second, gain_grad, 0.2),
        bias_grad,
        *adamw_update(biases, bias_first, bias_second, bias_grad, 0.1),
        bias_grad[6 * D + FF :],
    )


def solution(mesh):
    split, copied = P(AXES), P()
    rows, row = P(AXES, None, None), P(AXES, None)
    in_specs = (rows, row, row, rows) + (split,) * 12 + (copied,) * 6
    out_specs = (rows, rows) + (split,) * 16 + (copied,) * 9
    devices = math.prod(mesh.shape[axis] for axis in AXES)
    return jax.shard_map(
        functools.partial(shards, devices),
        mesh=mesh,
        in_specs=in_specs,
        out_specs=out_specs,
        check_vma=False,
    )
```

```python
import functools
import math

import jax
import jax.numpy as jnp
import numpy as np
from jax import lax
from jax.experimental import pallas as pl
from jax.experimental.pallas import tpu as pltpu
from jax.sharding import PartitionSpec as P

D = 480
HEAD_DIM = 24
FF = 1920
STEP = 3
AXES = ("wide", "narrow")

GROUP = 128
PER_GROUP = 5
GROUPS = 4
USED = PER_GROUP * HEAD_DIM
WIDTH = GROUPS * GROUP
HALF = HEAD_DIM // 2
BLOCK = 512
FAR = -1e30
LOG2E = math.log2(math.e)
SCALE = HEAD_DIM**-0.5
VMEM_LIMIT = 56 * 2**20
SAFE = 60.0
ATTEND = 1024
ATTEND_BACK = 512
SUM_ROWS = 16

f32 = jnp.float32
bf16 = jnp.bfloat16


def contract(left, right, left_dim, right_dim):
    return lax.dot_general(
        left, right, (((left_dim,), (right_dim,)), ((), ())), preferred_element_type=f32
    )


def lanes():
    return lax.broadcasted_iota(jnp.int32, (1, GROUP), 1)


def head_lanes(m):
    lane = lanes()
    return (lane >= HEAD_DIM * m) & (lane < HEAD_DIM * (m + 1))


def of_head(x, m):
    return jnp.where(head_lanes(m) | (lanes() >= USED), x, jnp.zeros_like(x))


def same_head():
    rows = lax.broadcasted_iota(jnp.int32, (GROUP, GROUP), 0) // HEAD_DIM
    columns = lax.broadcasted_iota(jnp.int32, (GROUP, GROUP), 1) // HEAD_DIM
    return jnp.where((rows == columns) & (rows < PER_GROUP), 1.0, 0.0).astype(bf16)


def head_sums(product, same):
    high = product.astype(bf16)
    low = (product - high.astype(f32)).astype(bf16)
    return contract(high, same, 1, 0) + contract(low, same, 1, 0)


def normalized(field):
    average = jnp.mean(field, axis=-1, keepdims=True)
    centered = field - average
    spread = jnp.mean(centered * centered, axis=-1, keepdims=True)
    root = lax.rsqrt(spread + 1e-05)
    return centered * root, root


def norm_back(grad, unit, root, gain_row):
    scaled = grad * gain_row
    return root * (
        scaled
        - jnp.mean(scaled, axis=-1, keepdims=True)
        - unit * jnp.mean(scaled * unit, axis=-1, keepdims=True)
    )


def takes(microseconds):
    return pl.CostEstimate(
        flops=int(microseconds * 1.1e9), bytes_accessed=1024, transcendentals=0
    )


def params(n_axes=1):
    return pltpu.CompilerParams(
        vmem_limit_bytes=VMEM_LIMIT, dimension_semantics=("arbitrary",) * n_axes
    )


def whole(shape):
    return pl.BlockSpec(shape, lambda *_: (0,) * len(shape))


def turn_kernel(
    segments_ref, mask_ref, tokens_ref, cotangent_ref, gains_ref, biases_ref,
    tokens_out, cotangent_out, normed_out, cosine_out, sine_out, query_out, key_out, pad_out, start_out,
):
    length = tokens_ref.shape[2]
    r = pl.program_id(0)
    segments = segments_ref[pl.ds(r, 1), :]
    counts = [jnp.sum(jnp.where(segments == c, 1.0, 0.0)) for c in range(3)]
    begins = [counts[0], counts[0] + counts[1], counts[0] + counts[1] + counts[2]]
    start = begins[2]
    for c, begin in ((2, begins[1]), (1, begins[0]), (0, 0.0)):
        start = jnp.where(counts[c] == float(BLOCK), begin, start)
    start_out[r] = start

    def places(shape, dim, first):
        place = lax.broadcasted_iota(jnp.int32, shape, dim).astype(f32) + (start + float(first))
        return jnp.where(place >= float(length), place - float(length), place)

    place = places((1, length), 1, 0)
    begin = jnp.where(place >= begins[0], begins[0], 0.0)
    for c in (1, 2):
        begin = jnp.where(place >= begins[c], begins[c], begin)
    exponent = lax.broadcasted_iota(jnp.int32, (16, 1), 0).astype(f32)
    phases = (place - begin) * jnp.exp(exponent * (-math.log(10000.0) / HALF))
    lane = lax.broadcasted_iota(jnp.int32, (16, GROUP), 1)
    entry = lax.broadcasted_iota(jnp.int32, (16, GROUP), 0)
    grid = jnp.where((lane < USED) & (lane % HALF == entry), 1.0, 0.0).astype(bf16)
    for part, out in ((jnp.cos(phases), cosine_out), (jnp.sin(phases), sine_out)):
        high, middle, low = split_three(part)
        out[...] = contract(high, grid, 0, 0) + contract(middle, grid, 0, 0) + contract(low, grid, 0, 0)

    mask = jnp.broadcast_to(mask_ref[pl.ds(r, 1), :].astype(f32), (GROUP, length)).astype(bf16)
    gain, offset = gains_ref[:, :D], biases_ref[:, :D]
    step = 256
    spare = lax.broadcasted_iota(jnp.int32, (step, GROUP), 1).astype(f32) - float(USED)
    for first in range(0, length, step):
        here = slice(first, first + step)
        source = lax.broadcasted_iota(jnp.int32, (step, length), 1).astype(f32)
        pick = jnp.where(places((step, length), 0, first) == source, 1.0, 0.0).astype(bf16)
        turned = contract(pick, tokens_ref[0], 1, 1)
        tokens_out[here, :] = turned.astype(bf16)
        unit, _ = normalized(turned)
        normed_out[here, :] = (unit * gain + offset).astype(bf16)
        cotangent_out[here, :] = contract(pick, cotangent_ref[0], 1, 1).astype(bf16)
        present = contract(pick, mask, 1, 1)
        place = places((step, GROUP), 0, first)
        segment = sum(jnp.where(place >= begin, 1.0, 0.0) for begin in begins)
        mine = segment == spare
        query_out[here, :] = jnp.where(mine, 1.0, 0.0).astype(bf16)
        key_out[here, :] = jnp.where(mine & (present > 0.5), 0.0, FAR).astype(bf16)
        pad_out[here, :] = (1.0 - present).astype(bf16)


def turn_rows(segments, mask, tokens, cotangent, gains, biases):
    rows, width, length = tokens.shape
    row = pl.BlockSpec((length, width), lambda r: (r, 0))
    flat = pl.BlockSpec((1, width, length), lambda r: (r, 0, 0))
    lane = pl.BlockSpec((length, GROUP), lambda r: (r, 0))
    tall = jax.ShapeDtypeStruct((rows * length, width), bf16)

    def lane_shape(kind):
        return jax.ShapeDtypeStruct((rows * length, GROUP), kind)

    return pl.pallas_call(
        turn_kernel,
        grid=(rows,),
        in_specs=[
            whole(segments.shape), whole(mask.shape), flat, flat, whole(gains.shape), whole(biases.shape),
        ],
        out_specs=[row] * 3 + [lane] * 5 + [pl.BlockSpec(memory_space=pltpu.SMEM)],
        out_shape=[tall, tall, tall, lane_shape(f32), lane_shape(f32)]
        + [lane_shape(bf16)] * 3
        + [jax.ShapeDtypeStruct((rows,), f32)],
        compiler_params=params(),
        cost_estimate=takes(12),
    )(segments, mask, tokens, cotangent, gains, biases)


def unturn_kernel(start_ref, rows_ref, out_ref):
    length = rows_ref.shape[0]
    start = start_ref[pl.program_id(0)]
    rows = rows_ref[...]
    high = rows.astype(bf16)
    step = 256
    for first in range(0, length, step):
        here = slice(first, first + step)
        target = lax.broadcasted_iota(jnp.int32, (length, step), 1).astype(f32) + (float(first) - start)
        target = jnp.where(target < 0.0, target + float(length), target)
        source = lax.broadcasted_iota(jnp.int32, (length, step), 0).astype(f32)
        pick = jnp.where(target == source, 1.0, 0.0).astype(bf16)
        got = contract(high, pick, 0, 0)
        if rows.dtype == f32:
            got = got + contract((rows - high.astype(f32)).astype(bf16), pick, 0, 0)
        out_ref[0, :, here] = got.astype(out_ref.dtype)


def unturn_rows(start, rows, length):
    total, width = rows.shape
    return pl.pallas_call(
        unturn_kernel,
        grid=(total // length,),
        in_specs=[
            pl.BlockSpec(memory_space=pltpu.SMEM),
            pl.BlockSpec((length, width), lambda r: (r, 0)),
        ],
        out_specs=pl.BlockSpec((1, width, length), lambda r: (r, 0, 0)),
        out_shape=jax.ShapeDtypeStruct((total // length, width, length), rows.dtype),
        compiler_params=params(),
        cost_estimate=takes(3 if rows.dtype == bf16 else 6),
    )(start, rows)


def swap_halves(field, forward):
    low_half = lanes() % HEAD_DIM < HALF
    up = pltpu.roll(field, GROUP - HALF, 1)
    down = pltpu.roll(field, HALF, 1)
    if forward:
        return jnp.where(low_half, -up, down)
    return jnp.where(low_half, up, -down)


def order_of(held_ref):
    shape = (D, held_ref.shape[1])
    row = lax.broadcasted_iota(jnp.int32, shape, 0)
    return jnp.where(row == held_ref[...], 1.0, 0.0).astype(bf16)


def group_order_of(held_ref):
    shape = (WIDTH, held_ref.shape[1])
    row = lax.broadcasted_iota(jnp.int32, shape, 0)
    row = jnp.where(row % GROUP < USED, row // GROUP * USED + row % GROUP, -2)
    return jnp.where(row == held_ref[...], 1.0, 0.0).astype(bf16)


def in_order(order, gathered_refs, columns):
    got, at = 0.0, 0
    for ref in gathered_refs:
        n = ref.shape[0]
        got = got + jnp.dot(order[:, at : at + n], ref[:, columns], preferred_element_type=f32)
        at += n
    return got


def put_parts(outs, order, columns, grad):
    n = outs[0].shape[0]
    for i, out in enumerate(outs):
        out[:n, columns] = contract(order[:, n * i : n * (i + 1)], grad, 0, 0).astype(bf16)


def split_three(x):
    high = x.astype(bf16)
    rest = x - high.astype(f32)
    middle = rest.astype(bf16)
    return high, middle, (rest - middle.astype(f32)).astype(bf16)


def put_sums(outs, sums_ref):
    for out in outs:
        n = out.shape[0] - SUM_ROWS
        block = jnp.concatenate(
            [part.astype(f32) for part in split_three(sums_ref[0:2, :])]
            + [jnp.zeros((SUM_ROWS - 6, out.shape[1]), f32)],
            axis=0,
        )
        out[n:, :] = block.astype(bf16)


def part_shapes(slots, width, parts):
    n = slots // parts
    return [jax.ShapeDtypeStruct((n, width), bf16)] + [
        jax.ShapeDtypeStruct((n + SUM_ROWS, width), bf16)
    ] * (parts - 1)


def project_kernel(n_gathered, *refs):
    gathered_refs = refs[:n_gathered]
    (
        normed_ref, held_ref, biases_ref, cosine_ref, sine_ref, query_lanes, key_lanes,
        q_out, k_out, v_out, weight_out, bias_ref,
    ) = refs[n_gathered:]

    @pl.when(pl.program_id(0) == 0)
    def _():
        weight_out[...] = in_order(order_of(held_ref), gathered_refs, slice(None)).astype(bf16)
        bias_ref[...] = jnp.zeros_like(bias_ref)
        for i in range(3 * GROUPS):
            at = D + USED * i
            bias_ref[:, GROUP * i : GROUP * i + USED] = biases_ref[:, at : at + USED]

    cosine, sine = cosine_ref[...], sine_ref[...]
    own = lanes() < USED
    for g in range(GROUPS):
        to = slice(GROUP * g, GROUP * (g + 1))
        for part, out, factor, spare in (
            (0, q_out, SCALE, query_lanes),
            (1, k_out, 1.0, key_lanes),
        ):
            at = slice(WIDTH * part + GROUP * g, WIDTH * part + GROUP * (g + 1))
            mixed = jnp.dot(
                normed_ref[...], weight_out[:, at], preferred_element_type=f32
            ) + bias_ref[:, at]
            turned = mixed * cosine + swap_halves(mixed, True) * sine
            out[:, to] = jnp.where(own, (turned * factor).astype(bf16), spare[...])
    values = slice(2 * WIDTH, 3 * WIDTH)
    v_out[...] = (
        jnp.dot(normed_ref[...], weight_out[:, values], preferred_element_type=f32)
        + bias_ref[:, values]
    ).astype(bf16)


def project(normed, gathered, held, biases, cosine, sine, query_lanes, key_lanes):
    total = normed.shape[0]
    tile = 512

    def tiled(width):
        return pl.BlockSpec((tile, width), lambda t: (t, 0))

    return pl.pallas_call(
        functools.partial(project_kernel, len(gathered)),
        grid=(total // tile,),
        in_specs=[whole(x.shape) for x in gathered]
        + [
            tiled(D), whole(held.shape), whole(biases.shape),
            tiled(GROUP), tiled(GROUP), tiled(GROUP), tiled(GROUP),
        ],
        out_specs=[tiled(WIDTH)] * 3 + [whole((D, 3 * WIDTH))],
        out_shape=[jax.ShapeDtypeStruct((total, WIDTH), bf16)] * 3
        + [jax.ShapeDtypeStruct((D, 3 * WIDTH), bf16)],
        scratch_shapes=[pltpu.VMEM((1, 3 * WIDTH), f32)],
        compiler_params=params(),
        cost_estimate=takes(10),
    )(*gathered, normed, held, biases, cosine, sine, query_lanes, key_lanes)


def heads_flat(field, spare):
    flat = field.astype(f32).T
    tail = jnp.full((8, field.shape[0]), spare, f32)
    return [
        jnp.concatenate([flat[HEAD_DIM * m : HEAD_DIM * (m + 1)], tail], axis=0).astype(bf16)
        for m in range(PER_GROUP)
    ]


def attend_kernel(q_ref, k_ref, v_ref, pad_ref, attended_out, probs_out, scale_out, own_out):
    length = q_ref.shape[0]
    same = same_head()
    own = lanes() < USED
    squares = []
    for ref in (q_ref, k_ref):
        kept = jnp.where(own, ref[...], jnp.zeros((), bf16))
        squares.append(jnp.max(contract(kept * kept, same, 1, 0), axis=0, keepdims=True))
    safe = jnp.max(squares[0] * squares[1]) <= SAFE * SAFE

    def diagonal(here):
        q, k = q_ref[here, :].astype(f32), k_ref[here, :].astype(f32)
        return head_sums(jnp.where(own, q * k, 0.0), same) * LOG2E

    def block_of(first):
        here = slice(first, first + BLOCK)
        values = jnp.concatenate([v_ref[here, :], jnp.ones((BLOCK, GROUP), bf16)], axis=1)
        return here, k_ref[here, :], values

    def rows_of(first, m):
        return pl.ds((first // BLOCK * PER_GROUP + m) * BLOCK, BLOCK)

    @pl.when(safe)
    def _():
        for first in range(0, length, BLOCK):
            here, k, values = block_of(first)
            total = jnp.zeros((BLOCK, GROUP), f32)
            weight = jnp.zeros((BLOCK, GROUP), f32)
            for m in range(PER_GROUP):
                scores = contract(of_head(q_ref[here, :], m), k, 1, 1)
                probs = jnp.exp2(scores * LOG2E).astype(bf16)
                probs_out[rows_of(first, m), :] = probs
                got = jnp.dot(probs, values, preferred_element_type=f32)
                total = jnp.where(head_lanes(m), got[:, :GROUP], total)
                weight = jnp.where(head_lanes(m), got[:, GROUP:], weight)
            extra = pad_ref[here, :].astype(f32) * jnp.exp2(diagonal(here))
            scale = 1.0 / jnp.where(own, weight + extra, 1.0)
            extra = extra * scale
            attended_out[here, :] = (total * scale + extra * v_ref[here, :].astype(f32)).astype(bf16)
            scale_out[here, :] = scale
            own_out[here, :] = extra.astype(bf16)

    @pl.when(jnp.logical_not(safe))
    def _():
        for first in range(0, length, BLOCK):
            here, k, values = block_of(first)
            padded = pad_ref[here, :].astype(f32)
            on_diagonal = jnp.where(padded > 0.5, diagonal(here), FAR)

            def one_head(m, carry):
                total, extra = carry
                scores = contract(of_head(q_ref[here, :], m), k, 1, 1) * LOG2E
                mine = jnp.where(head_lanes(m), on_diagonal, FAR)
                single = jnp.max(mine, axis=1, keepdims=True)
                highest = jnp.maximum(jnp.max(scores, axis=1, keepdims=True), single)
                weight = jnp.sum(jnp.exp2(scores - highest), axis=1, keepdims=True)
                shift = highest + jnp.log2(weight + jnp.exp2(single - highest))
                probs = jnp.exp2(scores - shift).astype(bf16)
                probs_out[rows_of(first, m), :] = probs
                got = jnp.dot(probs, values, preferred_element_type=f32)
                return (
                    jnp.where(head_lanes(m), got[:, :GROUP], total),
                    jnp.where(head_lanes(m), jnp.exp2(single - shift), extra),
                )

            zero = jnp.zeros((BLOCK, GROUP), f32)
            total, extra = lax.fori_loop(0, PER_GROUP, one_head, (zero, zero))
            attended_out[here, :] = (total + extra * v_ref[here, :].astype(f32)).astype(bf16)
            scale_out[here, :] = jnp.ones((BLOCK, GROUP), f32)
            own_out[here, :] = extra.astype(bf16)


def attend(q, k, v, pad, first, count):
    total = q.shape[0]
    block = pl.BlockSpec((ATTEND, GROUP), lambda r, g: (r, first + g))
    out = pl.BlockSpec((ATTEND, GROUP), lambda r, g: (r, g))
    pads = pl.BlockSpec((ATTEND, GROUP), lambda r, g: (r, 0))
    width = GROUP * count
    return pl.pallas_call(
        attend_kernel,
        grid=(total // ATTEND, count),
        in_specs=[block, block, block, pads],
        out_specs=[
            out, pl.BlockSpec((PER_GROUP * ATTEND, BLOCK), lambda r, g: (r * count + g, 0)), out, out,
        ],
        out_shape=[
            jax.ShapeDtypeStruct((total, width), bf16),
            jax.ShapeDtypeStruct((total * count * PER_GROUP, BLOCK), bf16),
            jax.ShapeDtypeStruct((total, width), f32),
            jax.ShapeDtypeStruct((total, width), bf16),
        ],
        compiler_params=params(2),
        cost_estimate=takes(8 * count),
    )(q, k, v, pad)


def attend_back_kernel(
    q_ref, k_ref, v_ref, grad_ref, attended_ref, probs_ref, scale_ref, own_ref, cosine_ref, sine_ref,
    q_out, k_out, v_out,
):
    same = same_head()
    own = lanes() < USED
    for first in range(0, q_ref.shape[0], BLOCK):
        here = slice(first, first + BLOCK)
        v = v_ref[here, :]
        qf, kf, vf = q_ref[here, :].astype(f32), k_ref[here, :].astype(f32), v.astype(f32)
        gf, scale = grad_ref[here, :].astype(f32), scale_ref[here, :]
        delta = head_sums(gf * attended_ref[here, :].astype(f32), same)
        scaled = (gf * scale).astype(bf16)
        scaled_delta = delta * scale
        q_flat = heads_flat(jnp.where(own, qf, 0.0), 0.0)
        grad_flat = heads_flat(scaled, 0.0)
        k_flat = heads_flat(jnp.where(own, kf, 0.0), 0.0)
        grad_queries, grad_keys, grad_values = [], [], []
        for m in range(PER_GROUP):
            column = slice(HEAD_DIM * m, HEAD_DIM * m + 1)
            row = (first // BLOCK * PER_GROUP + m) * BLOCK
            probs = probs_ref[row : row + BLOCK, :]
            grad_probs = contract(scaled, jnp.where(head_lanes(m), v, jnp.zeros_like(v)), 1, 1)
            signal = (probs.astype(f32) * (grad_probs - scaled_delta[:, column])).astype(bf16)
            grad_values.append(contract(grad_flat[m], probs, 1, 0)[:HEAD_DIM])
            grad_keys.append(contract(q_flat[m], signal, 1, 0)[:HEAD_DIM])
            grad_queries.append(contract(k_flat[m], signal, 1, 1)[:HEAD_DIM])
        spare = jnp.zeros((GROUP - USED, BLOCK), f32)
        grad_q = jnp.concatenate(grad_queries + [spare], axis=0).T
        grad_k = jnp.concatenate(grad_keys + [spare], axis=0).T
        grad_v = jnp.concatenate(grad_values + [spare], axis=0).T
        own_prob = own_ref[here, :].astype(f32)
        own_signal = own_prob * (head_sums(gf * vf, same) - delta)
        grad_q = jnp.where(own, grad_q + own_signal * kf, 0.0)
        grad_k = jnp.where(own, grad_k + own_signal * qf, 0.0)
        grad_v = grad_v + own_prob * gf
        cosine, sine = cosine_ref[here, :], sine_ref[here, :]
        q_out[here, :] = (
            SCALE * (grad_q * cosine + swap_halves(grad_q, False) * sine)
        ).astype(bf16)
        k_out[here, :] = (grad_k * cosine + swap_halves(grad_k, False) * sine).astype(bf16)
        v_out[here, :] = grad_v.astype(bf16)


def attend_back(q, k, v, grad, attended, probs, scale, own, cosine, sine, first, count, held):
    total = q.shape[0]
    kept, per = attended.shape[1] // GROUP, ATTEND // ATTEND_BACK

    def at(offset):
        return pl.BlockSpec((ATTEND_BACK, GROUP), lambda r, g: (r, offset + g))

    saved, row = at(first - held), pl.BlockSpec((ATTEND_BACK, GROUP), lambda r, g: (r, 0))
    probs_block = pl.BlockSpec(
        (PER_GROUP * ATTEND_BACK, BLOCK),
        lambda r, g: ((r // per * kept + first - held + g) * per + r % per, 0),
    )
    return pl.pallas_call(
        attend_back_kernel,
        grid=(total // ATTEND_BACK, count),
        in_specs=[at(first)] * 4 + [saved, probs_block, saved, saved, row, row],
        out_specs=[at(0)] * 3,
        out_shape=[jax.ShapeDtypeStruct((total, GROUP * count), bf16)] * 3,
        compiler_params=params(2),
        cost_estimate=takes(14 * count),
    )(q, k, v, grad, attended, probs, scale, own, cosine, sine)


def gelu_both(v):
    e = jnp.exp2(v * v * (-0.5 * LOG2E))
    t = 1.0 / (1.0 + (0.3275911 / math.sqrt(2.0)) * jnp.abs(v))
    poly = t * (0.5 * 1.061405429) + (0.5 * -1.453152027)
    poly = poly * t + (0.5 * 1.421413741)
    poly = poly * t + (0.5 * -0.284496736)
    poly = poly * t + (0.5 * 0.254829592)
    tail = poly * t * e
    phi = jnp.where(v >= 0.0, 1.0 - tail, tail)
    return v * phi, phi + v * e * (1.0 / math.sqrt(2.0 * math.pi))


UP_AT, DOWN_AT, OUT_AT = 0, FF, FF + 4 * 512
PACK = FF + 4 * 512 + 512
CHUNK = 640


def feed_kernel(
    n_attended, n_gathered, *refs
):
    attended_refs, refs = refs[:n_attended], refs[n_attended:]
    gathered_refs, refs = refs[:n_gathered], refs[n_gathered:]
    (
        tokens_ref, cotangent_ref, held_ref, gains_ref, biases_ref,
        outputs_out, grad_middle_out, grad_attended_out, sums_out, *refs,
    ) = refs
    *grads_outs, w_out, w_up, w_down, w_tall, d_out, d_up, d_down = refs
    step = pl.program_id(0)

    @pl.when(step == 0)
    def _():
        order = order_of(held_ref)
        w_up[...] = in_order(order, gathered_refs, slice(UP_AT, UP_AT + FF)).astype(bf16)
        for m in range(4):
            at = DOWN_AT + 512 * m
            part = in_order(order, gathered_refs, slice(at, at + 512))
            for c in range(0, 512, GROUP):
                w_tall[c // GROUP, pl.ds(m, D, stride=4), :] = part[:, c : c + GROUP]
        for c in range(4):
            n = min(GROUP, D - GROUP * c)
            w_down[:, GROUP * c : GROUP * c + n] = w_tall[c, :, :n].astype(bf16)
        w_out[...] = in_order(group_order_of(held_ref), gathered_refs, slice(OUT_AT, OUT_AT + 512))[
            :, :D
        ].astype(bf16)
        d_out[...] = jnp.zeros_like(d_out)
        d_up[...] = jnp.zeros_like(d_up)
        d_down[...] = jnp.zeros_like(d_down)
        sums_out[...] = jnp.zeros_like(sums_out)

    attended = jnp.concatenate([ref[...] for ref in attended_refs], axis=1)
    cotangent = cotangent_ref[...]
    out_bias, offset = biases_ref[:, 4 * D : 5 * D], biases_ref[:, 5 * D : 6 * D]
    gain, down_bias = gains_ref[:, D:], biases_ref[:, 6 * D + FF :]
    middle = (
        tokens_ref[...].astype(f32)
        + jnp.dot(attended, w_out[...], preferred_element_type=f32)
        + out_bias
    )
    unit, root = normalized(middle)
    normed = (unit * gain + offset).astype(bf16)
    result = middle + down_bias
    grad_normed = jnp.zeros_like(middle)
    for first in range(0, FF, CHUNK):
        at = slice(first, first + CHUNK)
        hidden = (
            jnp.dot(normed, w_up[:, at], preferred_element_type=f32) + biases_ref[:, 6 * D + first : 6 * D + first + CHUNK]
        )
        active, slope = gelu_both(hidden)
        active = active.astype(bf16)
        result = result + jnp.dot(active, w_down[at, :], preferred_element_type=f32)
        grad_hidden = (contract(cotangent, w_down[at, :], 1, 1) * slope).astype(bf16)
        d_down[at, :] += contract(active, cotangent, 0, 0)
        d_up[:, at] += contract(normed, grad_hidden, 0, 0)
        grad_normed = grad_normed + contract(grad_hidden, w_up[:, at], 1, 1)
        sums_out[0:1, at] += jnp.sum(grad_hidden.astype(f32), axis=0, keepdims=True)
    outputs_out[...] = result.astype(bf16)
    grad_middle = cotangent.astype(f32) + norm_back(grad_normed, unit, root, gain)
    grad_middle_out[...] = grad_middle
    grad_branch = grad_middle.astype(bf16)
    d_out[...] += contract(attended, grad_branch, 0, 0)
    grad_attended_out[...] = contract(grad_branch, w_out[...], 1, 1).astype(bf16)
    for i, terms in enumerate(
        (cotangent.astype(f32), grad_branch.astype(f32), grad_normed * unit, grad_normed)
    ):
        at = FF + 512 * i
        sums_out[0:1, at : at + D] += jnp.sum(terms, axis=0, keepdims=True)

    @pl.when(step == pl.num_programs(0) - 1)
    def _():
        order = order_of(held_ref)
        put_parts(grads_outs, order, slice(UP_AT, UP_AT + FF), d_up[...].astype(bf16))
        for c in range(4):
            n = min(GROUP, D - GROUP * c)
            w_tall[c, :, :n] = d_down[:, GROUP * c : GROUP * c + n]
        for m in range(4):
            for c in range(4):
                at = DOWN_AT + 512 * m + GROUP * c
                part = w_tall[c, pl.ds(m, D, stride=4), :].astype(bf16)
                put_parts(grads_outs, order, slice(at, at + GROUP), part)
        put_parts(
            grads_outs, group_order_of(held_ref), slice(OUT_AT, OUT_AT + D), d_out[...].astype(bf16)
        )
        put_sums(grads_outs[1:], sums_out)


def feed(attended, tokens, cotangent, gathered, held, gains, biases, parts):
    total = tokens.shape[0]
    tile = 512

    def tiled(width):
        return pl.BlockSpec((tile, width), lambda t: (t, 0))

    grads = part_shapes(held.shape[1], PACK, parts)
    return pl.pallas_call(
        functools.partial(feed_kernel, len(attended), len(gathered)),
        grid=(total // tile,),
        in_specs=[tiled(x.shape[1]) for x in attended]
        + [whole(x.shape) for x in gathered]
        + [
            tiled(D), tiled(D), whole(held.shape), whole(gains.shape), whole(biases.shape),
        ],
        out_specs=[tiled(D), tiled(D), tiled(WIDTH), whole((8, PACK))]
        + [whole(x.shape) for x in grads],
        out_shape=[
            jax.ShapeDtypeStruct((total, D), bf16),
            jax.ShapeDtypeStruct((total, D), f32),
            jax.ShapeDtypeStruct((total, WIDTH), bf16),
            jax.ShapeDtypeStruct((8, PACK), f32),
        ]
        + grads,
        scratch_shapes=[
            pltpu.VMEM((WIDTH, D), bf16),
            pltpu.VMEM((D, FF), bf16),
            pltpu.VMEM((FF, D), bf16),
            pltpu.VMEM((4, FF, GROUP), f32),
            pltpu.VMEM((WIDTH, D), f32),
            pltpu.VMEM((D, FF), f32),
            pltpu.VMEM((FF, D), f32),
        ],
        compiler_params=params(),
        cost_estimate=takes(50),
    )(*attended, *gathered, tokens, cotangent, held, gains, biases)


def project_back_kernel(n_parts, *refs):
    grad_refs = [refs[n_parts * i : n_parts * (i + 1)] for i in range(3)]
    (
        normed_ref, tokens_ref, grad_middle_ref, weight_ref, held_ref, gains_ref,
        grad_out, sums_out, *grads_outs, d_weight,
    ) = refs[3 * n_parts :]
    step = pl.program_id(0)

    @pl.when(step == 0)
    def _():
        d_weight[...] = jnp.zeros_like(d_weight)
        sums_out[...] = jnp.zeros_like(sums_out)

    grad_normed = jnp.zeros(tokens_ref.shape, f32)
    for i, parts in enumerate(grad_refs):
        at = slice(WIDTH * i, WIDTH * (i + 1))
        grad = jnp.concatenate([ref[...] for ref in parts], axis=1)
        d_weight[:, at] += contract(normed_ref[...], grad, 0, 0)
        grad_normed = grad_normed + contract(grad, weight_ref[:, at], 1, 1)
        sums_out[0:1, at] += jnp.sum(grad.astype(f32), axis=0, keepdims=True)
    unit, root = normalized(tokens_ref[...].astype(f32))
    grad_out[...] = grad_middle_ref[...] + norm_back(grad_normed, unit, root, gains_ref[:, :D])
    sums_out[1:2, :D] += jnp.sum(grad_normed * unit, axis=0, keepdims=True)
    sums_out[1:2, 512 : 512 + D] += jnp.sum(grad_normed, axis=0, keepdims=True)

    @pl.when(step == pl.num_programs(0) - 1)
    def _():
        put_parts(grads_outs, order_of(held_ref), slice(None), d_weight[...].astype(bf16))
        put_sums(grads_outs[1:], sums_out)


def project_back(dq, dk, dv, normed, tokens, grad_middle, weight, held, gains, parts):
    total = tokens.shape[0]
    tile = 512

    def tiled(width):
        return pl.BlockSpec((tile, width), lambda t: (t, 0))

    grads = part_shapes(held.shape[1], 3 * WIDTH, parts)
    return pl.pallas_call(
        functools.partial(project_back_kernel, len(dq)),
        grid=(total // tile,),
        in_specs=[tiled(x.shape[1]) for x in dq + dk + dv]
        + [tiled(D)] * 3
        + [whole(weight.shape), whole(held.shape), whole(gains.shape)],
        out_specs=[tiled(D), whole((8, 3 * WIDTH))] + [whole(x.shape) for x in grads],
        out_shape=[
            jax.ShapeDtypeStruct((total, D), f32),
            jax.ShapeDtypeStruct((8, 3 * WIDTH), f32),
        ]
        + grads,
        scratch_shapes=[pltpu.VMEM((D, 3 * WIDTH), f32)],
        compiler_params=params(),
        cost_estimate=takes(12),
    )(*dq, *dk, *dv, normed, tokens, grad_middle, weight, held, gains)


def merge_kernel(n_got, n_parts, *refs):
    kept_ref, got_refs = refs[0], refs[1 : 1 + n_got]
    own_ref = refs[1 + n_got]
    kept_out, sums_out, *sent_outs = refs[2 + n_got :]
    rows = kept_ref.shape[0]
    n = rows // n_parts
    for i in range(n_parts):
        at = slice(n * i, n * (i + 1))
        block = kept_ref[at, :].astype(f32)
        for ref in got_refs:
            block = block + ref[at, :].astype(f32)
        if i == 0:
            kept_out[...] = block
        else:
            sent_outs[i - 1][:n, :] = block.astype(bf16)
    terms = [own_ref[0:2, :]]
    for ref in got_refs:
        tail = ref[rows:, :].astype(f32)
        terms.append((tail[0:2] + tail[2:4]) + tail[4:6])
    while len(terms) > 1:
        terms = [a + b for a, b in zip(terms[0::2], terms[1::2])]
    sums_out[...] = jnp.zeros_like(sums_out)
    sums_out[0:2, :] = terms[0]
    put_sums(sent_outs, sums_out)


def merge(kept, got, sums, parts):
    rows, width = kept.shape
    n = rows // parts
    sent = [jax.ShapeDtypeStruct((n + SUM_ROWS, width), bf16)] * (parts - 1)
    shapes = [jax.ShapeDtypeStruct((n, width), f32), jax.ShapeDtypeStruct(sums.shape, f32)] + sent
    return pl.pallas_call(
        functools.partial(merge_kernel, len(got), parts),
        in_specs=[pl.BlockSpec(memory_space=pltpu.VMEM)] * (2 + len(got)),
        out_specs=[pl.BlockSpec(memory_space=pltpu.VMEM)] * len(shapes),
        out_shape=shapes,
        compiler_params=pltpu.CompilerParams(vmem_limit_bytes=20 * 2**20),
        cost_estimate=takes(2),
    )(kept, *got, sums)


class Exchange:
    def __init__(self, count):
        self.count = count
        bits = [1 << b for b in reversed(range(count.bit_length() - 1))]
        self.stages = []
        for i in range(0, len(bits) - 1, 2):
            low, high = bits[i + 1], bits[i]
            self.stages.append([low, high, low | high])
        if len(bits) % 2:
            self.stages.append([bits[-1]])
        self.masks = [0]
        for stage in self.stages:
            self.masks = [bit ^ mask for bit in [0] + stage for mask in self.masks]
        self.parts = len(self.stages[-1]) + 1 if self.stages else 1

    def swap(self, x, bit):
        return lax.ppermute(x, AXES, [(i, i ^ bit) for i in range(self.count)])

    def swaps(self, x, stage):
        return [self.swap(x, bit) for bit in stage]

    def gather(self, x, works=()):
        results = []
        for i, stage in enumerate(self.stages):
            got = self.swaps(x, stage)
            if i < len(works):
                results.append(works[i](x))
                got = [after(part, results[-1]) for part in got]
            last = i == len(self.stages) - 1
            x = [x] + got if last else jnp.concatenate([x] + got, axis=0)
        results += [work(x[0]) for work in works[len(self.stages) :]]
        return x, results

    def scatter_sum(self, kept, sent, sums, works):
        stages, results = self.stages[::-1], []
        for i, stage in enumerate(stages):
            got = [self.swap(x, bit) for x, bit in zip(sent, stage)]
            if i < len(works):
                results.append(works[i](kept))
                got = [after(part, results[-1]) for part in got]
            parts = len(stages[i + 1]) + 1 if i + 1 < len(stages) else 1
            kept, sums, *sent = merge(kept, got, sums, parts)
        results += [work(kept) for work in works[len(stages) :]]
        return kept, sums, results

    def total(self, x):
        for stage in self.stages:
            terms = [x] + self.swaps(x, stage)
            while len(terms) > 1:
                terms = [a + b for a, b in zip(terms[0::2], terms[1::2])]
            x = terms[0]
        return x


def after(x, earlier):
    return lax.optimization_barrier((x, earlier))[0]


def adamw_update(weight, first, second, gradient, learn_rate):
    first_new = 0.5 * first + 0.5 * gradient
    second_new = 0.5 * second + 0.5 * gradient * gradient
    correction = 1.0 - 0.5 ** float(STEP)
    stepped = first_new / correction / (jnp.sqrt(second_new / correction) + 1e-08)
    return (weight - learn_rate * (stepped + 0.01 * weight), first_new, second_new)


def grouped(rows):
    n, width = rows.shape
    split = rows.reshape(n, width // USED, USED)
    return jnp.pad(split, ((0, 0), (0, 0), (0, GROUP - USED))).reshape(n, width // USED * GROUP)


def ungrouped(rows):
    n, width = rows.shape
    return rows.reshape(n, width // GROUP, GROUP)[:, :, :USED].reshape(n, width // GROUP * USED)


def packed_feed(up, down, out):
    n = up.shape[0]
    down = jnp.pad(down.reshape(n, 4, D), ((0, 0), (0, 0), (0, 512 - D))).reshape(n, 4 * 512)
    return jnp.concatenate([up, down, jnp.pad(out, ((0, 0), (0, 512 - D)))], axis=1)


def unpacked_feed(rows):
    n = rows.shape[0]
    down = rows[:, DOWN_AT : DOWN_AT + 4 * 512].reshape(n, 4, 512)[:, :, :D].reshape(n, FF)
    return rows[:, :FF], down, rows[:, OUT_AT : OUT_AT + D]


def pad_rows(rows, to):
    return jnp.pad(rows, ((0, to - rows.shape[0]), (0, 0)))


def shards(
    devices, tokens, segment_ids, pad_mask, cotangent,
    qkv_weight, qkv_first, qkv_second, out_weight, out_first, out_second,
    up_weight, up_first, up_second, down_weight, down_first, down_second,
    gains, gain_first, gain_second, biases, bias_first, bias_second,
):
    row_count, length, _ = tokens.shape
    ring = Exchange(devices)
    own_rows = out_weight.shape[0] // D
    by_rows = out_weight.shape[0] % D == 0
    slot = -(-own_rows // 16) * 16 if by_rows else D
    parts = ring.parts if by_rows else 1

    flat_gains, flat_biases = gains.reshape(1, -1), biases.reshape(1, -1)
    if by_rows:
        slots = slot * devices
        place = np.arange(slots)
        masks = jnp.asarray(np.asarray(ring.masks)[place // slot], jnp.int32)
        inner = place % slot
        me = lax.axis_index(AXES)
        held = jnp.where(inner < own_rows, (me ^ masks) * own_rows + inner, -1)[None, :]
    else:
        held = jnp.arange(D, dtype=jnp.int32)[None, :]

    def turned(sent):
        return turn_rows(
            segment_ids, pad_mask, after(jnp.swapaxes(tokens, 1, 2), sent),
            jnp.swapaxes(cotangent, 1, 2), flat_gains, flat_biases,
        )

    def prepared(sent):
        feed_weights, out_weights, own_held = after(((up_weight, down_weight), out_weight, held), sent)
        if by_rows:
            feed_rows = packed_feed(
                feed_weights[0].astype(bf16).reshape(own_rows, FF),
                feed_weights[1].astype(bf16).reshape(own_rows, FF),
                out_weights.astype(bf16).reshape(own_rows, D),
            )
            feed_rows = pad_rows(feed_rows, slot)
        else:
            feed_rows = packed_feed(
                fetch(feed_weights[0], FF), fetch(feed_weights[1], FF), fetch(out_weights, D)
            )
        return own_held, feed_rows

    def fetch(weight, width):
        flat = lax.all_gather(weight.astype(bf16), AXES, axis=0, tiled=True)
        return flat.reshape(D, width)

    if by_rows:
        qkv_rows = grouped(qkv_weight.astype(bf16).reshape(own_rows, 3 * D))
        qkv_all, (small, first_turned) = ring.gather(pad_rows(qkv_rows, slot), (prepared, turned))
    else:
        qkv_all = [grouped(fetch(qkv_weight, 3 * D))]
        first_turned, small = turned(qkv_all[0]), prepared(qkv_all[0])
    tokens_low, cotangent_low, normed, cosine, sine, query_lanes, key_lanes, pad, start = first_turned
    held, feed_rows = small

    def projected(sent):
        return project(
            after(normed, sent), qkv_all, held, flat_biases, cosine, sine, query_lanes, key_lanes
        )

    made = []

    def attending(first, count):
        def work(sent):
            q, k, v, _ = made[0]
            made.append(attend(after(q, sent), k, v, pad, first, count))
            return made[-1]

        return work

    def projecting(sent):
        made.append(projected(sent))
        return made[-1]

    works = (projecting, attending(0, 3), attending(3, 1))
    if by_rows:
        feed_all, _ = ring.gather(feed_rows, works)
    else:
        feed_all = [feed_rows]
        for work in works:
            work(feed_rows)
    (q, k, v, qkv_wide), *saved = made
    outputs_low, grad_middle, grad_attended, feed_sums, *feed_grads = feed(
        [attended for attended, *_ in saved], tokens_low, cotangent_low, feed_all, held,
        flat_gains, flat_biases, parts,
    )

    def outputs_back(sent):
        return jnp.swapaxes(unturn_rows(start, after(outputs_low, sent), length), 1, 2)

    def attending_back(first, count, which, held):
        def work(sent):
            return attend_back(
                q, k, v, after(grad_attended, sent), *saved[which], cosine, sine, first, count,
                held,
            )

        return work

    backs = []

    def last_group(sent):
        backs.append(attending_back(3, 1, 1, 3)(sent))
        return backs[-1]

    def first_groups(sent):
        backs.append(attending_back(0, 3, 0, 0)(sent))
        return backs[-1]

    def projecting_back(sent):
        dq, dk, dv = (list(x) for x in zip(*backs[::-1]))
        return project_back(
            dq, dk, dv, after(normed, sent), tokens_low, grad_middle, qkv_wide, held, flat_gains, parts
        )

    works = (last_group, first_groups, projecting_back)
    if by_rows:
        feed_part, feed_sums, results = ring.scatter_sum(
            feed_grads[0], feed_grads[1:], feed_sums, works
        )
    else:
        feed_part, results = feed_grads[0], [work(feed_sums) for work in works]
    grad_tokens, qkv_sums, *qkv_grads = results[-1]

    def grads_back(sent):
        return jnp.swapaxes(unturn_rows(start, after(grad_tokens, sent), length), 1, 2)

    def feed_updated(sent):
        part = after(feed_part, sent)
        if by_rows:
            grads = [x.reshape(-1) for x in unpacked_feed(part[:own_rows])]
        else:
            grads = [reduce(x) for x in unpacked_feed(part)]
        up_grad, down_grad, out_grad = grads
        return (
            (up_grad, *adamw_update(up_weight, up_first, up_second, up_grad, 0.05)),
            (down_grad, *adamw_update(down_weight, down_first, down_second, down_grad, 0.03)),
            (out_grad, *adamw_update(out_weight, out_first, out_second, out_grad, 0.3)),
        )

    def reduce(part):
        return lax.psum_scatter(part.astype(f32).reshape(-1), AXES, scatter_dimension=0, tiled=True)

    works = (feed_updated, grads_back, outputs_back)
    if by_rows:
        qkv_part, qkv_sums, results = ring.scatter_sum(qkv_grads[0], qkv_grads[1:], qkv_sums, works)
        qkv_grad = ungrouped(qkv_part[:own_rows]).reshape(-1)
    else:
        results = [work(qkv_sums) for work in works]
        qkv_grad = reduce(ungrouped(qkv_grads[0]))
        feed_sums, qkv_sums = ring.total(feed_sums), ring.total(qkv_sums)
    (up_results, down_results, out_results), input_grad, outputs = results
    down_sum, out_sum, gain_sum, offset_sum = (
        feed_sums[0, at : at + D] for at in range(FF, FF + 4 * 512, 512)
    )
    gain_grad = jnp.concatenate([qkv_sums[1, :D], gain_sum])
    bias_grad = jnp.concatenate(
        [
            qkv_sums[1, 512 : 512 + D], ungrouped(qkv_sums[0:1])[0], out_sum, offset_sum,
            feed_sums[0, :FF], down_sum,
        ]
    )
    return (
        outputs,
        input_grad,
        qkv_grad,
        *adamw_update(qkv_weight, qkv_first, qkv_second, qkv_grad, 0.05),
        *out_results,
        *up_results,
        *down_results,
        gain_grad,
        *adamw_update(gains, gain_first, gain_second, gain_grad, 0.2),
        bias_grad,
        *adamw_update(biases, bias_first, bias_second, bias_grad, 0.1),
        bias_grad[6 * D + FF :],
    )


def solution(mesh):
    split, copied = P(AXES), P()
    rows, row = P(AXES, None, None), P(AXES, None)
    in_specs = (rows, row, row, rows) + (split,) * 12 + (copied,) * 6
    out_specs = (rows, rows) + (split,) * 16 + (copied,) * 9
    devices = math.prod(mesh.shape[axis] for axis in AXES)
    return jax.shard_map(
        functools.partial(shards, devices),
        mesh=mesh,
        in_specs=in_specs,
        out_specs=out_specs,
        check_vma=False,
    )
```

```python
import functools
import math

import jax
import jax.numpy as jnp
import numpy as np
from jax import lax
from jax.experimental import pallas as pl
from jax.experimental.pallas import tpu as pltpu
from jax.sharding import PartitionSpec as P

D = 480
HEAD_DIM = 24
FF = 1920
STEP = 3
AXES = ("wide", "narrow")

GROUP = 128
PER_GROUP = 5
GROUPS = 4
USED = PER_GROUP * HEAD_DIM
WIDTH = GROUPS * GROUP
HALF = HEAD_DIM // 2
BLOCK = 512
FAR = -1e30
LOG2E = math.log2(math.e)
SCALE = HEAD_DIM**-0.5
VMEM_LIMIT = 56 * 2**20
SAFE = 60.0
ATTEND = 1024
ATTEND_BACK = 512
SUM_ROWS = 16

f32 = jnp.float32
bf16 = jnp.bfloat16


def contract(left, right, left_dim, right_dim):
    return lax.dot_general(
        left, right, (((left_dim,), (right_dim,)), ((), ())), preferred_element_type=f32
    )


def lanes():
    return lax.broadcasted_iota(jnp.int32, (1, GROUP), 1)


def head_lanes(m):
    lane = lanes()
    return (lane >= HEAD_DIM * m) & (lane < HEAD_DIM * (m + 1))


def of_head(x, m):
    return jnp.where(head_lanes(m) | (lanes() >= USED), x, jnp.zeros_like(x))


def same_head():
    rows = lax.broadcasted_iota(jnp.int32, (GROUP, GROUP), 0) // HEAD_DIM
    columns = lax.broadcasted_iota(jnp.int32, (GROUP, GROUP), 1) // HEAD_DIM
    return jnp.where((rows == columns) & (rows < PER_GROUP), 1.0, 0.0).astype(bf16)


def head_sums(product, same):
    high = product.astype(bf16)
    low = (product - high.astype(f32)).astype(bf16)
    return contract(high, same, 1, 0) + contract(low, same, 1, 0)


def normalized(field):
    average = jnp.mean(field, axis=-1, keepdims=True)
    centered = field - average
    spread = jnp.mean(centered * centered, axis=-1, keepdims=True)
    root = lax.rsqrt(spread + 1e-05)
    return centered * root, root


def norm_back(grad, unit, root, gain_row):
    scaled = grad * gain_row
    return root * (
        scaled
        - jnp.mean(scaled, axis=-1, keepdims=True)
        - unit * jnp.mean(scaled * unit, axis=-1, keepdims=True)
    )


def takes(microseconds):
    return pl.CostEstimate(
        flops=int(microseconds * 1.1e9), bytes_accessed=1024, transcendentals=0
    )


def params(n_axes=1):
    return pltpu.CompilerParams(
        vmem_limit_bytes=VMEM_LIMIT, dimension_semantics=("arbitrary",) * n_axes
    )


def params_of(mib, n_axes=1):
    return pltpu.CompilerParams(
        vmem_limit_bytes=mib * 2**20, dimension_semantics=("arbitrary",) * n_axes
    )


def whole(shape):
    return pl.BlockSpec(shape, lambda *_: (0,) * len(shape))


def turn_kernel(
    segments_ref, mask_ref, tokens_ref, cotangent_ref, gains_ref, biases_ref,
    tokens_out, cotangent_out, normed_out, cosine_out, sine_out, query_out, key_out, pad_out, start_out,
):
    length = tokens_ref.shape[2]
    r = pl.program_id(0)
    segments = segments_ref[pl.ds(r, 1), :]
    counts = [jnp.sum(jnp.where(segments == c, 1.0, 0.0)) for c in range(3)]
    begins = [counts[0], counts[0] + counts[1], counts[0] + counts[1] + counts[2]]
    start = begins[2]
    for c, begin in ((2, begins[1]), (1, begins[0]), (0, 0.0)):
        start = jnp.where(counts[c] == float(BLOCK), begin, start)
    start_out[r] = start

    def places(shape, dim, first):
        place = lax.broadcasted_iota(jnp.int32, shape, dim).astype(f32) + (start + float(first))
        return jnp.where(place >= float(length), place - float(length), place)

    place = places((1, length), 1, 0)
    begin = jnp.where(place >= begins[0], begins[0], 0.0)
    for c in (1, 2):
        begin = jnp.where(place >= begins[c], begins[c], begin)
    exponent = lax.broadcasted_iota(jnp.int32, (16, 1), 0).astype(f32)
    phases = (place - begin) * jnp.exp(exponent * (-math.log(10000.0) / HALF))
    lane = lax.broadcasted_iota(jnp.int32, (16, GROUP), 1)
    entry = lax.broadcasted_iota(jnp.int32, (16, GROUP), 0)
    grid = jnp.where((lane < USED) & (lane % HALF == entry), 1.0, 0.0).astype(bf16)
    for part, out in ((jnp.cos(phases), cosine_out), (jnp.sin(phases), sine_out)):
        high, middle, low = split_three(part)
        out[...] = contract(high, grid, 0, 0) + contract(middle, grid, 0, 0) + contract(low, grid, 0, 0)

    mask = jnp.broadcast_to(mask_ref[pl.ds(r, 1), :].astype(f32), (GROUP, length)).astype(bf16)
    gain, offset = gains_ref[:, :D], biases_ref[:, :D]
    step = 256
    spare = lax.broadcasted_iota(jnp.int32, (step, GROUP), 1).astype(f32) - float(USED)
    for first in range(0, length, step):
        here = slice(first, first + step)
        source = lax.broadcasted_iota(jnp.int32, (step, length), 1).astype(f32)
        pick = jnp.where(places((step, length), 0, first) == source, 1.0, 0.0).astype(bf16)
        turned = contract(pick, tokens_ref[0], 1, 1)
        tokens_out[here, :] = turned.astype(bf16)
        unit, _ = normalized(turned)
        normed_out[here, :] = (unit * gain + offset).astype(bf16)
        cotangent_out[here, :] = contract(pick, cotangent_ref[0], 1, 1).astype(bf16)
        present = contract(pick, mask, 1, 1)
        place = places((step, GROUP), 0, first)
        segment = sum(jnp.where(place >= begin, 1.0, 0.0) for begin in begins)
        mine = segment == spare
        query_out[here, :] = jnp.where(mine, 1.0, 0.0).astype(bf16)
        key_out[here, :] = jnp.where(mine & (present > 0.5), 0.0, FAR).astype(bf16)
        pad_out[here, :] = (1.0 - present).astype(bf16)


def turn_rows(segments, mask, tokens, cotangent, gains, biases):
    rows, width, length = tokens.shape
    row = pl.BlockSpec((length, width), lambda r: (r, 0))
    flat = pl.BlockSpec((1, width, length), lambda r: (r, 0, 0))
    lane = pl.BlockSpec((length, GROUP), lambda r: (r, 0))
    tall = jax.ShapeDtypeStruct((rows * length, width), bf16)

    def lane_shape(kind):
        return jax.ShapeDtypeStruct((rows * length, GROUP), kind)

    return pl.pallas_call(
        turn_kernel,
        grid=(rows,),
        in_specs=[
            whole(segments.shape), whole(mask.shape), flat, flat, whole(gains.shape), whole(biases.shape),
        ],
        out_specs=[row] * 3 + [lane] * 5 + [pl.BlockSpec(memory_space=pltpu.SMEM)],
        out_shape=[tall, tall, tall, lane_shape(f32), lane_shape(f32)]
        + [lane_shape(bf16)] * 3
        + [jax.ShapeDtypeStruct((rows,), f32)],
        compiler_params=params(),
        cost_estimate=takes(12),
    )(segments, mask, tokens, cotangent, gains, biases)


def unturn_kernel(start_ref, rows_ref, out_ref):
    length = rows_ref.shape[0]
    start = start_ref[pl.program_id(0)]
    rows = rows_ref[...]
    high = rows.astype(bf16)
    step = 256
    for first in range(0, length, step):
        here = slice(first, first + step)
        target = lax.broadcasted_iota(jnp.int32, (length, step), 1).astype(f32) + (float(first) - start)
        target = jnp.where(target < 0.0, target + float(length), target)
        source = lax.broadcasted_iota(jnp.int32, (length, step), 0).astype(f32)
        pick = jnp.where(target == source, 1.0, 0.0).astype(bf16)
        got = contract(high, pick, 0, 0)
        if rows.dtype == f32:
            got = got + contract((rows - high.astype(f32)).astype(bf16), pick, 0, 0)
        out_ref[0, :, here] = got.astype(out_ref.dtype)


def unturn_rows(start, rows, length):
    total, width = rows.shape
    return pl.pallas_call(
        unturn_kernel,
        grid=(total // length,),
        in_specs=[
            pl.BlockSpec(memory_space=pltpu.SMEM),
            pl.BlockSpec((length, width), lambda r: (r, 0)),
        ],
        out_specs=pl.BlockSpec((1, width, length), lambda r: (r, 0, 0)),
        out_shape=jax.ShapeDtypeStruct((total // length, width, length), rows.dtype),
        compiler_params=params(),
        cost_estimate=takes(3 if rows.dtype == bf16 else 6),
    )(start, rows)


def swap_halves(field, forward):
    low_half = lanes() % HEAD_DIM < HALF
    up = pltpu.roll(field, GROUP - HALF, 1)
    down = pltpu.roll(field, HALF, 1)
    if forward:
        return jnp.where(low_half, -up, down)
    return jnp.where(low_half, up, -down)


def order_of(held_ref):
    shape = (D, held_ref.shape[1])
    row = lax.broadcasted_iota(jnp.int32, shape, 0)
    return jnp.where(row == held_ref[...], 1.0, 0.0).astype(bf16)


def group_order_of(held_ref):
    shape = (WIDTH, held_ref.shape[1])
    row = lax.broadcasted_iota(jnp.int32, shape, 0)
    row = jnp.where(row % GROUP < USED, row // GROUP * USED + row % GROUP, -2)
    return jnp.where(row == held_ref[...], 1.0, 0.0).astype(bf16)


def in_order(order, gathered_refs, columns):
    got, at = 0.0, 0
    for ref in gathered_refs:
        n = ref.shape[0]
        got = got + jnp.dot(order[:, at : at + n], ref[:, columns], preferred_element_type=f32)
        at += n
    return got


def put_parts(outs, order, columns, grad):
    n = outs[0].shape[0]
    for i, out in enumerate(outs):
        out[:n, columns] = contract(order[:, n * i : n * (i + 1)], grad, 0, 0).astype(bf16)


def split_three(x):
    high = x.astype(bf16)
    rest = x - high.astype(f32)
    middle = rest.astype(bf16)
    return high, middle, (rest - middle.astype(f32)).astype(bf16)


def put_sums(outs, sums_ref):
    for out in outs:
        n = out.shape[0] - SUM_ROWS
        block = jnp.concatenate(
            [part.astype(f32) for part in split_three(sums_ref[0:2, :])]
            + [jnp.zeros((SUM_ROWS - 6, out.shape[1]), f32)],
            axis=0,
        )
        out[n:, :] = block.astype(bf16)


def part_shapes(slots, width, parts):
    n = slots // parts
    return [jax.ShapeDtypeStruct((n, width), bf16)] + [
        jax.ShapeDtypeStruct((n + SUM_ROWS, width), bf16)
    ] * (parts - 1)


def project_kernel(n_gathered, *refs):
    gathered_refs = refs[:n_gathered]
    (
        normed_ref, held_ref, biases_ref, cosine_ref, sine_ref, query_lanes, key_lanes,
        q_out, k_out, v_out, weight_out, bias_ref,
    ) = refs[n_gathered:]

    @pl.when(pl.program_id(0) == 0)
    def _():
        weight_out[...] = in_order(order_of(held_ref), gathered_refs, slice(None)).astype(bf16)
        bias_ref[...] = jnp.zeros_like(bias_ref)
        for i in range(3 * GROUPS):
            at = D + USED * i
            bias_ref[:, GROUP * i : GROUP * i + USED] = biases_ref[:, at : at + USED]

    cosine, sine = cosine_ref[...], sine_ref[...]
    own = lanes() < USED
    for g in range(GROUPS):
        to = slice(GROUP * g, GROUP * (g + 1))
        for part, out, factor, spare in (
            (0, q_out, SCALE, query_lanes),
            (1, k_out, 1.0, key_lanes),
        ):
            at = slice(WIDTH * part + GROUP * g, WIDTH * part + GROUP * (g + 1))
            mixed = jnp.dot(
                normed_ref[...], weight_out[:, at], preferred_element_type=f32
            ) + bias_ref[:, at]
            turned = mixed * cosine + swap_halves(mixed, True) * sine
            out[:, to] = jnp.where(own, (turned * factor).astype(bf16), spare[...])
    values = slice(2 * WIDTH, 3 * WIDTH)
    v_out[...] = (
        jnp.dot(normed_ref[...], weight_out[:, values], preferred_element_type=f32)
        + bias_ref[:, values]
    ).astype(bf16)


def project(normed, gathered, held, biases, cosine, sine, query_lanes, key_lanes):
    total = normed.shape[0]
    tile = 512

    def tiled(width):
        return pl.BlockSpec((tile, width), lambda t: (t, 0))

    return pl.pallas_call(
        functools.partial(project_kernel, len(gathered)),
        grid=(total // tile,),
        in_specs=[whole(x.shape) for x in gathered]
        + [
            tiled(D), whole(held.shape), whole(biases.shape),
            tiled(GROUP), tiled(GROUP), tiled(GROUP), tiled(GROUP),
        ],
        out_specs=[tiled(WIDTH)] * 3 + [whole((D, 3 * WIDTH))],
        out_shape=[jax.ShapeDtypeStruct((total, WIDTH), bf16)] * 3
        + [jax.ShapeDtypeStruct((D, 3 * WIDTH), bf16)],
        scratch_shapes=[pltpu.VMEM((1, 3 * WIDTH), f32)],
        compiler_params=params(),
        cost_estimate=takes(10),
    )(*gathered, normed, held, biases, cosine, sine, query_lanes, key_lanes)


def heads_flat(field, spare):
    flat = field.astype(f32).T
    tail = jnp.full((8, field.shape[0]), spare, f32)
    return [
        jnp.concatenate([flat[HEAD_DIM * m : HEAD_DIM * (m + 1)], tail], axis=0).astype(bf16)
        for m in range(PER_GROUP)
    ]


def attend_kernel(q_ref, k_ref, v_ref, pad_ref, attended_out, probs_out, scale_out, own_out):
    length = q_ref.shape[0]
    same = same_head()
    own = lanes() < USED
    squares = []
    for ref in (q_ref, k_ref):
        kept = jnp.where(own, ref[...], jnp.zeros((), bf16))
        squares.append(jnp.max(contract(kept * kept, same, 1, 0), axis=0, keepdims=True))
    safe = jnp.max(squares[0] * squares[1]) <= SAFE * SAFE

    def diagonal(here):
        q, k = q_ref[here, :].astype(f32), k_ref[here, :].astype(f32)
        return head_sums(jnp.where(own, q * k, 0.0), same) * LOG2E

    def block_of(first):
        here = slice(first, first + BLOCK)
        values = jnp.concatenate([v_ref[here, :], jnp.ones((BLOCK, GROUP), bf16)], axis=1)
        return here, k_ref[here, :], values

    def rows_of(first, m):
        return pl.ds((first // BLOCK * PER_GROUP + m) * BLOCK, BLOCK)

    @pl.when(safe)
    def _():
        for first in range(0, length, BLOCK):
            here, k, values = block_of(first)
            total = jnp.zeros((BLOCK, GROUP), f32)
            weight = jnp.zeros((BLOCK, GROUP), f32)
            for m in range(PER_GROUP):
                scores = contract(of_head(q_ref[here, :], m), k, 1, 1)
                probs = jnp.exp2(scores * LOG2E).astype(bf16)
                probs_out[rows_of(first, m), :] = probs
                got = jnp.dot(probs, values, preferred_element_type=f32)
                total = jnp.where(head_lanes(m), got[:, :GROUP], total)
                weight = jnp.where(head_lanes(m), got[:, GROUP:], weight)
            extra = pad_ref[here, :].astype(f32) * jnp.exp2(diagonal(here))
            scale = 1.0 / jnp.where(own, weight + extra, 1.0)
            extra = extra * scale
            attended_out[here, :] = (total * scale + extra * v_ref[here, :].astype(f32)).astype(bf16)
            scale_out[here, :] = scale
            own_out[here, :] = extra.astype(bf16)

    @pl.when(jnp.logical_not(safe))
    def _():
        for first in range(0, length, BLOCK):
            here, k, values = block_of(first)
            padded = pad_ref[here, :].astype(f32)
            on_diagonal = jnp.where(padded > 0.5, diagonal(here), FAR)

            def one_head(m, carry):
                total, extra = carry
                scores = contract(of_head(q_ref[here, :], m), k, 1, 1) * LOG2E
                mine = jnp.where(head_lanes(m), on_diagonal, FAR)
                single = jnp.max(mine, axis=1, keepdims=True)
                highest = jnp.maximum(jnp.max(scores, axis=1, keepdims=True), single)
                weight = jnp.sum(jnp.exp2(scores - highest), axis=1, keepdims=True)
                shift = highest + jnp.log2(weight + jnp.exp2(single - highest))
                probs = jnp.exp2(scores - shift).astype(bf16)
                probs_out[rows_of(first, m), :] = probs
                got = jnp.dot(probs, values, preferred_element_type=f32)
                return (
                    jnp.where(head_lanes(m), got[:, :GROUP], total),
                    jnp.where(head_lanes(m), jnp.exp2(single - shift), extra),
                )

            zero = jnp.zeros((BLOCK, GROUP), f32)
            total, extra = lax.fori_loop(0, PER_GROUP, one_head, (zero, zero))
            attended_out[here, :] = (total + extra * v_ref[here, :].astype(f32)).astype(bf16)
            scale_out[here, :] = jnp.ones((BLOCK, GROUP), f32)
            own_out[here, :] = extra.astype(bf16)


def attend(q, k, v, pad, first, count):
    total = q.shape[0]
    block = pl.BlockSpec((ATTEND, GROUP), lambda r, g: (r, first + g))
    out = pl.BlockSpec((ATTEND, GROUP), lambda r, g: (r, g))
    pads = pl.BlockSpec((ATTEND, GROUP), lambda r, g: (r, 0))
    width = GROUP * count
    return pl.pallas_call(
        attend_kernel,
        grid=(total // ATTEND, count),
        in_specs=[block, block, block, pads],
        out_specs=[
            out, pl.BlockSpec((PER_GROUP * ATTEND, BLOCK), lambda r, g: (r * count + g, 0)), out, out,
        ],
        out_shape=[
            jax.ShapeDtypeStruct((total, width), bf16),
            jax.ShapeDtypeStruct((total * count * PER_GROUP, BLOCK), bf16),
            jax.ShapeDtypeStruct((total, width), f32),
            jax.ShapeDtypeStruct((total, width), bf16),
        ],
        compiler_params=params(2),
        cost_estimate=takes(8 * count),
    )(q, k, v, pad)


def attend_back_kernel(
    q_ref, k_ref, v_ref, grad_ref, attended_ref, probs_ref, scale_ref, own_ref, cosine_ref, sine_ref,
    q_out, k_out, v_out,
):
    same = same_head()
    own = lanes() < USED
    for first in range(0, q_ref.shape[0], BLOCK):
        here = slice(first, first + BLOCK)
        v = v_ref[here, :]
        qf, kf, vf = q_ref[here, :].astype(f32), k_ref[here, :].astype(f32), v.astype(f32)
        gf, scale = grad_ref[here, :].astype(f32), scale_ref[here, :]
        delta = head_sums(gf * attended_ref[here, :].astype(f32), same)
        scaled = (gf * scale).astype(bf16)
        scaled_delta = delta * scale
        q_flat = heads_flat(jnp.where(own, qf, 0.0), 0.0)
        grad_flat = heads_flat(scaled, 0.0)
        k_flat = heads_flat(jnp.where(own, kf, 0.0), 0.0)
        grad_queries, grad_keys, grad_values = [], [], []
        for m in range(PER_GROUP):
            column = slice(HEAD_DIM * m, HEAD_DIM * m + 1)
            row = (first // BLOCK * PER_GROUP + m) * BLOCK
            probs = probs_ref[row : row + BLOCK, :]
            grad_probs = contract(scaled, jnp.where(head_lanes(m), v, jnp.zeros_like(v)), 1, 1)
            signal = (probs.astype(f32) * (grad_probs - scaled_delta[:, column])).astype(bf16)
            grad_values.append(contract(grad_flat[m], probs, 1, 0)[:HEAD_DIM])
            grad_keys.append(contract(q_flat[m], signal, 1, 0)[:HEAD_DIM])
            grad_queries.append(contract(k_flat[m], signal, 1, 1)[:HEAD_DIM])
        spare = jnp.zeros((GROUP - USED, BLOCK), f32)
        grad_q = jnp.concatenate(grad_queries + [spare], axis=0).T
        grad_k = jnp.concatenate(grad_keys + [spare], axis=0).T
        grad_v = jnp.concatenate(grad_values + [spare], axis=0).T
        own_prob = own_ref[here, :].astype(f32)
        own_signal = own_prob * (head_sums(gf * vf, same) - delta)
        grad_q = jnp.where(own, grad_q + own_signal * kf, 0.0)
        grad_k = jnp.where(own, grad_k + own_signal * qf, 0.0)
        grad_v = grad_v + own_prob * gf
        cosine, sine = cosine_ref[here, :], sine_ref[here, :]
        q_out[here, :] = (
            SCALE * (grad_q * cosine + swap_halves(grad_q, False) * sine)
        ).astype(bf16)
        k_out[here, :] = (grad_k * cosine + swap_halves(grad_k, False) * sine).astype(bf16)
        v_out[here, :] = grad_v.astype(bf16)


def attend_back(q, k, v, grad, attended, probs, scale, own, cosine, sine, first, count, held):
    total = q.shape[0]
    kept, per = attended.shape[1] // GROUP, ATTEND // ATTEND_BACK

    def at(offset):
        return pl.BlockSpec((ATTEND_BACK, GROUP), lambda r, g: (r, offset + g))

    saved, row = at(first - held), pl.BlockSpec((ATTEND_BACK, GROUP), lambda r, g: (r, 0))
    probs_block = pl.BlockSpec(
        (PER_GROUP * ATTEND_BACK, BLOCK),
        lambda r, g: ((r // per * kept + first - held + g) * per + r % per, 0),
    )
    return pl.pallas_call(
        attend_back_kernel,
        grid=(total // ATTEND_BACK, count),
        in_specs=[at(first)] * 4 + [saved, probs_block, saved, saved, row, row],
        out_specs=[at(0)] * 3,
        out_shape=[jax.ShapeDtypeStruct((total, GROUP * count), bf16)] * 3,
        compiler_params=params(2),
        cost_estimate=takes(14 * count),
    )(q, k, v, grad, attended, probs, scale, own, cosine, sine)


def gelu_both(v):
    e = jnp.exp2(v * v * (-0.5 * LOG2E))
    t = 1.0 / (1.0 + (0.3275911 / math.sqrt(2.0)) * jnp.abs(v))
    poly = t * (0.5 * 1.061405429) + (0.5 * -1.453152027)
    poly = poly * t + (0.5 * 1.421413741)
    poly = poly * t + (0.5 * -0.284496736)
    poly = poly * t + (0.5 * 0.254829592)
    tail = poly * t * e
    phi = jnp.where(v >= 0.0, 1.0 - tail, tail)
    return v * phi, phi + v * e * (1.0 / math.sqrt(2.0 * math.pi))


UP_AT, DOWN_AT, OUT_AT = 0, FF, FF + 4 * 512
PACK = FF + 4 * 512 + 512
CHUNK = 640


def feed_kernel(
    n_attended, n_gathered, *refs
):
    attended_refs, refs = refs[:n_attended], refs[n_attended:]
    gathered_refs, refs = refs[:n_gathered], refs[n_gathered:]
    (
        tokens_ref, cotangent_ref, held_ref, gains_ref, biases_ref,
        outputs_out, grad_middle_out, grad_attended_out, sums_out, *refs,
    ) = refs
    *grads_outs, w_out, w_up, w_down, w_tall, d_out, d_up, d_down = refs
    step = pl.program_id(0)

    @pl.when(step == 0)
    def _():
        order = order_of(held_ref)
        w_up[...] = in_order(order, gathered_refs, slice(UP_AT, UP_AT + FF)).astype(bf16)
        for m in range(4):
            at = DOWN_AT + 512 * m
            part = in_order(order, gathered_refs, slice(at, at + 512))
            for c in range(0, 512, GROUP):
                w_tall[c // GROUP, pl.ds(m, D, stride=4), :] = part[:, c : c + GROUP]
        for c in range(4):
            n = min(GROUP, D - GROUP * c)
            w_down[:, GROUP * c : GROUP * c + n] = w_tall[c, :, :n].astype(bf16)
        w_out[...] = in_order(group_order_of(held_ref), gathered_refs, slice(OUT_AT, OUT_AT + 512))[
            :, :D
        ].astype(bf16)
        d_out[...] = jnp.zeros_like(d_out)
        d_up[...] = jnp.zeros_like(d_up)
        d_down[...] = jnp.zeros_like(d_down)
        sums_out[...] = jnp.zeros_like(sums_out)

    attended = jnp.concatenate([ref[...] for ref in attended_refs], axis=1)
    cotangent = cotangent_ref[...]
    out_bias, offset = biases_ref[:, 4 * D : 5 * D], biases_ref[:, 5 * D : 6 * D]
    gain, down_bias = gains_ref[:, D:], biases_ref[:, 6 * D + FF :]
    middle = (
        tokens_ref[...].astype(f32)
        + jnp.dot(attended, w_out[...], preferred_element_type=f32)
        + out_bias
    )
    unit, root = normalized(middle)
    normed = (unit * gain + offset).astype(bf16)
    result = middle + down_bias
    grad_normed = jnp.zeros_like(middle)
    for first in range(0, FF, CHUNK):
        at = slice(first, first + CHUNK)
        hidden = (
            jnp.dot(normed, w_up[:, at], preferred_element_type=f32) + biases_ref[:, 6 * D + first : 6 * D + first + CHUNK]
        )
        active, slope = gelu_both(hidden)
        active = active.astype(bf16)
        result = result + jnp.dot(active, w_down[at, :], preferred_element_type=f32)
        grad_hidden = (contract(cotangent, w_down[at, :], 1, 1) * slope).astype(bf16)
        d_down[at, :] += contract(active, cotangent, 0, 0)
        d_up[:, at] += contract(normed, grad_hidden, 0, 0)
        grad_normed = grad_normed + contract(grad_hidden, w_up[:, at], 1, 1)
        sums_out[0:1, at] += jnp.sum(grad_hidden.astype(f32), axis=0, keepdims=True)
    outputs_out[...] = result.astype(bf16)
    grad_middle = cotangent.astype(f32) + norm_back(grad_normed, unit, root, gain)
    grad_middle_out[...] = grad_middle
    grad_branch = grad_middle.astype(bf16)
    d_out[...] += contract(attended, grad_branch, 0, 0)
    grad_attended_out[...] = contract(grad_branch, w_out[...], 1, 1).astype(bf16)
    for i, terms in enumerate(
        (cotangent.astype(f32), grad_branch.astype(f32), grad_normed * unit, grad_normed)
    ):
        at = FF + 512 * i
        sums_out[0:1, at : at + D] += jnp.sum(terms, axis=0, keepdims=True)

    @pl.when(step == pl.num_programs(0) - 1)
    def _():
        order = order_of(held_ref)
        put_parts(grads_outs, order, slice(UP_AT, UP_AT + FF), d_up[...].astype(bf16))
        for c in range(4):
            n = min(GROUP, D - GROUP * c)
            w_tall[c, :, :n] = d_down[:, GROUP * c : GROUP * c + n]
        for m in range(4):
            for c in range(4):
                at = DOWN_AT + 512 * m + GROUP * c
                part = w_tall[c, pl.ds(m, D, stride=4), :].astype(bf16)
                put_parts(grads_outs, order, slice(at, at + GROUP), part)
        put_parts(
            grads_outs, group_order_of(held_ref), slice(OUT_AT, OUT_AT + D), d_out[...].astype(bf16)
        )
        put_sums(grads_outs[1:], sums_out)


def feed(attended, tokens, cotangent, gathered, held, gains, biases, parts):
    total = tokens.shape[0]
    tile = 512

    def tiled(width):
        return pl.BlockSpec((tile, width), lambda t: (t, 0))

    grads = part_shapes(held.shape[1], PACK, parts)
    return pl.pallas_call(
        functools.partial(feed_kernel, len(attended), len(gathered)),
        grid=(total // tile,),
        in_specs=[tiled(x.shape[1]) for x in attended]
        + [whole(x.shape) for x in gathered]
        + [
            tiled(D), tiled(D), whole(held.shape), whole(gains.shape), whole(biases.shape),
        ],
        out_specs=[tiled(D), tiled(D), tiled(WIDTH), whole((8, PACK))]
        + [whole(x.shape) for x in grads],
        out_shape=[
            jax.ShapeDtypeStruct((total, D), bf16),
            jax.ShapeDtypeStruct((total, D), f32),
            jax.ShapeDtypeStruct((total, WIDTH), bf16),
            jax.ShapeDtypeStruct((8, PACK), f32),
        ]
        + grads,
        scratch_shapes=[
            pltpu.VMEM((WIDTH, D), bf16),
            pltpu.VMEM((D, FF), bf16),
            pltpu.VMEM((FF, D), bf16),
            pltpu.VMEM((4, FF, GROUP), f32),
            pltpu.VMEM((WIDTH, D), f32),
            pltpu.VMEM((D, FF), f32),
            pltpu.VMEM((FF, D), f32),
        ],
        compiler_params=params(),
        cost_estimate=takes(50),
    )(*attended, *gathered, tokens, cotangent, held, gains, biases)


def project_back_kernel(n_parts, *refs):
    grad_refs = [refs[n_parts * i : n_parts * (i + 1)] for i in range(3)]
    (
        normed_ref, tokens_ref, grad_middle_ref, weight_ref, held_ref, gains_ref,
        grad_out, sums_out, *grads_outs, d_weight,
    ) = refs[3 * n_parts :]
    step = pl.program_id(0)

    @pl.when(step == 0)
    def _():
        d_weight[...] = jnp.zeros_like(d_weight)
        sums_out[...] = jnp.zeros_like(sums_out)

    grad_normed = jnp.zeros(tokens_ref.shape, f32)
    for i, parts in enumerate(grad_refs):
        at = slice(WIDTH * i, WIDTH * (i + 1))
        grad = jnp.concatenate([ref[...] for ref in parts], axis=1)
        d_weight[:, at] += contract(normed_ref[...], grad, 0, 0)
        grad_normed = grad_normed + contract(grad, weight_ref[:, at], 1, 1)
        sums_out[0:1, at] += jnp.sum(grad.astype(f32), axis=0, keepdims=True)
    unit, root = normalized(tokens_ref[...].astype(f32))
    grad_out[...] = grad_middle_ref[...] + norm_back(grad_normed, unit, root, gains_ref[:, :D])
    sums_out[1:2, :D] += jnp.sum(grad_normed * unit, axis=0, keepdims=True)
    sums_out[1:2, 512 : 512 + D] += jnp.sum(grad_normed, axis=0, keepdims=True)

    @pl.when(step == pl.num_programs(0) - 1)
    def _():
        put_parts(grads_outs, order_of(held_ref), slice(None), d_weight[...].astype(bf16))
        put_sums(grads_outs[1:], sums_out)


def project_back(dq, dk, dv, normed, tokens, grad_middle, weight, held, gains, parts):
    total = tokens.shape[0]
    tile = 512

    def tiled(width):
        return pl.BlockSpec((tile, width), lambda t: (t, 0))

    grads = part_shapes(held.shape[1], 3 * WIDTH, parts)
    return pl.pallas_call(
        functools.partial(project_back_kernel, len(dq)),
        grid=(total // tile,),
        in_specs=[tiled(x.shape[1]) for x in dq + dk + dv]
        + [tiled(D)] * 3
        + [whole(weight.shape), whole(held.shape), whole(gains.shape)],
        out_specs=[tiled(D), whole((8, 3 * WIDTH))] + [whole(x.shape) for x in grads],
        out_shape=[
            jax.ShapeDtypeStruct((total, D), f32),
            jax.ShapeDtypeStruct((8, 3 * WIDTH), f32),
        ]
        + grads,
        scratch_shapes=[pltpu.VMEM((D, 3 * WIDTH), f32)],
        compiler_params=params_of(40),
        cost_estimate=takes(12),
    )(*dq, *dk, *dv, normed, tokens, grad_middle, weight, held, gains)


def merge_kernel(n_got, n_parts, *refs):
    kept_ref, got_refs = refs[0], refs[1 : 1 + n_got]
    own_ref = refs[1 + n_got]
    kept_out, sums_out, *sent_outs = refs[2 + n_got :]
    rows = kept_ref.shape[0]
    n = rows // n_parts
    for i in range(n_parts):
        at = slice(n * i, n * (i + 1))
        block = kept_ref[at, :].astype(f32)
        for ref in got_refs:
            block = block + ref[at, :].astype(f32)
        if i == 0:
            kept_out[...] = block
        else:
            sent_outs[i - 1][:n, :] = block.astype(bf16)
    terms = [own_ref[0:2, :]]
    for ref in got_refs:
        tail = ref[rows:, :].astype(f32)
        terms.append((tail[0:2] + tail[2:4]) + tail[4:6])
    while len(terms) > 1:
        terms = [a + b for a, b in zip(terms[0::2], terms[1::2])]
    sums_out[...] = jnp.zeros_like(sums_out)
    sums_out[0:2, :] = terms[0]
    put_sums(sent_outs, sums_out)


def merge(kept, got, sums, parts):
    rows, width = kept.shape
    n = rows // parts
    sent = [jax.ShapeDtypeStruct((n + SUM_ROWS, width), bf16)] * (parts - 1)
    shapes = [jax.ShapeDtypeStruct((n, width), f32), jax.ShapeDtypeStruct(sums.shape, f32)] + sent
    return pl.pallas_call(
        functools.partial(merge_kernel, len(got), parts),
        in_specs=[pl.BlockSpec(memory_space=pltpu.VMEM)] * (2 + len(got)),
        out_specs=[pl.BlockSpec(memory_space=pltpu.VMEM)] * len(shapes),
        out_shape=shapes,
        compiler_params=pltpu.CompilerParams(vmem_limit_bytes=20 * 2**20),
        cost_estimate=takes(2),
    )(kept, *got, sums)


class Exchange:
    def __init__(self, count):
        self.count = count
        bits = [1 << b for b in reversed(range(count.bit_length() - 1))]
        self.stages = []
        for i in range(0, len(bits) - 1, 2):
            low, high = bits[i + 1], bits[i]
            self.stages.append([low, high, low | high])
        if len(bits) % 2:
            self.stages.append([bits[-1]])
        self.masks = [0]
        for stage in self.stages:
            self.masks = [bit ^ mask for bit in [0] + stage for mask in self.masks]
        self.parts = len(self.stages[-1]) + 1 if self.stages else 1

    def swap(self, x, bit):
        return lax.ppermute(x, AXES, [(i, i ^ bit) for i in range(self.count)])

    def swaps(self, x, stage):
        return [self.swap(x, bit) for bit in stage]

    def gather(self, x, works=()):
        results = []
        for i, stage in enumerate(self.stages):
            got = self.swaps(x, stage)
            if i < len(works):
                results.append(works[i](x))
                got = [after(part, results[-1]) for part in got]
            last = i == len(self.stages) - 1
            x = [x] + got if last else jnp.concatenate([x] + got, axis=0)
        results += [work(x[0]) for work in works[len(self.stages) :]]
        return x, results

    def scatter_sum(self, kept, sent, sums, works):
        stages, results = self.stages[::-1], []
        for i, stage in enumerate(stages):
            got = [self.swap(x, bit) for x, bit in zip(sent, stage)]
            if i < len(works):
                results.append(works[i](kept))
                got = [after(part, results[-1]) for part in got]
            parts = len(stages[i + 1]) + 1 if i + 1 < len(stages) else 1
            kept, sums, *sent = merge(kept, got, sums, parts)
        results += [work(kept) for work in works[len(stages) :]]
        return kept, sums, results

    def total(self, x):
        for stage in self.stages:
            terms = [x] + self.swaps(x, stage)
            while len(terms) > 1:
                terms = [a + b for a, b in zip(terms[0::2], terms[1::2])]
            x = terms[0]
        return x


def after(x, earlier):
    return lax.optimization_barrier((x, earlier))[0]


def adamw_update(weight, first, second, gradient, learn_rate):
    first_new = 0.5 * first + 0.5 * gradient
    second_new = 0.5 * second + 0.5 * gradient * gradient
    correction = 1.0 - 0.5 ** float(STEP)
    stepped = first_new / correction / (jnp.sqrt(second_new / correction) + 1e-08)
    return (weight - learn_rate * (stepped + 0.01 * weight), first_new, second_new)


def grouped(rows):
    n, width = rows.shape
    split = rows.reshape(n, width // USED, USED)
    return jnp.pad(split, ((0, 0), (0, 0), (0, GROUP - USED))).reshape(n, width // USED * GROUP)


def ungrouped(rows):
    n, width = rows.shape
    return rows.reshape(n, width // GROUP, GROUP)[:, :, :USED].reshape(n, width // GROUP * USED)


def packed_feed(up, down, out):
    n = up.shape[0]
    down = jnp.pad(down.reshape(n, 4, D), ((0, 0), (0, 0), (0, 512 - D))).reshape(n, 4 * 512)
    return jnp.concatenate([up, down, jnp.pad(out, ((0, 0), (0, 512 - D)))], axis=1)


def unpacked_feed(rows):
    n = rows.shape[0]
    down = rows[:, DOWN_AT : DOWN_AT + 4 * 512].reshape(n, 4, 512)[:, :, :D].reshape(n, FF)
    return rows[:, :FF], down, rows[:, OUT_AT : OUT_AT + D]


def pad_rows(rows, to):
    return jnp.pad(rows, ((0, to - rows.shape[0]), (0, 0)))


def shards(
    devices, tokens, segment_ids, pad_mask, cotangent,
    qkv_weight, qkv_first, qkv_second, out_weight, out_first, out_second,
    up_weight, up_first, up_second, down_weight, down_first, down_second,
    gains, gain_first, gain_second, biases, bias_first, bias_second,
):
    row_count, length, _ = tokens.shape
    ring = Exchange(devices)
    own_rows = out_weight.shape[0] // D
    by_rows = out_weight.shape[0] % D == 0
    slot = -(-own_rows // 16) * 16 if by_rows else D
    parts = ring.parts if by_rows else 1

    flat_gains, flat_biases = gains.reshape(1, -1), biases.reshape(1, -1)
    if by_rows:
        slots = slot * devices
        place = np.arange(slots)
        masks = jnp.asarray(np.asarray(ring.masks)[place // slot], jnp.int32)
        inner = place % slot
        me = lax.axis_index(AXES)
        held = jnp.where(inner < own_rows, (me ^ masks) * own_rows + inner, -1)[None, :]
    else:
        held = jnp.arange(D, dtype=jnp.int32)[None, :]

    def turned(sent):
        return turn_rows(
            segment_ids, pad_mask, after(jnp.swapaxes(tokens, 1, 2), sent),
            jnp.swapaxes(cotangent, 1, 2), flat_gains, flat_biases,
        )

    def prepared(sent):
        feed_weights, out_weights, own_held = after(((up_weight, down_weight), out_weight, held), sent)
        if by_rows:
            feed_rows = packed_feed(
                feed_weights[0].astype(bf16).reshape(own_rows, FF),
                feed_weights[1].astype(bf16).reshape(own_rows, FF),
                out_weights.astype(bf16).reshape(own_rows, D),
            )
            feed_rows = pad_rows(feed_rows, slot)
        else:
            feed_rows = packed_feed(
                fetch(feed_weights[0], FF), fetch(feed_weights[1], FF), fetch(out_weights, D)
            )
        return own_held, feed_rows

    def fetch(weight, width):
        flat = lax.all_gather(weight.astype(bf16), AXES, axis=0, tiled=True)
        return flat.reshape(D, width)

    if by_rows:
        qkv_rows = grouped(qkv_weight.astype(bf16).reshape(own_rows, 3 * D))
        qkv_all, (small, first_turned) = ring.gather(pad_rows(qkv_rows, slot), (prepared, turned))
    else:
        qkv_all = [grouped(fetch(qkv_weight, 3 * D))]
        first_turned, small = turned(qkv_all[0]), prepared(qkv_all[0])
    tokens_low, cotangent_low, normed, cosine, sine, query_lanes, key_lanes, pad, start = first_turned
    held, feed_rows = small

    def projected(sent):
        return project(
            after(normed, sent), qkv_all, held, flat_biases, cosine, sine, query_lanes, key_lanes
        )

    made = []

    def attending(first, count):
        def work(sent):
            q, k, v, _ = made[0]
            made.append(attend(after(q, sent), k, v, pad, first, count))
            return made[-1]

        return work

    def projecting(sent):
        made.append(projected(sent))
        return made[-1]

    works = (projecting, attending(0, 3), attending(3, 1))
    if by_rows:
        feed_all, _ = ring.gather(feed_rows, works)
    else:
        feed_all = [feed_rows]
        for work in works:
            work(feed_rows)
    (q, k, v, qkv_wide), *saved = made
    outputs_low, grad_middle, grad_attended, feed_sums, *feed_grads = feed(
        [attended for attended, *_ in saved], tokens_low, cotangent_low, feed_all, held,
        flat_gains, flat_biases, parts,
    )

    def outputs_back(sent):
        return jnp.swapaxes(unturn_rows(start, after(outputs_low, sent), length), 1, 2)

    def attending_back(first, count, which, held):
        def work(sent):
            return attend_back(
                q, k, v, after(grad_attended, sent), *saved[which], cosine, sine, first, count,
                held,
            )

        return work

    backs = []

    def last_group(sent):
        backs.append(attending_back(3, 1, 1, 3)(sent))
        return backs[-1]

    def first_groups(sent):
        backs.append(attending_back(0, 3, 0, 0)(sent))
        return backs[-1]

    def projecting_back(sent):
        dq, dk, dv = (list(x) for x in zip(*backs[::-1]))
        return project_back(
            dq, dk, dv, after(normed, sent), tokens_low, grad_middle, qkv_wide, held, flat_gains, parts
        )

    works = (last_group, first_groups, projecting_back)
    if by_rows:
        feed_part, feed_sums, results = ring.scatter_sum(
            feed_grads[0], feed_grads[1:], feed_sums, works
        )
    else:
        feed_part, results = feed_grads[0], [work(feed_sums) for work in works]
    grad_tokens, qkv_sums, *qkv_grads = results[-1]

    def grads_back(sent):
        return jnp.swapaxes(unturn_rows(start, after(grad_tokens, sent), length), 1, 2)

    def feed_updated(sent):
        part = after(feed_part, sent)
        if by_rows:
            grads = [x.reshape(-1) for x in unpacked_feed(part[:own_rows])]
        else:
            grads = [reduce(x) for x in unpacked_feed(part)]
        up_grad, down_grad, out_grad = grads
        return (
            (up_grad, *adamw_update(up_weight, up_first, up_second, up_grad, 0.05)),
            (down_grad, *adamw_update(down_weight, down_first, down_second, down_grad, 0.03)),
            (out_grad, *adamw_update(out_weight, out_first, out_second, out_grad, 0.3)),
        )

    def reduce(part):
        return lax.psum_scatter(part.astype(f32).reshape(-1), AXES, scatter_dimension=0, tiled=True)

    works = (feed_updated, grads_back, outputs_back)
    if by_rows:
        qkv_part, qkv_sums, results = ring.scatter_sum(qkv_grads[0], qkv_grads[1:], qkv_sums, works)
        qkv_grad = ungrouped(qkv_part[:own_rows]).reshape(-1)
    else:
        results = [work(qkv_sums) for work in works]
        qkv_grad = reduce(ungrouped(qkv_grads[0]))
        feed_sums, qkv_sums = ring.total(feed_sums), ring.total(qkv_sums)
    (up_results, down_results, out_results), input_grad, outputs = results
    down_sum, out_sum, gain_sum, offset_sum = (
        feed_sums[0, at : at + D] for at in range(FF, FF + 4 * 512, 512)
    )
    gain_grad = jnp.concatenate([qkv_sums[1, :D], gain_sum])
    bias_grad = jnp.concatenate(
        [
            qkv_sums[1, 512 : 512 + D], ungrouped(qkv_sums[0:1])[0], out_sum, offset_sum,
            feed_sums[0, :FF], down_sum,
        ]
    )
    return (
        outputs,
        input_grad,
        qkv_grad,
        *adamw_update(qkv_weight, qkv_first, qkv_second, qkv_grad, 0.05),
        *out_results,
        *up_results,
        *down_results,
        gain_grad,
        *adamw_update(gains, gain_first, gain_second, gain_grad, 0.2),
        bias_grad,
        *adamw_update(biases, bias_first, bias_second, bias_grad, 0.1),
        bias_grad[6 * D + FF :],
    )


def solution(mesh):
    split, copied = P(AXES), P()
    rows, row = P(AXES, None, None), P(AXES, None)
    in_specs = (rows, row, row, rows) + (split,) * 12 + (copied,) * 6
    out_specs = (rows, rows) + (split,) * 16 + (copied,) * 9
    devices = math.prod(mesh.shape[axis] for axis in AXES)
    return jax.shard_map(
        functools.partial(shards, devices),
        mesh=mesh,
        in_specs=in_specs,
        out_specs=out_specs,
        check_vma=False,
    )
```
